512 devices in a mesh: section: 8 (over x, core), head: 8 (over z), dp: 8 (over y).
Axes of the slice: x: 4, y: 8, z: 8, core: 2. Of those that a mesh axis runs over, the one named last changes fastest.
Arguments:
- teacher_q: bfloat16 [8, 1024, 8192], P('section', 'dp', 'head'), may hold values from -150 to 150
- teacher_k: bfloat16 [8, 1024, 1024], P('section', 'dp', 'head'), may hold values from -150 to 150
- student_q: bfloat16 [8, 2, 1024, 4096], P('section', None, 'dp', 'head'), may hold values from -150 to 150
- student_k: bfloat16 [8, 2, 1024, 1024], P('section', None, 'dp', 'head'), may hold values from -150 to 150
- student_scale: float32 [8, 32], P(None, 'head'), may hold values from 0.5 to 2
- pairing: int32 [8], replicated, may hold values from 0 to 7, as said below
- placement: int32 [8], replicated, may hold values from 0 to 7, as said below
Outputs:
- student_q_grad: bfloat16 [8, 2, 1024, 4096], P('section', None, 'dp', 'head')
- student_k_grad: bfloat16 [8, 2, 1024, 1024], P('section', None, 'dp', 'head')
- layer_kl: float32 [8, 8], P('dp')
- scale_grad: float32 [8, 32], P(None, 'head')
The draws below stay inside these ranges and needn't reach their ends.
Inputs may be any that keep to these rules, and one draw needn't show every extreme that they name: `pairing`: each teacher layer of the window is paired with exactly one student layer. `placement`: a section holds at most 2 student layers, in increasing order of layer index, and some section holds exactly 2.
All inputs are finite; a program needn't handle non-finite values.
Results may differ from the reference program's by a relative error of at most 0.0048.
Values may be sent and summed in bfloat16 or wider, within the bound.
No kernel may reach another device: no remote copies, remote signals or barrier semaphores. Data moves between devices by JAX's collectives and lax.ppermute only.
A program may use at most 64 MiB of HBM per device.

```python
import math
import jax
import jax.numpy as jnp
from jax import lax

TH = 64
TKV = 8
STUDENT_HEADS = 32
STUDENT_KEY_HEADS = 8
HEAD_WIDTH = 128
REPLICA_TOKENS = 128
SECTION_SLOTS = 2
TLAYERS = 8
SLAYERS = 8
N_SECTION = 8
N_DP = 8


def matched_layer_pair(key, leading, kv_heads, per_group):
    key_query, key_keys = jax.random.split(key, 2)
    keys_all = jax.random.normal(key_keys, leading + (N_DP, REPLICA_TOKENS, kv_heads, HEAD_WIDTH), jnp.float32)
    queries = jax.random.normal(key_query, leading + (N_DP, REPLICA_TOKENS, kv_heads, per_group, HEAD_WIDTH), jnp.float32)
    queries = queries.reshape(leading + (N_DP * REPLICA_TOKENS, kv_heads * per_group * HEAD_WIDTH))
    keys_all = keys_all.reshape(leading + (N_DP * REPLICA_TOKENS, kv_heads * HEAD_WIDTH))
    return (queries, keys_all)


def teacher_pair(key):
    return matched_layer_pair(jax.random.fold_in(key, 11), (TLAYERS,), TKV, TH // TKV)


def student_pair(key):
    return matched_layer_pair(jax.random.fold_in(key, 23), (N_SECTION, SECTION_SLOTS), STUDENT_KEY_HEADS, STUDENT_HEADS // STUDENT_KEY_HEADS)


def draw_teacher_q(key, part):
    return teacher_pair(key)[0].astype(jnp.bfloat16)


def draw_teacher_k(key, part):
    return teacher_pair(key)[1].astype(jnp.bfloat16)


def draw_student_q(key, part):
    return student_pair(key)[0].astype(jnp.bfloat16)


def draw_student_k(key, part):
    return student_pair(key)[1].astype(jnp.bfloat16)


def layout_helper(key):
    key_heavy, key_slots, key_layers = jax.random.split(jax.random.fold_in(key, 37), 3)
    total_slots = N_SECTION * SECTION_SLOTS
    heavy = jax.random.randint(key_heavy, (), 0, N_SECTION).astype(jnp.int32)
    slot_order = jax.random.permutation(key_slots, total_slots).astype(jnp.int32)
    section_order = slot_order // SECTION_SLOTS
    priority = jnp.where(section_order == heavy, slot_order % SECTION_SLOTS - SECTION_SLOTS, jnp.arange(total_slots, dtype=jnp.int32))
    picked = jnp.argsort(priority, stable=True)[:SLAYERS]
    sections_taken = section_order[picked].astype(jnp.int32)
    layer_order = jax.random.permutation(key_layers, SLAYERS)
    placed = jnp.zeros((SLAYERS,), jnp.int32).at[layer_order].set(sections_taken)
    return (placed, heavy)


def force_value(order, layer_at, wanted):
    layer_ids = jnp.arange(SLAYERS, dtype=jnp.int32)
    holder = jnp.sum(jnp.where(order == wanted, layer_ids, 0)).astype(jnp.int32)
    current = jnp.sum(jnp.where(layer_ids == layer_at, order, 0)).astype(jnp.int32)
    order = jnp.where(layer_ids == holder, current, order)
    return jnp.where(layer_ids == layer_at, wanted, order).astype(jnp.int32)


def draw_placement(key, part):
    return layout_helper(key)[0]


def draw_pairing(key, part):
    placed, heavy = layout_helper(key)
    layer_ids = jnp.arange(SLAYERS, dtype=jnp.int32)
    order = jax.random.permutation(jax.random.fold_in(key, 53), TLAYERS).astype(jnp.int32)
    first_layer = jnp.min(jnp.where(placed == heavy, layer_ids, SLAYERS)).astype(jnp.int32)
    second_layer = jnp.max(jnp.where(placed == heavy, layer_ids, -1)).astype(jnp.int32)
    order = force_value(order, first_layer, (heavy + N_SECTION - 1) % N_SECTION)
    order = force_value(order, second_layer, (heavy + N_SECTION // 2) % N_SECTION)
    return order


def levels(key, dims, shards, low, top_value):
    factor_of = 1.0
    for dim, parts in shards:
        heights = jax.random.uniform(jax.random.fold_in(jax.random.fold_in(key, 6), dim), (parts,), jnp.float32, low / len(shards), top_value / len(shards))
        factor_of = factor_of * jnp.repeat(jnp.exp(heights), dims[dim] // parts).reshape((-1,) + (1,) * (len(dims) - 1 - dim))
    return factor_of


def setup_inputs(seed: int = 0) -> dict:
    key_of = jax.random.split(jax.random.key(seed), 8)
    teacher_q = draw_teacher_q(jax.random.fold_in(key_of[7], 71), 0)
    teacher_k = draw_teacher_k(jax.random.fold_in(key_of[7], 71), 0)
    student_q = draw_student_q(jax.random.fold_in(key_of[7], 71), 0)
    student_k = draw_student_k(jax.random.fold_in(key_of[7], 71), 0)
    student_scale = jnp.clip(jnp.exp(math.log(2.0) - 1.3862944 * jax.random.uniform(key_of[4], (SLAYERS, STUDENT_HEADS), jnp.float32) ** levels(key_of[4], (SLAYERS, STUDENT_HEADS), ((1, 8),), -0.2, 0.2)), 0.5, 2.0)
    pairing = draw_pairing(jax.random.fold_in(key_of[7], 71), 0)
    placement = draw_placement(jax.random.fold_in(key_of[7], 71), 0)
    return {"teacher_q": teacher_q, "teacher_k": teacher_k, "student_q": student_q, "student_k": student_k, "student_scale": student_scale, "pairing": pairing, "placement": placement}


def causal_mask(length):
    row_ids = lax.broadcasted_iota(jnp.int32, (length, length), 0)
    col_ids = lax.broadcasted_iota(jnp.int32, (length, length), 1)
    return col_ids <= row_ids

def head_terms(query_twins, teacher_key, query_head, student_key, scale_value, mask):
    width = teacher_key.shape[-1]
    inverse = 1.0 / math.sqrt(width)
    teacher_scores = jnp.einsum('hid,jd->hij', query_twins.astype(jnp.float32), teacher_key.astype(jnp.float32)) * inverse
    teacher_logp = jax.nn.log_softmax(jnp.where(mask, teacher_scores, -1e+30), axis=-1)
    target_logp = jnp.logaddexp(teacher_logp[0], teacher_logp[1]) - math.log(2.0)
    raw_scores = jnp.dot(query_head, student_key.T, preferred_element_type=jnp.float32) * inverse
    student_logp = jax.nn.log_softmax(jnp.where(mask, scale_value * raw_scores, -1e+30), axis=-1)
    target_prob = jnp.exp(target_logp)
    student_prob = jnp.exp(student_logp)
    divergence = jnp.sum(jnp.where(mask, target_prob * (target_logp - student_logp), 0.0))
    difference = jnp.where(mask, student_prob - target_prob, 0.0)
    scale_term = jnp.sum(difference * raw_scores)
    logit_grad = (difference * (scale_value * inverse)).astype(jnp.bfloat16)
    query_grad = jnp.dot(logit_grad, student_key, preferred_element_type=jnp.float32)
    key_grad = jnp.dot(logit_grad.T, query_head, preferred_element_type=jnp.float32)
    return (query_grad, key_grad, divergence, scale_term)

def group_terms(teacher_query, teacher_key, student_query, student_key, scales, mask):
    length = teacher_key.shape[0]
    width = teacher_key.shape[1]
    heads_here = scales.shape[0]
    teacher_heads = teacher_query.reshape(length, heads_here, 2, width).transpose(1, 2, 0, 3)
    student_heads = student_query.reshape(length, heads_here, width).transpose(1, 0, 2)

    def one_head(items):
        return head_terms(items[0], teacher_key, items[1], student_key, items[2], mask)
    query_grads, key_gradient_list, divergences, scale_terms = lax.map(one_head, (teacher_heads, student_heads, scales))
    query_grads = query_grads.transpose(1, 0, 2).reshape(length, heads_here * width)
    return (query_grads, lax.optimization_barrier(jnp.sum(key_gradient_list, 0)), jnp.sum(divergences), scale_terms)

def reference(teacher_q, teacher_k, student_q, student_k, student_scale, pairing, placement):
    mask = causal_mask(REPLICA_TOKENS)
    groups = TKV
    query_out = jnp.zeros(student_q.shape, jnp.bfloat16)
    key_out = jnp.zeros(student_k.shape, jnp.bfloat16)
    divergence_out = jnp.zeros((N_DP, SLAYERS), jnp.float32)
    scale_out = jnp.zeros((SLAYERS, STUDENT_HEADS), jnp.float32)
    layer_ids = jnp.arange(SLAYERS, dtype=jnp.int32)
    for layer in range(SLAYERS):
        section_of = placement[layer]
        slot_of = jnp.sum(((layer_ids < layer) & (placement == section_of)).astype(jnp.int32)).astype(jnp.int32)
        teacher_layer = pairing[layer]
        teacher_query_layer = teacher_q[teacher_layer]
        teacher_key_layer = teacher_k[teacher_layer]
        student_query_layer = student_q[section_of, slot_of]
        student_key_layer = student_k[section_of, slot_of]
        scales = student_scale[layer].reshape(groups, STUDENT_HEADS // groups)

        def split_rows(array, replica):
            rows = lax.dynamic_slice_in_dim(array, (replica * REPLICA_TOKENS).astype(jnp.int32), REPLICA_TOKENS, 0)
            return rows.reshape(REPLICA_TOKENS, groups, -1).transpose(1, 0, 2)

        def replica_terms(replica):
            items = (split_rows(teacher_query_layer, replica), split_rows(teacher_key_layer, replica), split_rows(student_query_layer, replica), split_rows(student_key_layer, replica), scales)

            def group_call(group_items):
                return group_terms(group_items[0], group_items[1], group_items[2], group_items[3], group_items[4], mask)
            return lax.map(group_call, items)
        query_grads, key_gradient_list, divergences, scale_terms = lax.map(replica_terms, jnp.arange(N_DP, dtype=jnp.int32))
        query_grads = query_grads.transpose(0, 2, 1, 3).reshape(N_DP * REPLICA_TOKENS, STUDENT_HEADS * HEAD_WIDTH)
        key_gradient_list = key_gradient_list.transpose(0, 2, 1, 3).reshape(N_DP * REPLICA_TOKENS, STUDENT_KEY_HEADS * HEAD_WIDTH)
        query_out = query_out.at[section_of, slot_of].set(query_grads.astype(jnp.bfloat16))
        key_out = key_out.at[section_of, slot_of].set(key_gradient_list.astype(jnp.bfloat16))
        divergence_out = divergence_out.at[:, layer].set(lax.optimization_barrier(jnp.sum(divergences, 1)) / (STUDENT_HEADS * REPLICA_TOKENS))
        scale_out = scale_out.at[layer].set(lax.optimization_barrier(jnp.sum(scale_terms, 0)).reshape(STUDENT_HEADS))
    return (query_out, key_out, divergence_out, scale_out)
```

```python
import functools
import math

import jax
import jax.numpy as jnp
from jax import lax
from jax.experimental import pallas as pl
from jax.experimental.pallas import tpu as pltpu
from jax.sharding import PartitionSpec as P

STUDENT_HEADS = 32
HEAD_WIDTH = 128
TOKENS = 128
LAYERS = 8
SLOTS = 2
HEADS = 4
PACKED = 2 * TOKENS + 8
SCALE_LANE = 32
INVERSE = 1.0 / math.sqrt(HEAD_WIDTH)
HIDDEN = -1e30
AXES = ("section", "head", "dp")


def dot(a, b, over_a, over_b):
    return lax.dot_general(
        a, b, (((over_a,), (over_b,)), ((), ())), preferred_element_type=jnp.float32
    )


def masks():
    row = lax.broadcasted_iota(jnp.int32, (TOKENS, TOKENS), 0)
    col = lax.broadcasted_iota(jnp.int32, (TOKENS, TOKENS), 1)
    return row, col


def log_softmax(scores, visible, axis):
    scores = jnp.where(visible, scores, HIDDEN)
    shifted = scores - jnp.max(scores, axis=axis, keepdims=True)
    return shifted - jnp.log(jnp.sum(jnp.exp(shifted), axis=axis, keepdims=True))


def teacher_kernel(pairing, placement, q_ref, k_ref, out_ref):
    me = lax.axis_index("section")
    home = jnp.int32(0)
    for layer in range(LAYERS):
        home = jnp.where(pairing[layer] == me, placement[layer], home)
    chip = home // 2
    row, col = masks()
    key = k_ref[0]

    def target(head, turned):
        logps = []
        for twin in (2 * head, 2 * head + 1):
            query = q_ref[0, :, twin * HEAD_WIDTH : (twin + 1) * HEAD_WIDTH]
            if turned:
                scores = dot(key, query, 1, 1) * INVERSE
                logps.append(log_softmax(scores, row <= col, 0))
            else:
                scores = dot(query, key, 1, 1) * INVERSE
                logps.append(log_softmax(scores, col <= row, 1))
        one, two = logps
        high = jnp.maximum(one, two)
        return high + jnp.log1p(jnp.exp(-jnp.abs(one - two))) - math.log(2.0)

    for pair in range(HEADS // 2):
        plain = target(2 * pair, False)
        turned = target(2 * pair + 1, True)
        out_ref[chip, pair * TOKENS : (pair + 1) * TOKENS, :] = jnp.where(
            col <= row, plain, turned
        )
        diagonal = jnp.sum(jnp.where(row == col, turned, 0.0), axis=0, keepdims=True)
        at = 2 * TOKENS + pair
        out_ref[chip, at : at + 1, :] = diagonal


def student_kernel(
    pairing, placement, scale_ref, packed_ref, q_ref, k_ref, sums_ref, grad_ref
):
    me = lax.axis_index("section")
    my_chip, my_core = me // 2, lax.rem(me, 2)
    row, col = masks()
    lane = lax.broadcasted_iota(jnp.int32, (1, TOKENS), 1)
    sums_ref[...] = jnp.zeros_like(sums_ref)

    def layer_step(layer, counts):
        home = placement[layer]
        chip, core = home // 2, lax.rem(home, 2)
        here = chip == my_chip
        slot = jnp.where(core == 0, counts[0], counts[1])

        @pl.when(here)
        def _():
            source = pairing[layer]
            source_chip, source_core = source // 2, lax.rem(source, 2)
            key = k_ref[core, slot]
            divergence = jnp.zeros((TOKENS, TOKENS), jnp.float32)
            found = jnp.zeros((1, TOKENS), jnp.float32)
            grads = []
            for head in range(HEADS):
                pair, turned = head // 2, head % 2 == 1
                query = q_ref[core, slot, :, head * HEAD_WIDTH : (head + 1) * HEAD_WIDTH]
                square = packed_ref[
                    source_core, source_chip, pair * TOKENS : (pair + 1) * TOKENS, :
                ]
                scale = scale_ref[layer, head]
                if turned:
                    at = 2 * TOKENS + pair
                    diagonal = packed_ref[source_core, source_chip, at : at + 1, :]
                    visible, axis = row <= col, 0
                    target_logp = jnp.where(
                        row < col, square, jnp.where(row == col, diagonal, HIDDEN)
                    )
                    raw = dot(key, query, 1, 1) * INVERSE
                else:
                    visible, axis = col <= row, 1
                    target_logp = jnp.where(visible, square, HIDDEN)
                    raw = dot(query, key, 1, 1) * INVERSE
                student_logp = log_softmax(scale * raw, visible, axis)
                target = jnp.exp(target_logp)
                divergence += jnp.where(
                    visible, target * (target_logp - student_logp), 0.0
                )
                difference = jnp.where(visible, jnp.exp(student_logp) - target, 0.0)
                found = jnp.where(
                    lane == SCALE_LANE + HEADS * layer + head,
                    jnp.sum(difference * raw),
                    found,
                )
                grads.append((difference * (scale * INVERSE)).astype(jnp.bfloat16))
            found = jnp.where(lane == layer, jnp.sum(divergence), found)
            sums_ref[...] += jnp.broadcast_to(found, sums_ref.shape)

            @pl.when(core == my_core)
            def _():
                for head in range(HEADS):
                    grad_ref[slot, head] = grads[head]

        one = jnp.int32(1)
        return (
            counts[0] + jnp.where(here & (core == 0), one, 0),
            counts[1] + jnp.where(here & (core == 1), one, 0),
        )

    lax.fori_loop(0, LAYERS, layer_step, (jnp.int32(0), jnp.int32(0)))


def gradient_kernel(placement, grad_ref, q_ref, k_ref, q_out, k_out):
    me = lax.axis_index("section")
    held = jnp.int32(0)
    for layer in range(LAYERS):
        held += (placement[layer] == me).astype(jnp.int32)
    for slot in range(SLOTS):

        @pl.when(slot < held)
        def _():
            key = k_ref[0, slot]
            total = jnp.zeros((TOKENS, HEAD_WIDTH), jnp.float32)
            for head in range(HEADS):
                lanes = slice(head * HEAD_WIDTH, (head + 1) * HEAD_WIDTH)
                query = q_ref[0, slot, :, lanes]
                grad = grad_ref[slot, head]
                over = head % 2
                q_out[0, slot, :, lanes] = dot(grad, key, 1 - over, 0).astype(jnp.bfloat16)
                total += dot(grad, query, over, 0)
            k_out[0, slot] = total.astype(jnp.bfloat16)

        @pl.when(slot >= held)
        def _():
            q_out[0, slot] = jnp.zeros(q_out.shape[2:], jnp.bfloat16)
            k_out[0, slot] = jnp.zeros(k_out.shape[2:], jnp.bfloat16)


def final_kernel(rows_ref, kl_ref, scale_ref):
    divergence = jnp.sum(rows_ref[0], axis=0, keepdims=True)
    kl_ref[...] = divergence[:, :LAYERS] / (STUDENT_HEADS * TOKENS)
    terms = jnp.sum(rows_ref[1], axis=0, keepdims=True)
    terms = jnp.broadcast_to(terms, (LAYERS, TOKENS))
    lane = lax.broadcasted_iota(jnp.int32, (LAYERS, TOKENS), 1)
    layer = lax.broadcasted_iota(jnp.int32, (LAYERS, TOKENS), 0)
    at = lane - SCALE_LANE - HEADS * layer
    for head in range(HEADS):
        scale_ref[:, head : head + 1] = jnp.sum(
            jnp.where(at == head, terms, 0.0), axis=1, keepdims=True
        )


VMEM = pl.BlockSpec(memory_space=pltpu.VMEM)
SMEM = pl.BlockSpec(memory_space=pltpu.SMEM)


def cost(flops, moved):
    return pl.CostEstimate(flops=flops, bytes_accessed=moved, transcendentals=0)


def local(chips, groups, teacher_q, teacher_k, student_q, student_k, student_scale, pairing, placement):
    f32, bf16 = jnp.float32, jnp.bfloat16
    over_x = [[2 * x + core for x in range(chips)] for core in range(2)]
    of_chip = [[2 * x, 2 * x + 1] for x in range(chips)]
    members = len(groups[0])

    packed = pl.pallas_call(
        teacher_kernel,
        out_shape=jax.ShapeDtypeStruct((chips, PACKED, TOKENS), f32),
        in_specs=[SMEM, SMEM, VMEM, VMEM],
        out_specs=VMEM,
        cost_estimate=cost(8 * 2 * TOKENS**3, 400_000),
        name="teacher",
    )(pairing, placement, teacher_q, teacher_k)
    arrived = lax.all_to_all(
        packed, "section", 0, 0, tiled=True, axis_index_groups=over_x
    )
    chip_q = lax.all_gather(student_q[0], "section", axis_index_groups=of_chip)
    chip_k = lax.all_gather(student_k[0], "section", axis_index_groups=of_chip)
    chip_packed = lax.all_gather(arrived, "section", axis_index_groups=of_chip)

    sums, grads = pl.pallas_call(
        student_kernel,
        out_shape=(
            jax.ShapeDtypeStruct((members, TOKENS), f32),
            jax.ShapeDtypeStruct((SLOTS, HEADS, TOKENS, TOKENS), bf16),
        ),
        in_specs=[SMEM, SMEM, SMEM, VMEM, VMEM, VMEM],
        out_specs=(VMEM, VMEM),
        cost_estimate=cost(8 * 2 * TOKENS**3, 1_800_000),
        name="student",
    )(pairing, placement, student_scale, chip_packed, chip_q, chip_k)

    rows = lax.all_to_all(
        sums.reshape(members, 1, TOKENS), AXES, 0, 0, tiled=True, axis_index_groups=groups
    )
    q_grad, k_grad = pl.pallas_call(
        gradient_kernel,
        out_shape=(
            jax.ShapeDtypeStruct(student_q.shape, bf16),
            jax.ShapeDtypeStruct(student_k.shape, bf16),
        ),
        in_specs=[SMEM, VMEM, VMEM, VMEM],
        out_specs=(VMEM, VMEM),
        cost_estimate=cost(16 * 2 * TOKENS**3, 900_000),
        name="gradient",
    )(placement, grads, student_q, student_k)

    both = lax.all_gather(
        rows.reshape(members, TOKENS), "section", axis_index_groups=of_chip
    )
    layer_kl, scale_grad = pl.pallas_call(
        final_kernel,
        out_shape=(
            jax.ShapeDtypeStruct((1, LAYERS), f32),
            jax.ShapeDtypeStruct((LAYERS, HEADS), f32),
        ),
        in_specs=[VMEM],
        out_specs=(VMEM, VMEM),
        name="final",
    )(both)
    return (q_grad, k_grad, layer_kl, scale_grad)


def reduction_groups(sections, heads, replicas):
    def flat(section, head, replica):
        return (section * heads + head) * replicas + replica

    chips = range(sections // 2)
    first = [
        [flat(2 * x, h, d) for x in chips for h in range(heads)] for d in range(replicas)
    ]
    second = [
        [flat(2 * x + 1, h, d) for x in chips for d in range(replicas)] for h in range(heads)
    ]
    return first + second


def solution(mesh):
    sections, heads, replicas = (mesh.shape[a] for a in AXES)
    return jax.shard_map(
        functools.partial(local, sections // 2, reduction_groups(sections, heads, replicas)),
        mesh=mesh,
        in_specs=(
            P("section", "dp", "head"),
            P("section", "dp", "head"),
            P("section", None, "dp", "head"),
            P("section", None, "dp", "head"),
            P(None, "head"),
            P(),
            P(),
        ),
        out_specs=(
            P("section", None, "dp", "head"),
            P("section", None, "dp", "head"),
            P("dp", None),
            P(None, "head"),
        ),
        check_vma=False,
    )
```

```python
import functools
import math

import jax
import jax.numpy as jnp
from jax import lax
from jax.experimental import pallas as pl
from jax.experimental.pallas import tpu as pltpu
from jax.sharding import PartitionSpec as P

STUDENT_HEADS = 32
HEAD_WIDTH = 128
TOKENS = 128
LAYERS = 8
SLOTS = 2
HEADS = 4
PACKED = 2 * TOKENS + 8
SCALE_LANE = 32
INVERSE = 1.0 / math.sqrt(HEAD_WIDTH)
HIDDEN = -1e30
AXES = ("section", "head", "dp")


def dot(a, b, over_a, over_b):
    return lax.dot_general(
        a, b, (((over_a,), (over_b,)), ((), ())), preferred_element_type=jnp.float32
    )


def masks():
    row = lax.broadcasted_iota(jnp.int32, (TOKENS, TOKENS), 0)
    col = lax.broadcasted_iota(jnp.int32, (TOKENS, TOKENS), 1)
    return row, col


def log_softmax(scores, visible, axis):
    scores = jnp.where(visible, scores, HIDDEN)
    shifted = scores - jnp.max(scores, axis=axis, keepdims=True)
    return shifted - jnp.log(jnp.sum(jnp.exp(shifted), axis=axis, keepdims=True))


def teacher_kernel(pairing, placement, q_ref, k_ref, out_ref):
    me = lax.axis_index("section")
    home = jnp.int32(0)
    for layer in range(LAYERS):
        home = jnp.where(pairing[layer] == me, placement[layer], home)
    chip = home // 2
    row, col = masks()
    key = k_ref[0]

    def target(head, turned):
        logps = []
        for twin in (2 * head, 2 * head + 1):
            query = q_ref[0, :, twin * HEAD_WIDTH : (twin + 1) * HEAD_WIDTH]
            if turned:
                scores = dot(key, query, 1, 1) * INVERSE
                logps.append(log_softmax(scores, row <= col, 0))
            else:
                scores = dot(query, key, 1, 1) * INVERSE
                logps.append(log_softmax(scores, col <= row, 1))
        one, two = logps
        high = jnp.maximum(one, two)
        return high + jnp.log1p(jnp.exp(-jnp.abs(one - two))) - math.log(2.0)

    for pair in range(HEADS // 2):
        plain = target(2 * pair, False)
        turned = target(2 * pair + 1, True)
        out_ref[chip, pair * TOKENS : (pair + 1) * TOKENS, :] = jnp.where(
            col <= row, plain, turned
        )
        diagonal = jnp.sum(jnp.where(row == col, turned, 0.0), axis=0, keepdims=True)
        at = 2 * TOKENS + pair
        out_ref[chip, at : at + 1, :] = diagonal


def slots_of(placement, me):
    held, layers = jnp.int32(0), [jnp.int32(0)] * SLOTS
    for layer in range(LAYERS):
        here = placement[layer] == me
        layers = [
            jnp.where(here & (held == slot), layer, had) for slot, had in enumerate(layers)
        ]
        held += here.astype(jnp.int32)
    return layers, held


def scores_kernel(placement, scale_ref, q_ref, k_ref, raw_ref, logp_ref):
    layers, held = slots_of(placement, lax.axis_index("section"))
    row, col = masks()
    for slot in range(SLOTS):

        @pl.when(slot < held)
        def _():
            key = k_ref[0, slot]
            for head in range(HEADS):
                query = q_ref[0, slot, :, head * HEAD_WIDTH : (head + 1) * HEAD_WIDTH]
                scale = scale_ref[head, layers[slot]]
                if head % 2:
                    raw = dot(key, query, 1, 1) * INVERSE
                    logp_ref[slot, head] = log_softmax(scale * raw, row <= col, 0)
                else:
                    raw = dot(query, key, 1, 1) * INVERSE
                    logp_ref[slot, head] = log_softmax(scale * raw, col <= row, 1)
                raw_ref[slot, head] = raw


def student_kernel(
    pairing, placement, scale_ref, arrived_ref, swapped_ref, raw_ref, logp_ref, sums_ref, grad_ref
):
    me = lax.axis_index("section")
    layers, held = slots_of(placement, me)
    row, col = masks()
    lane = lax.broadcasted_iota(jnp.int32, (1, TOKENS), 1)
    sums_ref[...] = jnp.zeros_like(sums_ref)
    for slot in range(SLOTS):

        @pl.when(slot < held)
        def _():
            layer = layers[slot]
            source = pairing[layer]
            chip, direct = source // 2, lax.rem(source, 2) == lax.rem(me, 2)

            def packed(at, rows):
                near = arrived_ref[chip, at : at + rows, :]
                far = swapped_ref[chip, at : at + rows, :]
                return jnp.where(direct, near, far)

            divergence = jnp.zeros((TOKENS, TOKENS), jnp.float32)
            found = jnp.zeros((1, TOKENS), jnp.float32)
            for head in range(HEADS):
                pair = head // 2
                scale = scale_ref[head, layer]
                square = packed(pair * TOKENS, TOKENS)
                if head % 2:
                    diagonal = packed(2 * TOKENS + pair, 1)
                    visible = row <= col
                    target_logp = jnp.where(row == col, diagonal, square)
                else:
                    visible = col <= row
                    target_logp = square
                target_logp = jnp.where(visible, target_logp, HIDDEN)
                student_logp = logp_ref[slot, head]
                target = jnp.exp(target_logp)
                divergence += jnp.where(
                    visible, target * (target_logp - student_logp), 0.0
                )
                difference = jnp.where(visible, jnp.exp(student_logp) - target, 0.0)
                found = jnp.where(
                    lane == SCALE_LANE + LAYERS * head + layer,
                    jnp.sum(difference * raw_ref[slot, head]),
                    found,
                )
                grad_ref[slot, head] = (difference * (scale * INVERSE)).astype(jnp.bfloat16)
            sums_ref[...] += jnp.where(lane == layer, jnp.sum(divergence), found)


def gradient_kernel(placement, grad_ref, q_ref, k_ref, q_out, k_out):
    _, held = slots_of(placement, lax.axis_index("section"))
    for slot in range(SLOTS):

        @pl.when(slot < held)
        def _():
            key = k_ref[0, slot]
            total = jnp.zeros((TOKENS, HEAD_WIDTH), jnp.float32)
            for head in range(HEADS):
                lanes = slice(head * HEAD_WIDTH, (head + 1) * HEAD_WIDTH)
                query = q_ref[0, slot, :, lanes]
                grad = grad_ref[slot, head]
                over = head % 2
                q_out[0, slot, :, lanes] = dot(grad, key, 1 - over, 0).astype(jnp.bfloat16)
                total += dot(grad, query, over, 0)
            k_out[0, slot] = total.astype(jnp.bfloat16)

        @pl.when(slot >= held)
        def _():
            q_out[0, slot] = jnp.zeros(q_out.shape[2:], jnp.bfloat16)
            k_out[0, slot] = jnp.zeros(k_out.shape[2:], jnp.bfloat16)


def final_kernel(rows_ref, kl_ref, scale_ref):
    divergence = jnp.sum(rows_ref[0], axis=0, keepdims=True)
    kl_ref[...] = divergence[:, :LAYERS] / (STUDENT_HEADS * TOKENS)
    terms = jnp.sum(rows_ref[1], axis=0, keepdims=True)
    scale_ref[...] = jnp.concatenate(
        [terms[:, SCALE_LANE + LAYERS * h : SCALE_LANE + LAYERS * (h + 1)] for h in range(HEADS)], axis=0
    )


VMEM = pl.BlockSpec(memory_space=pltpu.VMEM)
SMEM = pl.BlockSpec(memory_space=pltpu.SMEM)


def cost(flops, moved):
    return pl.CostEstimate(flops=flops, bytes_accessed=moved, transcendentals=0)


def local(chips, groups, teacher_q, teacher_k, student_q, student_k, student_scale, pairing, placement):
    f32, bf16 = jnp.float32, jnp.bfloat16
    over_x = [[2 * x + core for x in range(chips)] for core in range(2)]
    of_chip = [[2 * x, 2 * x + 1] for x in range(chips)]
    members = len(groups[0])

    packed = pl.pallas_call(
        teacher_kernel,
        out_shape=jax.ShapeDtypeStruct((chips, PACKED, TOKENS), f32),
        in_specs=[SMEM, SMEM, VMEM, VMEM],
        out_specs=VMEM,
        cost_estimate=cost(8 * 2 * TOKENS**3, 400_000),
        name="teacher",
    )(pairing, placement, teacher_q, teacher_k)
    arrived = lax.all_to_all(
        packed, "section", 0, 0, tiled=True, axis_index_groups=over_x
    )
    square = jax.ShapeDtypeStruct((SLOTS, HEADS, TOKENS, TOKENS), f32)
    raw, logp = pl.pallas_call(
        scores_kernel,
        out_shape=(square, square),
        in_specs=[SMEM, SMEM, VMEM, VMEM],
        out_specs=(VMEM, VMEM),
        cost_estimate=cost(8 * 2 * TOKENS**3, 1_400_000),
        name="scores",
    )(placement, student_scale.T, student_q, student_k)
    swap = [(s, s ^ 1) for s in range(2 * chips)]
    swapped = lax.ppermute(arrived, "section", swap)

    sums, grads = pl.pallas_call(
        student_kernel,
        out_shape=(
            jax.ShapeDtypeStruct((1, TOKENS), f32),
            jax.ShapeDtypeStruct((SLOTS, HEADS, TOKENS, TOKENS), bf16),
        ),
        in_specs=[SMEM, SMEM, SMEM, VMEM, VMEM, VMEM, VMEM],
        out_specs=(VMEM, VMEM),
        cost_estimate=cost(8 * 2 * TOKENS**3, 1_800_000),
        name="student",
    )(pairing, placement, student_scale.T, arrived, swapped, raw, logp)

    sums = lax.all_gather(sums, "section", axis_index_groups=of_chip).sum(axis=0)
    rows = lax.all_to_all(
        jnp.broadcast_to(sums[None], (members, 1, TOKENS)),
        AXES,
        0,
        0,
        tiled=True,
        axis_index_groups=groups,
    )
    q_grad, k_grad = pl.pallas_call(
        gradient_kernel,
        out_shape=(
            jax.ShapeDtypeStruct(student_q.shape, bf16),
            jax.ShapeDtypeStruct(student_k.shape, bf16),
        ),
        in_specs=[SMEM, VMEM, VMEM, VMEM],
        out_specs=(VMEM, VMEM),
        cost_estimate=cost(16 * 2 * TOKENS**3, 900_000),
        name="gradient",
    )(placement, grads, student_q, student_k)

    both = lax.all_gather(
        rows.reshape(members, TOKENS), "section", axis_index_groups=of_chip
    )
    layer_kl, scale_grad = pl.pallas_call(
        final_kernel,
        out_shape=(
            jax.ShapeDtypeStruct((1, LAYERS), f32),
            jax.ShapeDtypeStruct((HEADS, LAYERS), f32),
        ),
        in_specs=[VMEM],
        out_specs=(VMEM, VMEM),
        name="final",
    )(both)
    return (q_grad, k_grad, layer_kl, scale_grad.T)


def reduction_groups(sections, heads, replicas):
    def flat(section, head, replica):
        return (section * heads + head) * replicas + replica

    chips = range(sections // 2)
    first = [
        [flat(2 * x, h, d) for x in chips for h in range(heads)] for d in range(replicas)
    ]
    second = [
        [flat(2 * x + 1, h, d) for x in chips for d in range(replicas)] for h in range(heads)
    ]
    return first + second


def solution(mesh):
    sections, heads, replicas = (mesh.shape[a] for a in AXES)
    return jax.shard_map(
        functools.partial(local, sections // 2, reduction_groups(sections, heads, replicas)),
        mesh=mesh,
        in_specs=(
            P("section", "dp", "head"),
            P("section", "dp", "head"),
            P("section", None, "dp", "head"),
            P("section", None, "dp", "head"),
            P(None, "head"),
            P(),
            P(),
        ),
        out_specs=(
            P("section", None, "dp", "head"),
            P("section", None, "dp", "head"),
            P("dp", None),
            P(None, "head"),
        ),
        check_vma=False,
    )
```

```python
import functools
import math

import jax
import jax.numpy as jnp
from jax import lax
from jax.experimental import pallas as pl
from jax.experimental.pallas import tpu as pltpu
from jax.sharding import PartitionSpec as P

STUDENT_HEADS = 32
HEAD_WIDTH = 128
TOKENS = 128
LAYERS = 8
SLOTS = 2
HEADS = 4
PACKED = 2 * TOKENS + 8
SCALE_LANE = 32
INVERSE = 1.0 / math.sqrt(HEAD_WIDTH)
HIDDEN = -1e30
AXES = ("section", "head", "dp")


def dot(a, b, over_a, over_b):
    return lax.dot_general(
        a, b, (((over_a,), (over_b,)), ((), ())), preferred_element_type=jnp.float32
    )


def masks():
    row = lax.broadcasted_iota(jnp.int32, (TOKENS, TOKENS), 0)
    col = lax.broadcasted_iota(jnp.int32, (TOKENS, TOKENS), 1)
    return row, col


def log_softmax(scores, visible, axis):
    scores = jnp.where(visible, scores, HIDDEN)
    shifted = scores - jnp.max(scores, axis=axis, keepdims=True)
    return shifted - jnp.log(jnp.sum(jnp.exp(shifted), axis=axis, keepdims=True))


def teacher_kernel(pairing, placement, q_ref, k_ref, out_ref):
    me = lax.axis_index("section")
    home = jnp.int32(0)
    for layer in range(LAYERS):
        home = jnp.where(pairing[layer] == me, placement[layer], home)
    chip = home // 2
    row, col = masks()
    key = k_ref[0]

    def target(head, turned):
        logps = []
        for twin in (2 * head, 2 * head + 1):
            query = q_ref[0, :, twin * HEAD_WIDTH : (twin + 1) * HEAD_WIDTH]
            if turned:
                scores = dot(key, query, 1, 1) * INVERSE
                logps.append(log_softmax(scores, row <= col, 0))
            else:
                scores = dot(query, key, 1, 1) * INVERSE
                logps.append(log_softmax(scores, col <= row, 1))
        one, two = logps
        high = jnp.maximum(one, two)
        return high + jnp.log1p(jnp.exp(-jnp.abs(one - two))) - math.log(2.0)

    for pair in range(HEADS // 2):
        plain = target(2 * pair, False)
        turned = target(2 * pair + 1, True)
        out_ref[chip, pair * TOKENS : (pair + 1) * TOKENS, :] = jnp.where(
            col <= row, plain, turned
        )
        diagonal = jnp.sum(jnp.where(row == col, turned, 0.0), axis=0, keepdims=True)
        at = 2 * TOKENS + pair
        out_ref[chip, at : at + 1, :] = diagonal


def slots_of(placement, me):
    held, layers = jnp.int32(0), [jnp.int32(0)] * SLOTS
    for layer in range(LAYERS):
        here = placement[layer] == me
        layers = [
            jnp.where(here & (held == slot), layer, had) for slot, had in enumerate(layers)
        ]
        held += here.astype(jnp.int32)
    return layers, held


def scores_kernel(placement, scale_ref, q_ref, k_ref, raw_ref, logp_ref):
    layers, held = slots_of(placement, lax.axis_index("section"))
    row, col = masks()
    for slot in range(SLOTS):

        @pl.when(slot < held)
        def _():
            key = k_ref[0, slot]
            for head in range(HEADS):
                query = q_ref[0, slot, :, head * HEAD_WIDTH : (head + 1) * HEAD_WIDTH]
                scale = scale_ref[head, layers[slot]]
                if head % 2:
                    raw = dot(key, query, 1, 1) * INVERSE
                    logp_ref[slot, head] = log_softmax(scale * raw, row <= col, 0)
                else:
                    raw = dot(query, key, 1, 1) * INVERSE
                    logp_ref[slot, head] = log_softmax(scale * raw, col <= row, 1)
                raw_ref[slot, head] = raw


def student_kernel(
    pairing, placement, scale_ref, arrived_ref, swapped_ref, raw_ref, logp_ref, sums_ref, grad_ref
):
    me = lax.axis_index("section")
    layers, held = slots_of(placement, me)
    row, col = masks()
    lane = lax.broadcasted_iota(jnp.int32, (1, TOKENS), 1)
    sums_ref[...] = jnp.zeros_like(sums_ref)
    for slot in range(SLOTS):

        @pl.when(slot < held)
        def _():
            layer = layers[slot]
            source = pairing[layer]
            chip, direct = source // 2, lax.rem(source, 2) == lax.rem(me, 2)

            def packed(at, rows):
                near = arrived_ref[chip, at : at + rows, :]
                far = swapped_ref[chip, at : at + rows, :]
                return jnp.where(direct, near, far)

            divergence = jnp.zeros((TOKENS, TOKENS), jnp.float32)
            found = jnp.zeros((1, TOKENS), jnp.float32)
            for head in range(HEADS):
                pair = head // 2
                scale = scale_ref[head, layer]
                square = packed(pair * TOKENS, TOKENS)
                if head % 2:
                    diagonal = packed(2 * TOKENS + pair, 1)
                    visible = row <= col
                    target_logp = jnp.where(row == col, diagonal, square)
                else:
                    visible = col <= row
                    target_logp = square
                target_logp = jnp.where(visible, target_logp, HIDDEN)
                student_logp = logp_ref[slot, head]
                target = jnp.exp(target_logp)
                divergence += jnp.where(
                    visible, target * (target_logp - student_logp), 0.0
                )
                difference = jnp.where(visible, jnp.exp(student_logp) - target, 0.0)
                found = jnp.where(
                    lane == SCALE_LANE + LAYERS * head + layer,
                    jnp.sum(difference * raw_ref[slot, head]),
                    found,
                )
                grad_ref[slot, head] = (difference * (scale * INVERSE)).astype(jnp.bfloat16)
            sums_ref[...] += jnp.where(lane == layer, jnp.sum(divergence), found)


def gradient_kernel(placement, grad_ref, q_ref, k_ref, q_out, k_out):
    _, held = slots_of(placement, lax.axis_index("section"))
    for slot in range(SLOTS):

        @pl.when(slot < held)
        def _():
            key = k_ref[0, slot]
            total = jnp.zeros((TOKENS, HEAD_WIDTH), jnp.float32)
            for head in range(HEADS):
                lanes = slice(head * HEAD_WIDTH, (head + 1) * HEAD_WIDTH)
                query = q_ref[0, slot, :, lanes]
                grad = grad_ref[slot, head]
                over = head % 2
                q_out[0, slot, :, lanes] = dot(grad, key, 1 - over, 0).astype(jnp.bfloat16)
                total += dot(grad, query, over, 0)
            k_out[0, slot] = total.astype(jnp.bfloat16)

        @pl.when(slot >= held)
        def _():
            q_out[0, slot] = jnp.zeros(q_out.shape[2:], jnp.bfloat16)
            k_out[0, slot] = jnp.zeros(k_out.shape[2:], jnp.bfloat16)


def final_kernel(rows_ref, kl_ref, scale_ref):
    divergence = jnp.sum(rows_ref[0], axis=0, keepdims=True)
    kl_ref[...] = divergence[:, :LAYERS] / (STUDENT_HEADS * TOKENS)
    terms = jnp.sum(rows_ref[1], axis=0, keepdims=True)
    scale_ref[...] = jnp.concatenate(
        [terms[:, SCALE_LANE + LAYERS * h : SCALE_LANE + LAYERS * (h + 1)] for h in range(HEADS)], axis=0
    )


VMEM = pl.BlockSpec(memory_space=pltpu.VMEM)
SMEM = pl.BlockSpec(memory_space=pltpu.SMEM)


def kept(array):
    return pltpu.with_memory_space_constraint(array, pltpu.VMEM)


def cost(flops, moved):
    return pl.CostEstimate(flops=flops, bytes_accessed=moved, transcendentals=0)


def local(chips, groups, teacher_q, teacher_k, student_q, student_k, student_scale, pairing, placement):
    f32, bf16 = jnp.float32, jnp.bfloat16
    over_x = [[2 * x + core for x in range(chips)] for core in range(2)]
    of_chip = [[2 * x, 2 * x + 1] for x in range(chips)]
    members = len(groups[0])

    packed = pl.pallas_call(
        teacher_kernel,
        out_shape=pltpu.VMEM((chips, PACKED, TOKENS), f32),
        in_specs=[SMEM, SMEM, VMEM, VMEM],
        out_specs=VMEM,
        cost_estimate=cost(8 * 2 * TOKENS**3, 400_000),
        name="teacher",
    )(pairing, placement, teacher_q, teacher_k)
    arrived = lax.all_to_all(
        packed, "section", 0, 0, tiled=True, axis_index_groups=over_x
    )
    square = pltpu.VMEM((SLOTS, HEADS, TOKENS, TOKENS), f32)
    raw, logp = pl.pallas_call(
        scores_kernel,
        out_shape=(square, square),
        in_specs=[SMEM, SMEM, VMEM, VMEM],
        out_specs=(VMEM, VMEM),
        cost_estimate=cost(8 * 2 * TOKENS**3, 1_400_000),
        name="scores",
    )(placement, student_scale.T, student_q, student_k)
    swap = [(s, s ^ 1) for s in range(2 * chips)]
    swapped = lax.ppermute(arrived, "section", swap)

    sums, grads = pl.pallas_call(
        student_kernel,
        out_shape=(
            pltpu.VMEM((1, TOKENS), f32),
            pltpu.VMEM((SLOTS, HEADS, TOKENS, TOKENS), bf16),
        ),
        in_specs=[SMEM, SMEM, SMEM, VMEM, VMEM, VMEM, VMEM],
        out_specs=(VMEM, VMEM),
        cost_estimate=cost(8 * 2 * TOKENS**3, 1_800_000),
        name="student",
    )(pairing, placement, student_scale.T, *map(kept, (arrived, swapped, raw, logp)))

    sums = lax.all_gather(sums, "section", axis_index_groups=of_chip).sum(axis=0)
    rows = lax.all_to_all(
        jnp.broadcast_to(sums[None], (members, 1, TOKENS)),
        AXES,
        0,
        0,
        tiled=True,
        axis_index_groups=groups,
    )
    q_grad, k_grad = pl.pallas_call(
        gradient_kernel,
        out_shape=(
            jax.ShapeDtypeStruct(student_q.shape, bf16),
            jax.ShapeDtypeStruct(student_k.shape, bf16),
        ),
        in_specs=[SMEM, VMEM, VMEM, VMEM],
        out_specs=(VMEM, VMEM),
        cost_estimate=cost(16 * 2 * TOKENS**3, 900_000),
        name="gradient",
    )(placement, kept(grads), student_q, student_k)

    both = lax.all_gather(
        rows.reshape(members, TOKENS), "section", axis_index_groups=of_chip
    )
    layer_kl, scale_grad = pl.pallas_call(
        final_kernel,
        out_shape=(
            jax.ShapeDtypeStruct((1, LAYERS), f32),
            jax.ShapeDtypeStruct((HEADS, LAYERS), f32),
        ),
        in_specs=[VMEM],
        out_specs=(VMEM, VMEM),
        name="final",
    )(kept(both))
    return (q_grad, k_grad, layer_kl, scale_grad.T)


def reduction_groups(sections, heads, replicas):
    def flat(section, head, replica):
        return (section * heads + head) * replicas + replica

    chips = range(sections // 2)
    first = [
        [flat(2 * x, h, d) for x in chips for h in range(heads)] for d in range(replicas)
    ]
    second = [
        [flat(2 * x + 1, h, d) for x in chips for d in range(replicas)] for h in range(heads)
    ]
    return first + second


def solution(mesh):
    sections, heads, replicas = (mesh.shape[a] for a in AXES)
    return jax.shard_map(
        functools.partial(local, sections // 2, reduction_groups(sections, heads, replicas)),
        mesh=mesh,
        in_specs=(
            P("section", "dp", "head"),
            P("section", "dp", "head"),
            P("section", None, "dp", "head"),
            P("section", None, "dp", "head"),
            P(None, "head"),
            P(),
            P(),
        ),
        out_specs=(
            P("section", None, "dp", "head"),
            P("section", None, "dp", "head"),
            P("dp", None),
            P(None, "head"),
        ),
        check_vma=False,
    )
```

```python
import functools
import math

import jax
import jax.numpy as jnp
from jax import lax
from jax.experimental import pallas as pl
from jax.experimental.pallas import tpu as pltpu
from jax.sharding import PartitionSpec as P

STUDENT_HEADS = 32
HEAD_WIDTH = 128
TOKENS = 128
LAYERS = 8
SLOTS = 2
HEADS = 4
PACKED = 2 * TOKENS + 8
SCALE_LANE = 32
INVERSE = 1.0 / math.sqrt(HEAD_WIDTH)
HIDDEN = -1e30
AXES = ("section", "head", "dp")


def dot(a, b, over_a, over_b):
    return lax.dot_general(
        a, b, (((over_a,), (over_b,)), ((), ())), preferred_element_type=jnp.float32
    )


def masks():
    row = lax.broadcasted_iota(jnp.int32, (TOKENS, TOKENS), 0)
    col = lax.broadcasted_iota(jnp.int32, (TOKENS, TOKENS), 1)
    return row, col


def log_softmax(scores, visible, axis):
    scores = jnp.where(visible, scores, HIDDEN)
    shifted = scores - jnp.max(scores, axis=axis, keepdims=True)
    return shifted - jnp.log(jnp.sum(jnp.exp(shifted), axis=axis, keepdims=True))


def teacher_kernel(pairing, placement, q_ref, k_ref, out_ref):
    me = lax.axis_index("section")
    home = jnp.int32(0)
    for layer in range(LAYERS):
        home = jnp.where(pairing[layer] == me, placement[layer], home)
    chip = home // 2
    row, col = masks()
    key = k_ref[0]

    def target(head, turned):
        logps = []
        for twin in (2 * head, 2 * head + 1):
            query = q_ref[0, :, twin * HEAD_WIDTH : (twin + 1) * HEAD_WIDTH]
            if turned:
                scores = dot(key, query, 1, 1) * INVERSE
                logps.append(log_softmax(scores, row <= col, 0))
            else:
                scores = dot(query, key, 1, 1) * INVERSE
                logps.append(log_softmax(scores, col <= row, 1))
        one, two = logps
        high = jnp.maximum(one, two)
        return high + jnp.log1p(jnp.exp(-jnp.abs(one - two))) - math.log(2.0)

    for pair in range(HEADS // 2):
        plain = target(2 * pair, False)
        turned = target(2 * pair + 1, True)
        out_ref[chip, pair * TOKENS : (pair + 1) * TOKENS, :] = jnp.where(
            col <= row, plain, turned
        )
        diagonal = jnp.sum(jnp.where(row == col, turned, 0.0), axis=0, keepdims=True)
        at = 2 * TOKENS + pair
        out_ref[chip, at : at + 1, :] = diagonal


def for_my_layers(pairing, placement, work):
    me = lax.axis_index("section")
    chip, core = me // 2, lax.rem(me, 2)

    def step(layer, carry):
        slots, rank = carry[:2], carry[2]
        home, source = placement[layer], pairing[layer]
        home_core = lax.rem(home, 2)
        here = home // 2 == chip
        mine = here & (lax.rem(source, 2) == core)
        slot = jnp.where(home_core == 0, slots[0], slots[1])

        @pl.when(mine)
        def _():
            work(layer, source // 2, home_core, slot, rank)

        return (
            slots[0] + (here & (home_core == 0)).astype(jnp.int32),
            slots[1] + (here & (home_core == 1)).astype(jnp.int32),
            rank + mine.astype(jnp.int32),
        )

    lax.fori_loop(0, LAYERS, step, (jnp.int32(0),) * 3)


def scores_kernel(pairing, placement, scale_ref, q_ref, k_ref, raw_ref, logp_ref):
    row, col = masks()

    def work(layer, source_chip, home_core, slot, rank):
        key = k_ref[home_core, slot]
        for head in range(HEADS):
            query = q_ref[home_core, slot, :, head * HEAD_WIDTH : (head + 1) * HEAD_WIDTH]
            scale = scale_ref[head, layer]
            if head % 2:
                raw = dot(key, query, 1, 1) * INVERSE
                logp_ref[rank, head] = log_softmax(scale * raw, row <= col, 0)
            else:
                raw = dot(query, key, 1, 1) * INVERSE
                logp_ref[rank, head] = log_softmax(scale * raw, col <= row, 1)
            raw_ref[rank, head] = raw

    for_my_layers(pairing, placement, work)


def student_kernel(
    pairing, placement, scale_ref, arrived_ref, raw_ref, logp_ref, sums_ref, grad_ref, sent_ref
):
    core = lax.rem(lax.axis_index("section"), 2)
    row, col = masks()
    lane = lax.broadcasted_iota(jnp.int32, (1, TOKENS), 1)
    sums_ref[...] = jnp.zeros_like(sums_ref)

    def work(layer, source_chip, home_core, slot, rank):
        divergence = jnp.zeros((TOKENS, TOKENS), jnp.float32)
        found = jnp.zeros((1, TOKENS), jnp.float32)
        grads = []
        for head in range(HEADS):
            pair = head // 2
            scale = scale_ref[head, layer]
            square = arrived_ref[source_chip, pair * TOKENS : (pair + 1) * TOKENS, :]
            if head % 2:
                at = 2 * TOKENS + pair
                diagonal = arrived_ref[source_chip, at : at + 1, :]
                visible = row <= col
                target_logp = jnp.where(row == col, diagonal, square)
            else:
                visible = col <= row
                target_logp = square
            target_logp = jnp.where(visible, target_logp, HIDDEN)
            student_logp = logp_ref[rank, head]
            target = jnp.exp(target_logp)
            divergence += jnp.where(visible, target * (target_logp - student_logp), 0.0)
            difference = jnp.where(visible, jnp.exp(student_logp) - target, 0.0)
            found = jnp.where(
                lane == SCALE_LANE + LAYERS * head + layer,
                jnp.sum(difference * raw_ref[rank, head]),
                found,
            )
            grads.append((difference * (scale * INVERSE)).astype(jnp.bfloat16))
        sums_ref[...] += jnp.where(lane == layer, jnp.sum(divergence), found)

        @pl.when(home_core == core)
        def _():
            for head in range(HEADS):
                grad_ref[slot, head] = grads[head]

        @pl.when(home_core != core)
        def _():
            for head in range(HEADS):
                sent_ref[slot, head] = grads[head]

    for_my_layers(pairing, placement, work)


def spread_kernel(pair_ref, out_ref):
    out_ref[...] = jnp.broadcast_to(pair_ref[0] + pair_ref[1], out_ref.shape)


def gradient_kernel(pairing, placement, grad_ref, sent_ref, q_ref, k_ref, q_out, k_out):
    me = lax.axis_index("section")
    core = lax.rem(me, 2)
    held, layers = jnp.int32(0), [jnp.int32(0)] * SLOTS
    for layer in range(LAYERS):
        here = placement[layer] == me
        layers = [
            jnp.where(here & (held == slot), layer, had) for slot, had in enumerate(layers)
        ]
        held += here.astype(jnp.int32)
    for slot in range(SLOTS):

        @pl.when(slot < held)
        def _():
            direct = lax.rem(pairing[layers[slot]], 2) == core
            key = k_ref[0, slot]
            total = jnp.zeros((TOKENS, HEAD_WIDTH), jnp.float32)
            for head in range(HEADS):
                lanes = slice(head * HEAD_WIDTH, (head + 1) * HEAD_WIDTH)
                query = q_ref[0, slot, :, lanes]
                grad = jnp.where(direct, grad_ref[slot, head], sent_ref[1 - core, slot, head])
                over = head % 2
                q_out[0, slot, :, lanes] = dot(grad, key, 1 - over, 0).astype(jnp.bfloat16)
                total += dot(grad, query, over, 0)
            k_out[0, slot] = total.astype(jnp.bfloat16)

        @pl.when(slot >= held)
        def _():
            q_out[0, slot] = jnp.zeros(q_out.shape[2:], jnp.bfloat16)
            k_out[0, slot] = jnp.zeros(k_out.shape[2:], jnp.bfloat16)


def final_kernel(rows_ref, kl_ref, scale_ref):
    divergence = jnp.sum(rows_ref[0], axis=0, keepdims=True)
    kl_ref[...] = divergence[:, :LAYERS] / (STUDENT_HEADS * TOKENS)
    terms = jnp.sum(rows_ref[1], axis=0, keepdims=True)
    scale_ref[...] = jnp.concatenate(
        [terms[:, SCALE_LANE + LAYERS * h : SCALE_LANE + LAYERS * (h + 1)] for h in range(HEADS)], axis=0
    )


VMEM = pl.BlockSpec(memory_space=pltpu.VMEM)
SMEM = pl.BlockSpec(memory_space=pltpu.SMEM)
SMALL = pltpu.CompilerParams(vmem_limit_bytes=16 * 2**20)


def kept(array):
    return pltpu.with_memory_space_constraint(array, pltpu.VMEM)


def cost(flops, moved):
    return pl.CostEstimate(flops=flops, bytes_accessed=moved, transcendentals=0)


def local(chips, groups, teacher_q, teacher_k, student_q, student_k, student_scale, pairing, placement):
    f32, bf16 = jnp.float32, jnp.bfloat16
    over_x = [[2 * x + core for x in range(chips)] for core in range(2)]
    of_chip = [[2 * x, 2 * x + 1] for x in range(chips)]
    members = len(groups[0])

    packed = pl.pallas_call(
        teacher_kernel,
        out_shape=pltpu.VMEM((chips, PACKED, TOKENS), f32),
        in_specs=[SMEM, SMEM, VMEM, VMEM],
        out_specs=VMEM,
        cost_estimate=cost(8 * 2 * TOKENS**3, 400_000),
        name="teacher",
    )(pairing, placement, teacher_q, teacher_k)
    arrived = lax.all_to_all(
        packed, "section", 0, 0, tiled=True, axis_index_groups=over_x
    )
    def of_both_cores(array):
        return lax.all_gather(array, "section", axis_index_groups=of_chip)

    at_once = 2 * SLOTS
    square = pltpu.VMEM((at_once, HEADS, TOKENS, TOKENS), f32)
    raw, logp = pl.pallas_call(
        scores_kernel,
        out_shape=(square, square),
        in_specs=[SMEM, SMEM, SMEM, VMEM, VMEM],
        out_specs=(VMEM, VMEM),
        cost_estimate=cost(8 * 2 * TOKENS**3, 1_400_000),
        compiler_params=SMALL,
        name="scores",
    )(
        pairing,
        placement,
        student_scale.T,
        kept(of_both_cores(student_q[0])),
        kept(of_both_cores(student_k[0])),
    )

    grad_shape = pltpu.VMEM((SLOTS, HEADS, TOKENS, TOKENS), bf16)
    sums, grads, sent = pl.pallas_call(
        student_kernel,
        out_shape=(pltpu.VMEM((1, TOKENS), f32), grad_shape, grad_shape),
        in_specs=[SMEM, SMEM, SMEM, VMEM, VMEM, VMEM],
        out_specs=(VMEM, VMEM, VMEM),
        cost_estimate=cost(8 * 2 * TOKENS**3, 1_800_000),
        compiler_params=SMALL,
        name="student",
    )(pairing, placement, student_scale.T, *map(kept, (arrived, raw, logp)))

    sums = pl.pallas_call(
        spread_kernel,
        out_shape=pltpu.VMEM((members, TOKENS), f32),
        in_specs=[VMEM],
        out_specs=VMEM,
        compiler_params=SMALL,
        name="spread",
    )(kept(of_both_cores(sums)))
    rows = lax.all_to_all(
        sums.reshape(members, 1, TOKENS), AXES, 0, 0, tiled=True, axis_index_groups=groups
    )
    q_grad, k_grad = pl.pallas_call(
        gradient_kernel,
        out_shape=(
            jax.ShapeDtypeStruct(student_q.shape, bf16),
            jax.ShapeDtypeStruct(student_k.shape, bf16),
        ),
        in_specs=[SMEM, SMEM, VMEM, VMEM, VMEM, VMEM],
        out_specs=(VMEM, VMEM),
        cost_estimate=cost(16 * 2 * TOKENS**3, 900_000),
        compiler_params=SMALL,
        name="gradient",
    )(pairing, placement, kept(grads), kept(of_both_cores(sent)), student_q, student_k)

    both = of_both_cores(rows.reshape(members, TOKENS))
    layer_kl, scale_grad = pl.pallas_call(
        final_kernel,
        out_shape=(
            jax.ShapeDtypeStruct((1, LAYERS), f32),
            jax.ShapeDtypeStruct((HEADS, LAYERS), f32),
        ),
        in_specs=[VMEM],
        out_specs=(VMEM, VMEM),
        compiler_params=SMALL,
        name="final",
    )(kept(both))
    return (q_grad, k_grad, layer_kl, scale_grad.T)


def reduction_groups(sections, heads, replicas):
    def flat(section, head, replica):
        return (section * heads + head) * replicas + replica

    chips = range(sections // 2)
    first = [
        [flat(2 * x, h, d) for x in chips for h in range(heads)] for d in range(replicas)
    ]
    second = [
        [flat(2 * x + 1, h, d) for x in chips for d in range(replicas)] for h in range(heads)
    ]
    return first + second


def solution(mesh):
    sections, heads, replicas = (mesh.shape[a] for a in AXES)
    return jax.shard_map(
        functools.partial(local, sections // 2, reduction_groups(sections, heads, replicas)),
        mesh=mesh,
        in_specs=(
            P("section", "dp", "head"),
            P("section", "dp", "head"),
            P("section", None, "dp", "head"),
            P("section", None, "dp", "head"),
            P(None, "head"),
            P(),
            P(),
        ),
        out_specs=(
            P("section", None, "dp", "head"),
            P("section", None, "dp", "head"),
            P("dp", None),
            P(None, "head"),
        ),
        check_vma=False,
    )
```

```python
import functools
import math

import jax
import jax.numpy as jnp
from jax import lax
from jax.experimental import pallas as pl
from jax.experimental.pallas import tpu as pltpu
from jax.sharding import PartitionSpec as P

STUDENT_HEADS = 32
HEAD_WIDTH = 128
TOKENS = 128
LAYERS = 8
SLOTS = 2
HEADS = 4
PACKED = 2 * TOKENS + 8
SCALE_LANE = 32
INVERSE = 1.0 / math.sqrt(HEAD_WIDTH)
HIDDEN = -1e30
AXES = ("section", "head", "dp")


def dot(a, b, over_a, over_b):
    return lax.dot_general(
        a, b, (((over_a,), (over_b,)), ((), ())), preferred_element_type=jnp.float32
    )


def masks():
    row = lax.broadcasted_iota(jnp.int32, (TOKENS, TOKENS), 0)
    col = lax.broadcasted_iota(jnp.int32, (TOKENS, TOKENS), 1)
    return row, col


def log_softmax(scores, visible, axis):
    scores = jnp.where(visible, scores, HIDDEN)
    shifted = scores - jnp.max(scores, axis=axis, keepdims=True)
    return shifted - jnp.log(jnp.sum(jnp.exp(shifted), axis=axis, keepdims=True))


def teacher_kernel(
    pairing, placement, q_hbm, k_hbm, out_ref, q_ref, k_ref, packed, in_sems, out_sems
):
    def part(head):
        lanes = slice(2 * head * HEAD_WIDTH, 2 * (head + 1) * HEAD_WIDTH)
        return pltpu.make_async_copy(
            q_hbm.at[0, :, lanes], q_ref.at[head], in_sems.at[head]
        )

    keys = pltpu.make_async_copy(k_hbm.at[0], k_ref, in_sems.at[HEADS])
    keys.start()
    for head in range(HEADS):
        part(head).start()

    me = lax.axis_index("section")
    home = jnp.int32(0)
    for layer in range(LAYERS):
        home = jnp.where(pairing[layer] == me, placement[layer], home)
    chip = home // 2
    row, col = masks()
    keys.wait()
    key = k_ref[...]

    def target(head, turned):
        part(head).wait()
        logps = []
        for twin in range(2):
            query = q_ref[head, :, twin * HEAD_WIDTH : (twin + 1) * HEAD_WIDTH]
            if turned:
                scores = dot(key, query, 1, 1) * INVERSE
                logps.append(log_softmax(scores, row <= col, 0))
            else:
                scores = dot(query, key, 1, 1) * INVERSE
                logps.append(log_softmax(scores, col <= row, 1))
        one, two = logps
        high = jnp.maximum(one, two)
        return high + jnp.log1p(jnp.exp(-jnp.abs(one - two))) - math.log(2.0)

    pairs = HEADS // 2
    packed[pairs * TOKENS :, :] = jnp.zeros((PACKED - pairs * TOKENS, TOKENS), jnp.float32)
    started = []
    for pair in range(pairs):
        plain = target(2 * pair, False)
        turned = target(2 * pair + 1, True)
        packed[pair * TOKENS : (pair + 1) * TOKENS, :] = jnp.where(col <= row, plain, turned)
        at = pairs * TOKENS + pair
        packed[at : at + 1, :] = jnp.sum(
            jnp.where(row == col, turned, 0.0), axis=0, keepdims=True
        )
        end = (pair + 1) * TOKENS if pair < pairs - 1 else PACKED
        rows = slice(pair * TOKENS, end)
        copy = pltpu.make_async_copy(
            packed.at[rows, :], out_ref.at[chip, rows, :], out_sems.at[pair]
        )
        copy.start()
        started.append(copy)
    for copy in started:
        copy.wait()


def for_my_layers(pairing, placement, work):
    me = lax.axis_index("section")
    chip, core = me // 2, lax.rem(me, 2)

    def step(layer, carry):
        slots, rank = carry[:2], carry[2]
        home, source = placement[layer], pairing[layer]
        home_core = lax.rem(home, 2)
        here = home // 2 == chip
        mine = here & (lax.rem(source, 2) == core)
        slot = jnp.where(home_core == 0, slots[0], slots[1])

        @pl.when(mine)
        def _():
            work(layer, source // 2, home_core, slot, rank)

        return (
            slots[0] + (here & (home_core == 0)).astype(jnp.int32),
            slots[1] + (here & (home_core == 1)).astype(jnp.int32),
            rank + mine.astype(jnp.int32),
        )

    lax.fori_loop(0, LAYERS, step, (jnp.int32(0),) * 3)


def scores_kernel(pairing, placement, scale_ref, q_ref, k_ref, raw_ref, logp_ref):
    row, col = masks()

    def work(layer, source_chip, home_core, slot, rank):
        key = k_ref[home_core, slot]
        for head in range(HEADS):
            query = q_ref[home_core, slot, :, head * HEAD_WIDTH : (head + 1) * HEAD_WIDTH]
            scale = scale_ref[head, layer]
            if head % 2:
                raw = dot(key, query, 1, 1) * INVERSE
                logp_ref[rank, head] = log_softmax(scale * raw, row <= col, 0)
            else:
                raw = dot(query, key, 1, 1) * INVERSE
                logp_ref[rank, head] = log_softmax(scale * raw, col <= row, 1)
            raw_ref[rank, head] = raw

    for_my_layers(pairing, placement, work)


def student_kernel(
    pairing, placement, scale_ref, arrived_ref, raw_ref, logp_ref, sums_ref, grad_ref, sent_ref
):
    core = lax.rem(lax.axis_index("section"), 2)
    row, col = masks()
    lane = lax.broadcasted_iota(jnp.int32, (1, TOKENS), 1)
    sums_ref[...] = jnp.zeros_like(sums_ref)

    def work(layer, source_chip, home_core, slot, rank):
        divergence = jnp.zeros((TOKENS, TOKENS), jnp.float32)
        found = jnp.zeros((1, TOKENS), jnp.float32)
        grads = []
        for head in range(HEADS):
            pair = head // 2
            scale = scale_ref[head, layer]
            square = arrived_ref[source_chip, pair * TOKENS : (pair + 1) * TOKENS, :]
            if head % 2:
                at = 2 * TOKENS + pair
                diagonal = arrived_ref[source_chip, at : at + 1, :]
                visible = row <= col
                target_logp = jnp.where(row == col, diagonal, square)
            else:
                visible = col <= row
                target_logp = square
            target_logp = jnp.where(visible, target_logp, HIDDEN)
            student_logp = logp_ref[rank, head]
            target = jnp.exp(target_logp)
            divergence += jnp.where(visible, target * (target_logp - student_logp), 0.0)
            difference = jnp.where(visible, jnp.exp(student_logp) - target, 0.0)
            found = jnp.where(
                lane == SCALE_LANE + LAYERS * head + layer,
                jnp.sum(difference * raw_ref[rank, head]),
                found,
            )
            grads.append((difference * (scale * INVERSE)).astype(jnp.bfloat16))
        found = jnp.where(lane == layer, jnp.sum(divergence), found)
        sums_ref[...] += jnp.broadcast_to(found, sums_ref.shape)

        @pl.when(home_core == core)
        def _():
            for head in range(HEADS):
                grad_ref[slot, head] = grads[head]

        @pl.when(home_core != core)
        def _():
            for head in range(HEADS):
                sent_ref[slot, head] = grads[head]

    for_my_layers(pairing, placement, work)


def gradient_kernel(pairing, placement, grad_ref, sent_ref, q_ref, k_ref, q_out, k_out):
    me = lax.axis_index("section")
    core = lax.rem(me, 2)
    held, layers = jnp.int32(0), [jnp.int32(0)] * SLOTS
    for layer in range(LAYERS):
        here = placement[layer] == me
        layers = [
            jnp.where(here & (held == slot), layer, had) for slot, had in enumerate(layers)
        ]
        held += here.astype(jnp.int32)
    for slot in range(SLOTS):

        @pl.when(slot < held)
        def _():
            direct = lax.rem(pairing[layers[slot]], 2) == core
            key = k_ref[core, slot]
            total = jnp.zeros((TOKENS, HEAD_WIDTH), jnp.float32)
            for head in range(HEADS):
                lanes = slice(head * HEAD_WIDTH, (head + 1) * HEAD_WIDTH)
                query = q_ref[core, slot, :, lanes]
                grad = jnp.where(direct, grad_ref[slot, head], sent_ref[1 - core, slot, head])
                over = head % 2
                q_out[0, slot, :, lanes] = dot(grad, key, 1 - over, 0).astype(jnp.bfloat16)
                total += dot(grad, query, over, 0)
            k_out[0, slot] = total.astype(jnp.bfloat16)

        @pl.when(slot >= held)
        def _():
            q_out[0, slot] = jnp.zeros(q_out.shape[2:], jnp.bfloat16)
            k_out[0, slot] = jnp.zeros(k_out.shape[2:], jnp.bfloat16)


def final_kernel(rows_ref, kl_ref, scale_ref):
    divergence = jnp.sum(rows_ref[0], axis=0, keepdims=True)
    kl_ref[...] = divergence[:, :LAYERS] / (STUDENT_HEADS * TOKENS)
    terms = jnp.sum(rows_ref[1], axis=0, keepdims=True)
    scale_ref[...] = jnp.concatenate(
        [terms[:, SCALE_LANE + LAYERS * h : SCALE_LANE + LAYERS * (h + 1)] for h in range(HEADS)], axis=0
    )


VMEM = pl.BlockSpec(memory_space=pltpu.VMEM)
ANY = pl.BlockSpec(memory_space=pl.ANY)
SMEM = pl.BlockSpec(memory_space=pltpu.SMEM)
SMALL = pltpu.CompilerParams(vmem_limit_bytes=16 * 2**20)


def far(array):
    return pltpu.with_memory_space_constraint(array, pltpu.HBM)


def kept(array):
    return pltpu.with_memory_space_constraint(array, pltpu.VMEM)


def cost(flops, moved):
    return pl.CostEstimate(flops=flops, bytes_accessed=moved, transcendentals=0)


def local(chips, groups, teacher_q, teacher_k, student_q, student_k, student_scale, pairing, placement):
    f32, bf16 = jnp.float32, jnp.bfloat16
    over_x = [[2 * x + core for x in range(chips)] for core in range(2)]
    of_chip = [[2 * x, 2 * x + 1] for x in range(chips)]
    members = len(groups[0])

    pairing, placement, scales = map(far, (pairing, placement, student_scale.T))
    packed = pl.pallas_call(
        teacher_kernel,
        out_shape=jax.ShapeDtypeStruct((chips, PACKED, TOKENS), f32),
        in_specs=[SMEM, SMEM, ANY, ANY],
        out_specs=ANY,
        scratch_shapes=[
            pltpu.VMEM((HEADS, TOKENS, 2 * HEAD_WIDTH), bf16),
            pltpu.VMEM((TOKENS, HEAD_WIDTH), bf16),
            pltpu.VMEM((PACKED, TOKENS), f32),
            pltpu.SemaphoreType.DMA((HEADS + 1,)),
            pltpu.SemaphoreType.DMA((HEADS // 2,)),
        ],
        cost_estimate=cost(8 * 2 * TOKENS**3, 400_000),
        name="teacher",
    )(pairing, placement, teacher_q, teacher_k)
    arrived = lax.all_to_all(
        packed, "section", 0, 0, tiled=True, axis_index_groups=over_x
    )
    def of_both_cores(array):
        return lax.all_gather(array, "section", axis_index_groups=of_chip)

    chip_q, chip_k = (kept(of_both_cores(a[0])) for a in (student_q, student_k))
    at_once = 2 * SLOTS
    square = pltpu.VMEM((at_once, HEADS, TOKENS, TOKENS), f32)
    raw, logp = pl.pallas_call(
        scores_kernel,
        out_shape=(square, square),
        in_specs=[SMEM, SMEM, SMEM, VMEM, VMEM],
        out_specs=(VMEM, VMEM),
        cost_estimate=cost(8 * 2 * TOKENS**3, 1_400_000),
        compiler_params=SMALL,
        name="scores",
    )(
        pairing,
        placement,
        scales,
        chip_q,
        chip_k,
    )

    grad_shape = pltpu.VMEM((SLOTS, HEADS, TOKENS, TOKENS), bf16)
    sums, grads, sent = pl.pallas_call(
        student_kernel,
        out_shape=(pltpu.HBM((members, TOKENS), f32), grad_shape, pltpu.HBM(grad_shape.shape, bf16)),
        in_specs=[SMEM, SMEM, SMEM, VMEM, VMEM, VMEM],
        out_specs=(VMEM, VMEM, VMEM),
        cost_estimate=cost(8 * 2 * TOKENS**3, 1_800_000),
        compiler_params=SMALL,
        name="student",
    )(pairing, placement, scales, *map(kept, (arrived, raw, logp)))

    sums = lax.psum(sums, "section", axis_index_groups=of_chip)
    rows = lax.all_to_all(
        sums.reshape(members, 1, TOKENS), AXES, 0, 0, tiled=True, axis_index_groups=groups
    )
    q_grad, k_grad = pl.pallas_call(
        gradient_kernel,
        out_shape=(
            jax.ShapeDtypeStruct(student_q.shape, bf16),
            jax.ShapeDtypeStruct(student_k.shape, bf16),
        ),
        in_specs=[SMEM, SMEM, VMEM, VMEM, VMEM, VMEM],
        out_specs=(VMEM, VMEM),
        cost_estimate=cost(16 * 2 * TOKENS**3, 900_000),
        compiler_params=SMALL,
        name="gradient",
    )(pairing, placement, kept(grads), kept(of_both_cores(sent)), chip_q, chip_k)

    both = of_both_cores(rows.reshape(members, TOKENS))
    layer_kl, scale_grad = pl.pallas_call(
        final_kernel,
        out_shape=(
            jax.ShapeDtypeStruct((1, LAYERS), f32),
            jax.ShapeDtypeStruct((HEADS, LAYERS), f32),
        ),
        in_specs=[VMEM],
        out_specs=(VMEM, VMEM),
        compiler_params=SMALL,
        name="final",
    )(kept(both))
    return (q_grad, k_grad, layer_kl, scale_grad.T)


def reduction_groups(sections, heads, replicas):
    def flat(section, head, replica):
        return (section * heads + head) * replicas + replica

    chips = range(sections // 2)
    first = [
        [flat(2 * x, h, d) for x in chips for h in range(heads)] for d in range(replicas)
    ]
    second = [
        [flat(2 * x + 1, h, d) for x in chips for d in range(replicas)] for h in range(heads)
    ]
    return first + second


def solution(mesh):
    sections, heads, replicas = (mesh.shape[a] for a in AXES)
    return jax.shard_map(
        functools.partial(local, sections // 2, reduction_groups(sections, heads, replicas)),
        mesh=mesh,
        in_specs=(
            P("section", "dp", "head"),
            P("section", "dp", "head"),
            P("section", None, "dp", "head"),
            P("section", None, "dp", "head"),
            P(None, "head"),
            P(),
            P(),
        ),
        out_specs=(
            P("section", None, "dp", "head"),
            P("section", None, "dp", "head"),
            P("dp", None),
            P(None, "head"),
        ),
        check_vma=False,
    )
```

```python
import functools
import math

import jax
import jax.numpy as jnp
from jax import lax
from jax.experimental import pallas as pl
from jax.experimental.pallas import tpu as pltpu
from jax.sharding import PartitionSpec as P

STUDENT_HEADS = 32
HEAD_WIDTH = 128
TOKENS = 128
LAYERS = 8
SLOTS = 2
HEADS = 4
PACKED = HEADS // 2 * TOKENS + 8
SCALE_LANE = 32
PAIRS = HEADS // 2
TAIL = 16
SLOT_ROWS = PAIRS * TOKENS + TAIL
SENT = SLOTS * SLOT_ROWS
INVERSE = 1.0 / math.sqrt(HEAD_WIDTH)
HIDDEN = -1e30
AXES = ("section", "head", "dp")


def dot(a, b, over_a, over_b):
    return lax.dot_general(
        a, b, (((over_a,), (over_b,)), ((), ())), preferred_element_type=jnp.float32
    )


def masks():
    row = lax.broadcasted_iota(jnp.int32, (TOKENS, TOKENS), 0)
    col = lax.broadcasted_iota(jnp.int32, (TOKENS, TOKENS), 1)
    return row, col


def log_softmax(scores, visible, axis):
    scores = jnp.where(visible, scores, HIDDEN)
    shifted = scores - jnp.max(scores, axis=axis, keepdims=True)
    return shifted - jnp.log(jnp.sum(jnp.exp(shifted), axis=axis, keepdims=True))


def teacher_kernel(
    pairing, placement, scale_ref, q_ref, k_ref, out_ref, table_ref, scale_out, packed, sems
):
    me = lax.axis_index("section")
    home = jnp.int32(0)
    for layer in range(LAYERS):
        home = jnp.where(pairing[layer] == me, placement[layer], home)
    chip = home // 2
    row, col = masks()
    key = k_ref[0]

    scale_out[...] = scale_ref[...]
    at_row = lax.broadcasted_iota(jnp.int32, (8, TOKENS), 0)
    at_lane = lax.broadcasted_iota(jnp.int32, (8, TOKENS), 1)
    table = jnp.zeros((8, TOKENS), jnp.int32)
    for layer in range(LAYERS):
        entry = jnp.where(at_row == 0, pairing[layer], placement[layer])
        table = jnp.where(at_lane == layer, entry, table)
    table_ref[...] = table

    def target(head, turned):
        logps = []
        for twin in (2 * head, 2 * head + 1):
            query = q_ref[0, :, twin * HEAD_WIDTH : (twin + 1) * HEAD_WIDTH]
            if turned:
                scores = dot(key, query, 1, 1) * INVERSE
                logps.append(log_softmax(scores, row <= col, 0))
            else:
                scores = dot(query, key, 1, 1) * INVERSE
                logps.append(log_softmax(scores, col <= row, 1))
        one, two = logps
        high = jnp.maximum(one, two)
        return high + jnp.log1p(jnp.exp(-jnp.abs(one - two))) - math.log(2.0)

    packed[PAIRS * TOKENS :, :] = jnp.zeros((PACKED - PAIRS * TOKENS, TOKENS), jnp.float32)
    started = []
    for pair in range(PAIRS):
        plain = target(2 * pair, False)
        turned = target(2 * pair + 1, True)
        packed[pair * TOKENS : (pair + 1) * TOKENS, :] = jnp.where(col <= row, plain, turned)
        at = PAIRS * TOKENS + pair
        packed[at : at + 1, :] = jnp.sum(
            jnp.where(row == col, turned, 0.0), axis=0, keepdims=True
        )
        end = (pair + 1) * TOKENS if pair < PAIRS - 1 else PACKED
        rows = slice(pair * TOKENS, end)
        copy = pltpu.make_async_copy(
            packed.at[rows, :], out_ref.at[chip, rows, :], sems.at[pair]
        )
        copy.start()
        started.append(copy)
    for copy in started:
        copy.wait()


def for_my_layers(table, work):
    me = lax.axis_index("section")
    chip, core = me // 2, lax.rem(me, 2)

    def step(layer, carry):
        slots, rank = carry[:2], carry[2]
        source, home = table[0, layer], table[1, layer]
        home_core = lax.rem(home, 2)
        here = home // 2 == chip
        mine = here & (lax.rem(source, 2) == core)
        slot = jnp.where(home_core == 0, slots[0], slots[1])

        @pl.when(mine)
        def _():
            work(layer, source // 2, home_core, slot, rank)

        return (
            slots[0] + (here & (home_core == 0)).astype(jnp.int32),
            slots[1] + (here & (home_core == 1)).astype(jnp.int32),
            rank + mine.astype(jnp.int32),
        )

    lax.fori_loop(0, LAYERS, step, (jnp.int32(0),) * 3)


def pack(ref, rank, pair, plain, turned):
    row, col = masks()
    ref[rank, pair * TOKENS : (pair + 1) * TOKENS, :] = jnp.where(col <= row, plain, turned)
    at = PAIRS * TOKENS + pair
    ref[rank, at : at + 1, :] = jnp.sum(
        jnp.where(row == col, turned, 0.0), axis=0, keepdims=True
    )


def scores_kernel(table, scale_ref, q_ref, k_ref, raw_ref, logp_ref):
    row, col = masks()

    def work(layer, source_chip, home_core, slot, rank):
        key = k_ref[home_core, slot]

        def query(head):
            return q_ref[home_core, slot, :, head * HEAD_WIDTH : (head + 1) * HEAD_WIDTH]

        empty = jnp.zeros((PACKED - PAIRS * TOKENS, TOKENS), jnp.float32)
        raw_ref[rank, PAIRS * TOKENS :, :] = empty
        logp_ref[rank, PAIRS * TOKENS :, :] = empty
        for pair in range(PAIRS):
            plain = dot(query(2 * pair), key, 1, 1) * INVERSE
            turned = dot(key, query(2 * pair + 1), 1, 1) * INVERSE
            pack(raw_ref, rank, pair, plain, turned)
            plain = log_softmax(scale_ref[2 * pair, layer] * plain, col <= row, 1)
            turned = log_softmax(scale_ref[2 * pair + 1, layer] * turned, row <= col, 0)
            pack(logp_ref, rank, pair, plain, turned)

    for_my_layers(table, work)


def student_kernel(table, scale_ref, arrived_ref, raw_ref, logp_ref, grad_ref, sent_ref, sums_ref):
    core = lax.rem(lax.axis_index("section"), 2)
    row, col = masks()
    lower = col <= row
    place = lax.broadcasted_iota(jnp.int32, (8, TOKENS), 0)
    lane = lax.broadcasted_iota(jnp.int32, (8, TOKENS), 1)
    tail_row = lax.broadcasted_iota(jnp.int32, (TAIL, TOKENS), 0)
    sums_ref[...] = jnp.zeros_like(sums_ref)

    def work(layer, source_chip, home_core, slot, rank):
        def terms(rows):
            target_logp = arrived_ref[source_chip, rows, :]
            student_logp = logp_ref[rank, rows, :]
            target = jnp.exp(target_logp)
            difference = jnp.exp(student_logp) - target
            return (
                jnp.sum(target * (target_logp - student_logp), axis=0, keepdims=True),
                difference,
                difference * raw_ref[rank, rows, :],
            )

        last, last_difference, last_moved = terms(slice(PAIRS * TOKENS, PACKED))
        found = jnp.zeros((8, TOKENS), jnp.float32)
        divergence = last
        tail = jnp.zeros((TAIL, TOKENS), jnp.float32)
        pieces = []
        for pair in range(PAIRS):
            one, difference, moved = terms(slice(pair * TOKENS, (pair + 1) * TOKENS))
            divergence += one
            first = scale_ref[2 * pair, layer] * INVERSE
            second = scale_ref[2 * pair + 1, layer] * INVERSE
            pieces.append(difference * jnp.where(lower, first, second))
            tail = jnp.where(tail_row == pair, last_difference[pair : pair + 1] * second, tail)
            of_first = jnp.sum(jnp.where(lower, moved, 0.0), axis=0, keepdims=True)
            of_second = jnp.sum(jnp.where(lower, 0.0, moved), axis=0, keepdims=True)
            of_second += last_moved[pair : pair + 1]
            found = jnp.where(place == 1 + 2 * pair, of_first, found)
            found = jnp.where(place == 2 + 2 * pair, of_second, found)
        found = jnp.where(place == 0, divergence, found)
        found = jnp.sum(found, axis=1, keepdims=True)
        goes_to = jnp.where(place == 0, layer, SCALE_LANE + LAYERS * (place - 1) + layer)
        found = jnp.where((lane == goes_to) & (place <= HEADS), found, 0.0)
        sums_ref[...] += jnp.sum(found, axis=0, keepdims=True)
        pieces.append(tail)

        def put(ref, at):
            for n, piece in enumerate(pieces):
                to = pl.multiple_of(at + n * TOKENS, TAIL)
                ref[pl.ds(to, piece.shape[0]), :] = piece.astype(jnp.bfloat16)

        @pl.when(home_core == core)
        def _():
            put(grad_ref, slot * SLOT_ROWS)

        @pl.when(home_core != core)
        def _():
            put(sent_ref, slot * SLOT_ROWS)

    for_my_layers(table, work)
    left, tile = sums_ref[...], jnp.zeros((TAIL, TOKENS), jnp.float32)
    for term in range(3):
        part = left.astype(jnp.bfloat16).astype(jnp.float32)
        tile = jnp.where(tail_row == term, part, tile)
        left -= part
    sent_ref[SENT:, :] = tile.astype(jnp.bfloat16)


def spread_kernel(pair_ref, out_ref):
    terms = pair_ref[:, SENT:, :].astype(jnp.float32)
    total = jnp.zeros((1, TOKENS), jnp.float32)
    for core in range(2):
        total += (terms[core, 0:1] + terms[core, 1:2]) + terms[core, 2:3]
    out_ref[...] = jnp.broadcast_to(total, out_ref.shape)


def gradient_kernel(table, grad_ref, sent_ref, q_ref, k_ref, q_out, k_out):
    me = lax.axis_index("section")
    core = lax.rem(me, 2)
    row, col = masks()
    held, layers = jnp.int32(0), [jnp.int32(0)] * SLOTS
    for layer in range(LAYERS):
        here = table[1, layer] == me
        layers = [
            jnp.where(here & (held == slot), layer, had) for slot, had in enumerate(layers)
        ]
        held += here.astype(jnp.int32)
    for slot in range(SLOTS):

        @pl.when(slot < held)
        def _():
            direct = lax.rem(table[0, layers[slot]], 2) == core
            key = k_ref[core, slot]
            total = jnp.zeros((TOKENS, HEAD_WIDTH), jnp.float32)

            def rows(at, count):
                at = slot * SLOT_ROWS + at
                near = grad_ref[at : at + count, :].astype(jnp.float32)
                other = sent_ref[1 - core, at : at + count, :].astype(jnp.float32)
                return jnp.where(direct, near, other)

            tail = rows(PAIRS * TOKENS, TAIL)
            for head in range(HEADS):
                pair, over = head // 2, head % 2
                square = rows(pair * TOKENS, TOKENS)
                if over:
                    diagonal = jnp.where(row == col, tail[pair : pair + 1], 0.0)
                    grad = jnp.where(row < col, square, diagonal)
                else:
                    grad = jnp.where(col <= row, square, 0.0)
                grad = grad.astype(jnp.bfloat16)
                lanes = slice(head * HEAD_WIDTH, (head + 1) * HEAD_WIDTH)
                query = q_ref[core, slot, :, lanes]
                q_out[0, slot, :, lanes] = dot(grad, key, 1 - over, 0).astype(jnp.bfloat16)
                total += dot(grad, query, over, 0)
            k_out[0, slot] = total.astype(jnp.bfloat16)

        @pl.when(slot >= held)
        def _():
            q_out[0, slot] = jnp.zeros(q_out.shape[2:], jnp.bfloat16)
            k_out[0, slot] = jnp.zeros(k_out.shape[2:], jnp.bfloat16)


def final_kernel(rows_ref, kl_ref, scale_ref):
    divergence = jnp.sum(rows_ref[0], axis=0, keepdims=True)
    kl_ref[...] = divergence[:, :LAYERS] / (STUDENT_HEADS * TOKENS)
    terms = jnp.sum(rows_ref[1], axis=0, keepdims=True)
    scale_ref[...] = jnp.concatenate(
        [terms[:, SCALE_LANE + LAYERS * h : SCALE_LANE + LAYERS * (h + 1)] for h in range(HEADS)], axis=0
    )


VMEM = pl.BlockSpec(memory_space=pltpu.VMEM)
ANY = pl.BlockSpec(memory_space=pl.ANY)
SMEM = pl.BlockSpec(memory_space=pltpu.SMEM)
SMALL = pltpu.CompilerParams(vmem_limit_bytes=16 * 2**20)


def kept(array):
    return pltpu.with_memory_space_constraint(array, pltpu.VMEM)


def cost(flops, moved):
    return pl.CostEstimate(flops=flops, bytes_accessed=moved, transcendentals=0)


def local(chips, groups, teacher_q, teacher_k, student_q, student_k, student_scale, pairing, placement):
    f32, bf16 = jnp.float32, jnp.bfloat16
    over_x = [[2 * x + core for x in range(chips)] for core in range(2)]
    of_chip = [[2 * x, 2 * x + 1] for x in range(chips)]
    members = len(groups[0])

    packed, table, scales = pl.pallas_call(
        teacher_kernel,
        out_shape=(
            jax.ShapeDtypeStruct((chips, PACKED, TOKENS), f32),
            pltpu.VMEM((8, TOKENS), jnp.int32),
            pltpu.VMEM((HEADS, LAYERS), f32),
        ),
        in_specs=[SMEM, SMEM, VMEM, VMEM, VMEM],
        out_specs=(ANY, VMEM, VMEM),
        scratch_shapes=[
            pltpu.VMEM((PACKED, TOKENS), f32),
            pltpu.SemaphoreType.DMA((PAIRS,)),
        ],
        cost_estimate=cost(8 * 2 * TOKENS**3, 400_000),
        name="teacher",
    )(pairing, placement, student_scale.T, teacher_q, teacher_k)
    table, scales = kept(table), kept(scales)
    arrived = lax.all_to_all(
        packed, "section", 0, 0, tiled=True, axis_index_groups=over_x
    )
    def of_both_cores(array):
        return lax.all_gather(array, "section", axis_index_groups=of_chip)

    chip_q, chip_k = (kept(of_both_cores(a[0])) for a in (student_q, student_k))
    at_once = 2 * SLOTS
    squares = pltpu.VMEM((at_once, PACKED, TOKENS), f32)
    raw, logp = pl.pallas_call(
        scores_kernel,
        out_shape=(squares, squares),
        in_specs=[SMEM, SMEM, VMEM, VMEM],
        out_specs=(VMEM, VMEM),
        cost_estimate=cost(8 * 2 * TOKENS**3, 1_400_000),
        compiler_params=SMALL,
        name="scores",
    )(table, scales, chip_q, chip_k)

    grads, sent = pl.pallas_call(
        student_kernel,
        out_shape=(
            pltpu.VMEM((SENT, TOKENS), bf16),
            pltpu.VMEM((SENT + TAIL, TOKENS), bf16),
        ),
        in_specs=[SMEM, SMEM, VMEM, VMEM, VMEM],
        out_specs=(VMEM, VMEM),
        scratch_shapes=[pltpu.VMEM((1, TOKENS), f32)],
        cost_estimate=cost(8 * 2 * TOKENS**3, 1_800_000),
        compiler_params=SMALL,
        name="student",
    )(table, scales, *map(kept, (arrived, raw, logp)))

    chip_sent = kept(of_both_cores(sent))
    sums = pl.pallas_call(
        spread_kernel,
        out_shape=jax.ShapeDtypeStruct((members, TOKENS), f32),
        in_specs=[VMEM],
        out_specs=VMEM,
        compiler_params=SMALL,
        name="spread",
    )(chip_sent)
    rows = lax.all_to_all(
        sums.reshape(members, 1, TOKENS), AXES, 0, 0, tiled=True, axis_index_groups=groups
    )
    q_grad, k_grad = pl.pallas_call(
        gradient_kernel,
        out_shape=(
            jax.ShapeDtypeStruct(student_q.shape, bf16),
            jax.ShapeDtypeStruct(student_k.shape, bf16),
        ),
        in_specs=[SMEM, VMEM, VMEM, VMEM, VMEM],
        out_specs=(VMEM, VMEM),
        cost_estimate=cost(16 * 2 * TOKENS**3, 900_000),
        compiler_params=SMALL,
        name="gradient",
    )(table, kept(grads), chip_sent, chip_q, chip_k)

    both = of_both_cores(rows.reshape(members, TOKENS))
    layer_kl, scale_grad = pl.pallas_call(
        final_kernel,
        out_shape=(
            jax.ShapeDtypeStruct((1, LAYERS), f32),
            jax.ShapeDtypeStruct((HEADS, LAYERS), f32),
        ),
        in_specs=[VMEM],
        out_specs=(VMEM, VMEM),
        compiler_params=SMALL,
        name="final",
    )(kept(both))
    return (q_grad, k_grad, layer_kl, scale_grad.T)


def reduction_groups(sections, heads, replicas):
    def flat(section, head, replica):
        return (section * heads + head) * replicas + replica

    chips = range(sections // 2)
    first = [
        [flat(2 * x, h, d) for x in chips for h in range(heads)] for d in range(replicas)
    ]
    second = [
        [flat(2 * x + 1, h, d) for x in chips for d in range(replicas)] for h in range(heads)
    ]
    return first + second


def solution(mesh):
    sections, heads, replicas = (mesh.shape[a] for a in AXES)
    return jax.shard_map(
        functools.partial(local, sections // 2, reduction_groups(sections, heads, replicas)),
        mesh=mesh,
        in_specs=(
            P("section", "dp", "head"),
            P("section", "dp", "head"),
            P("section", None, "dp", "head"),
            P("section", None, "dp", "head"),
            P(None, "head"),
            P(),
            P(),
        ),
        out_specs=(
            P("section", None, "dp", "head"),
            P("section", None, "dp", "head"),
            P("dp", None),
            P(None, "head"),
        ),
        check_vma=False,
    )
```

```python
import functools
import math

import jax
import jax.numpy as jnp
from jax import lax
from jax.experimental import pallas as pl
from jax.experimental.pallas import tpu as pltpu
from jax.sharding import PartitionSpec as P

STUDENT_HEADS = 32
HEAD_WIDTH = 128
TOKENS = 128
LAYERS = 8
SLOTS = 2
HEADS = 4
PACKED = HEADS // 2 * TOKENS + 8
SCALE_LANE = 32
PAIRS = HEADS // 2
TAIL = 16
SLOT_ROWS = PAIRS * TOKENS + TAIL
SENT = SLOTS * SLOT_ROWS
INVERSE = 1.0 / math.sqrt(HEAD_WIDTH)
HIDDEN = -1e30
SMALLEST = 1.2e-38
AXES = ("section", "head", "dp")


def dot(a, b, over_a, over_b):
    return lax.dot_general(
        a, b, (((over_a,), (over_b,)), ((), ())), preferred_element_type=jnp.float32
    )


def masks():
    row = lax.broadcasted_iota(jnp.int32, (TOKENS, TOKENS), 0)
    col = lax.broadcasted_iota(jnp.int32, (TOKENS, TOKENS), 1)
    return row, col


def log_softmax(scores, visible, axis):
    scores = jnp.where(visible, scores, HIDDEN)
    shifted = scores - jnp.max(scores, axis=axis, keepdims=True)
    return shifted - jnp.log(jnp.sum(jnp.exp(shifted), axis=axis, keepdims=True))


def softmax(scores, visible, axis):
    scores = jnp.where(visible, scores, HIDDEN)
    powers = jnp.exp(scores - jnp.max(scores, axis=axis, keepdims=True))
    return powers * (1.0 / jnp.sum(powers, axis=axis, keepdims=True))


def teacher_kernel(
    pairing, placement, scale_ref, q_ref, k_ref, out_ref, table_ref, scale_out, packed, sems
):
    me = lax.axis_index("section")
    home = jnp.int32(0)
    for layer in range(LAYERS):
        home = jnp.where(pairing[layer] == me, placement[layer], home)
    chip = home // 2
    row, col = masks()
    key = k_ref[0]

    scale_out[...] = scale_ref[...]
    at_row = lax.broadcasted_iota(jnp.int32, (2, LAYERS), 0)
    at_lane = lax.broadcasted_iota(jnp.int32, (2, LAYERS), 1)
    table = jnp.zeros((2, LAYERS), jnp.int32)
    for layer in range(LAYERS):
        entry = jnp.where(at_row == 0, pairing[layer], placement[layer])
        table = jnp.where(at_lane == layer, entry, table)
    table_ref[...] = table

    def target(head, turned):
        total = jnp.zeros((TOKENS, TOKENS), jnp.float32)
        for twin in (2 * head, 2 * head + 1):
            query = q_ref[0, :, twin * HEAD_WIDTH : (twin + 1) * HEAD_WIDTH]
            if turned:
                total += softmax(dot(key, query, 1, 1) * INVERSE, row <= col, 0)
            else:
                total += softmax(dot(query, key, 1, 1) * INVERSE, col <= row, 1)
        return total * 0.5

    packed[PAIRS * TOKENS :, :] = jnp.zeros((PACKED - PAIRS * TOKENS, TOKENS), jnp.float32)
    started = []
    for pair in range(PAIRS):
        plain = target(2 * pair, False)
        turned = target(2 * pair + 1, True)
        packed[pair * TOKENS : (pair + 1) * TOKENS, :] = jnp.where(col <= row, plain, turned)
        at = PAIRS * TOKENS + pair
        packed[at : at + 1, :] = jnp.sum(
            jnp.where(row == col, turned, 0.0), axis=0, keepdims=True
        )
        end = (pair + 1) * TOKENS if pair < PAIRS - 1 else PACKED
        rows = slice(pair * TOKENS, end)
        copy = pltpu.make_async_copy(
            packed.at[rows, :], out_ref.at[chip, rows, :], sems.at[pair]
        )
        copy.start()
        started.append(copy)
    for copy in started:
        copy.wait()


def for_my_layers(table, work):
    me = lax.axis_index("section")
    chip, core = me // 2, lax.rem(me, 2)

    def step(layer, carry):
        slots, rank = carry[:2], carry[2]
        source, home = table[0, layer], table[1, layer]
        home_core = lax.rem(home, 2)
        here = home // 2 == chip
        mine = here & (lax.rem(source, 2) == core)
        slot = jnp.where(home_core == 0, slots[0], slots[1])

        @pl.when(mine)
        def _():
            work(layer, source // 2, home_core, slot, rank)

        return (
            slots[0] + (here & (home_core == 0)).astype(jnp.int32),
            slots[1] + (here & (home_core == 1)).astype(jnp.int32),
            rank + mine.astype(jnp.int32),
        )

    lax.fori_loop(0, LAYERS, step, (jnp.int32(0),) * 3)


def pack(ref, rank, pair, plain, turned):
    row, col = masks()
    ref[rank, pair * TOKENS : (pair + 1) * TOKENS, :] = jnp.where(col <= row, plain, turned)
    at = PAIRS * TOKENS + pair
    ref[rank, at : at + 1, :] = jnp.sum(
        jnp.where(row == col, turned, 0.0), axis=0, keepdims=True
    )


def scores_kernel(table, scale_ref, qk_ref, raw_ref, logp_ref):
    row, col = masks()

    def work(layer, source_chip, home_core, slot, rank):
        key = qk_ref[home_core, slot, :, HEADS * HEAD_WIDTH :]

        def query(head):
            return qk_ref[home_core, slot, :, head * HEAD_WIDTH : (head + 1) * HEAD_WIDTH]

        empty = jnp.zeros((PACKED - PAIRS * TOKENS, TOKENS), jnp.float32)
        raw_ref[rank, PAIRS * TOKENS :, :] = empty
        logp_ref[rank, PAIRS * TOKENS :, :] = empty
        for pair in range(PAIRS):
            plain = dot(query(2 * pair), key, 1, 1) * INVERSE
            turned = dot(key, query(2 * pair + 1), 1, 1) * INVERSE
            pack(raw_ref, rank, pair, plain, turned)
            plain = log_softmax(scale_ref[2 * pair, layer] * plain, col <= row, 1)
            turned = log_softmax(scale_ref[2 * pair + 1, layer] * turned, row <= col, 0)
            pack(logp_ref, rank, pair, plain, turned)

    for_my_layers(table, work)


def student_kernel(table, scale_ref, arrived_ref, raw_ref, logp_ref, grad_ref, sent_ref, sums_ref):
    core = lax.rem(lax.axis_index("section"), 2)
    row, col = masks()
    lower = col <= row
    place = lax.broadcasted_iota(jnp.int32, (8, TOKENS), 0)
    lane = lax.broadcasted_iota(jnp.int32, (8, TOKENS), 1)
    tail_row = lax.broadcasted_iota(jnp.int32, (TAIL, TOKENS), 0)
    sums_ref[...] = jnp.zeros_like(sums_ref)

    def work(layer, source_chip, home_core, slot, rank):
        def terms(rows):
            target = arrived_ref[source_chip, rows, :]
            target_logp = jnp.log(jnp.maximum(target, SMALLEST))
            student_logp = logp_ref[rank, rows, :]
            difference = jnp.exp(student_logp) - target
            return (
                jnp.sum(target * (target_logp - student_logp), axis=0, keepdims=True),
                difference,
                difference * raw_ref[rank, rows, :],
            )

        last, last_difference, last_moved = terms(slice(PAIRS * TOKENS, PACKED))
        found = jnp.zeros((8, TOKENS), jnp.float32)
        divergence = last
        tail = jnp.zeros((TAIL, TOKENS), jnp.float32)
        pieces = []
        for pair in range(PAIRS):
            one, difference, moved = terms(slice(pair * TOKENS, (pair + 1) * TOKENS))
            divergence += one
            first = scale_ref[2 * pair, layer] * INVERSE
            second = scale_ref[2 * pair + 1, layer] * INVERSE
            pieces.append(difference * jnp.where(lower, first, second))
            tail = jnp.where(tail_row == pair, last_difference[pair : pair + 1] * second, tail)
            of_first = jnp.sum(jnp.where(lower, moved, 0.0), axis=0, keepdims=True)
            of_second = jnp.sum(jnp.where(lower, 0.0, moved), axis=0, keepdims=True)
            of_second += last_moved[pair : pair + 1]
            found = jnp.where(place == 1 + 2 * pair, of_first, found)
            found = jnp.where(place == 2 + 2 * pair, of_second, found)
        found = jnp.where(place == 0, divergence, found)
        found = jnp.sum(found, axis=1, keepdims=True)
        goes_to = jnp.where(place == 0, layer, SCALE_LANE + LAYERS * (place - 1) + layer)
        found = jnp.where((lane == goes_to) & (place <= HEADS), found, 0.0)
        sums_ref[...] += jnp.sum(found, axis=0, keepdims=True)
        pieces.append(tail)

        def put(ref, at):
            for n, piece in enumerate(pieces):
                to = pl.multiple_of(at + n * TOKENS, TAIL)
                ref[pl.ds(to, piece.shape[0]), :] = piece.astype(jnp.bfloat16)

        @pl.when(home_core == core)
        def _():
            put(grad_ref, slot * SLOT_ROWS)

        @pl.when(home_core != core)
        def _():
            put(sent_ref, slot * SLOT_ROWS)

    for_my_layers(table, work)
    left, tile = sums_ref[...], jnp.zeros((TAIL, TOKENS), jnp.float32)
    for term in range(3):
        part = left.astype(jnp.bfloat16).astype(jnp.float32)
        tile = jnp.where(tail_row == term, part, tile)
        left -= part
    sent_ref[SENT:, :] = tile.astype(jnp.bfloat16)


def spread_kernel(pair_ref, out_ref):
    terms = pair_ref[:, SENT:, :].astype(jnp.float32)
    total = jnp.zeros((1, TOKENS), jnp.float32)
    for core in range(2):
        total += (terms[core, 0:1] + terms[core, 1:2]) + terms[core, 2:3]
    out_ref[...] = jnp.broadcast_to(total, out_ref.shape)


def gradient_kernel(table, grad_ref, sent_ref, qk_ref, q_out, k_out):
    me = lax.axis_index("section")
    core = lax.rem(me, 2)
    row, col = masks()
    held, layers = jnp.int32(0), [jnp.int32(0)] * SLOTS
    for layer in range(LAYERS):
        here = table[1, layer] == me
        layers = [
            jnp.where(here & (held == slot), layer, had) for slot, had in enumerate(layers)
        ]
        held += here.astype(jnp.int32)
    for slot in range(SLOTS):

        @pl.when(slot < held)
        def _():
            direct = lax.rem(table[0, layers[slot]], 2) == core
            key = qk_ref[core, slot, :, HEADS * HEAD_WIDTH :]
            total = jnp.zeros((TOKENS, HEAD_WIDTH), jnp.float32)

            def rows(at, count):
                at = slot * SLOT_ROWS + at
                near = grad_ref[at : at + count, :].astype(jnp.float32)
                other = sent_ref[1 - core, at : at + count, :].astype(jnp.float32)
                return jnp.where(direct, near, other)

            tail = rows(PAIRS * TOKENS, TAIL)
            for head in range(HEADS):
                pair, over = head // 2, head % 2
                square = rows(pair * TOKENS, TOKENS)
                if over:
                    diagonal = jnp.where(row == col, tail[pair : pair + 1], 0.0)
                    grad = jnp.where(row < col, square, diagonal)
                else:
                    grad = jnp.where(col <= row, square, 0.0)
                grad = grad.astype(jnp.bfloat16)
                lanes = slice(head * HEAD_WIDTH, (head + 1) * HEAD_WIDTH)
                query = qk_ref[core, slot, :, lanes]
                q_out[0, slot, :, lanes] = dot(grad, key, 1 - over, 0).astype(jnp.bfloat16)
                total += dot(grad, query, over, 0)
            k_out[0, slot] = total.astype(jnp.bfloat16)

        @pl.when(slot >= held)
        def _():
            q_out[0, slot] = jnp.zeros(q_out.shape[2:], jnp.bfloat16)
            k_out[0, slot] = jnp.zeros(k_out.shape[2:], jnp.bfloat16)


def final_kernel(rows_ref, kl_ref, scale_ref):
    divergence = jnp.sum(rows_ref[0], axis=0, keepdims=True)
    kl_ref[...] = divergence[:, :LAYERS] / (STUDENT_HEADS * TOKENS)
    terms = jnp.sum(rows_ref[1], axis=0, keepdims=True)
    scale_ref[...] = jnp.concatenate(
        [terms[:, SCALE_LANE + LAYERS * h : SCALE_LANE + LAYERS * (h + 1)] for h in range(HEADS)], axis=0
    )


VMEM = pl.BlockSpec(memory_space=pltpu.VMEM)
ANY = pl.BlockSpec(memory_space=pl.ANY)
SMEM = pl.BlockSpec(memory_space=pltpu.SMEM)
SMALL = pltpu.CompilerParams(vmem_limit_bytes=16 * 2**20)


def kept(array):
    return pltpu.with_memory_space_constraint(array, pltpu.VMEM)


def cost(flops, moved):
    return pl.CostEstimate(flops=flops, bytes_accessed=moved, transcendentals=0)


def local(chips, groups, teacher_q, teacher_k, student_q, student_k, student_scale, pairing, placement):
    f32, bf16 = jnp.float32, jnp.bfloat16
    over_x = [[2 * x + core for x in range(chips)] for core in range(2)]
    of_chip = [[2 * x, 2 * x + 1] for x in range(chips)]
    members = len(groups[0])

    packed, table, scales = pl.pallas_call(
        teacher_kernel,
        out_shape=(
            jax.ShapeDtypeStruct((chips, PACKED, TOKENS), f32),
            pltpu.VMEM((2, LAYERS), jnp.int32),
            pltpu.VMEM((HEADS, LAYERS), f32),
        ),
        in_specs=[SMEM, SMEM, VMEM, VMEM, VMEM],
        out_specs=(ANY, VMEM, VMEM),
        scratch_shapes=[
            pltpu.VMEM((PACKED, TOKENS), f32),
            pltpu.SemaphoreType.DMA((PAIRS,)),
        ],
        cost_estimate=cost(8 * 2 * TOKENS**3, 400_000),
        name="teacher",
    )(pairing, placement, student_scale.T, teacher_q, teacher_k)
    table, scales = kept(table), kept(scales)
    arrived = lax.all_to_all(
        packed, "section", 0, 0, tiled=True, axis_index_groups=over_x
    )
    def of_both_cores(array):
        return lax.all_gather(array, "section", axis_index_groups=of_chip)

    chip_qk = kept(of_both_cores(jnp.concatenate((student_q[0], student_k[0]), axis=2)))
    at_once = 2 * SLOTS
    squares = pltpu.VMEM((at_once, PACKED, TOKENS), f32)
    raw, logp = pl.pallas_call(
        scores_kernel,
        out_shape=(squares, squares),
        in_specs=[SMEM, SMEM, VMEM],
        out_specs=(VMEM, VMEM),
        cost_estimate=cost(8 * 2 * TOKENS**3, 1_400_000),
        compiler_params=SMALL,
        name="scores",
    )(table, scales, chip_qk)

    grads, sent = pl.pallas_call(
        student_kernel,
        out_shape=(
            pltpu.VMEM((SENT, TOKENS), bf16),
            pltpu.VMEM((SENT + TAIL, TOKENS), bf16),
        ),
        in_specs=[SMEM, SMEM, VMEM, VMEM, VMEM],
        out_specs=(VMEM, VMEM),
        scratch_shapes=[pltpu.VMEM((1, TOKENS), f32)],
        cost_estimate=cost(8 * 2 * TOKENS**3, 1_800_000),
        compiler_params=SMALL,
        name="student",
    )(table, scales, *map(kept, (arrived, raw, logp)))

    chip_sent = kept(of_both_cores(sent))
    sums = pl.pallas_call(
        spread_kernel,
        out_shape=jax.ShapeDtypeStruct((members, TOKENS), f32),
        in_specs=[VMEM],
        out_specs=VMEM,
        compiler_params=SMALL,
        name="spread",
    )(chip_sent)
    rows = lax.all_to_all(
        sums.reshape(members, 1, TOKENS), AXES, 0, 0, tiled=True, axis_index_groups=groups
    )
    q_grad, k_grad = pl.pallas_call(
        gradient_kernel,
        out_shape=(
            jax.ShapeDtypeStruct(student_q.shape, bf16),
            jax.ShapeDtypeStruct(student_k.shape, bf16),
        ),
        in_specs=[SMEM, VMEM, VMEM, VMEM],
        out_specs=(VMEM, VMEM),
        cost_estimate=cost(16 * 2 * TOKENS**3, 900_000),
        compiler_params=SMALL,
        name="gradient",
    )(table, kept(grads), chip_sent, chip_qk)

    both = of_both_cores(rows.reshape(members, TOKENS))
    layer_kl, scale_grad = pl.pallas_call(
        final_kernel,
        out_shape=(
            jax.ShapeDtypeStruct((1, LAYERS), f32),
            jax.ShapeDtypeStruct((HEADS, LAYERS), f32),
        ),
        in_specs=[VMEM],
        out_specs=(VMEM, VMEM),
        compiler_params=SMALL,
        name="final",
    )(kept(both))
    return (q_grad, k_grad, layer_kl, scale_grad.T)


def reduction_groups(sections, heads, replicas):
    def flat(section, head, replica):
        return (section * heads + head) * replicas + replica

    chips = range(sections // 2)
    first = [
        [flat(2 * x, h, d) for x in chips for h in range(heads)] for d in range(replicas)
    ]
    second = [
        [flat(2 * x + 1, h, d) for x in chips for d in range(replicas)] for h in range(heads)
    ]
    return first + second


def solution(mesh):
    sections, heads, replicas = (mesh.shape[a] for a in AXES)
    return jax.shard_map(
        functools.partial(local, sections // 2, reduction_groups(sections, heads, replicas)),
        mesh=mesh,
        in_specs=(
            P("section", "dp", "head"),
            P("section", "dp", "head"),
            P("section", None, "dp", "head"),
            P("section", None, "dp", "head"),
            P(None, "head"),
            P(),
            P(),
        ),
        out_specs=(
            P("section", None, "dp", "head"),
            P("section", None, "dp", "head"),
            P("dp", None),
            P(None, "head"),
        ),
        check_vma=False,
    )
```

```python
import functools
import math

import jax
import jax.numpy as jnp
from jax import lax
from jax.experimental import pallas as pl
from jax.experimental.pallas import tpu as pltpu
from jax.sharding import PartitionSpec as P

STUDENT_HEADS = 32
HEAD_WIDTH = 128
TOKENS = 128
LAYERS = 8
SLOTS = 2
HEADS = 4
PACKED = HEADS // 2 * TOKENS + 8
SCALE_LANE = 32
PAIRS = HEADS // 2
TAIL = 16
SLOT_ROWS = PAIRS * TOKENS + TAIL
SENT = SLOTS * SLOT_ROWS
INVERSE = 1.0 / math.sqrt(HEAD_WIDTH)
HIDDEN = -1e30
SMALLEST = 1.2e-38
AXES = ("section", "head", "dp")


def dot(a, b, over_a, over_b):
    return lax.dot_general(
        a, b, (((over_a,), (over_b,)), ((), ())), preferred_element_type=jnp.float32
    )


def masks():
    row = lax.broadcasted_iota(jnp.int32, (TOKENS, TOKENS), 0)
    col = lax.broadcasted_iota(jnp.int32, (TOKENS, TOKENS), 1)
    return row, col


def log_softmax(scores, visible, axis):
    scores = jnp.where(visible, scores, HIDDEN)
    shifted = scores - jnp.max(scores, axis=axis, keepdims=True)
    return shifted - jnp.log(jnp.sum(jnp.exp(shifted), axis=axis, keepdims=True))


def softmax(scores, visible, axis):
    scores = jnp.where(visible, scores, HIDDEN)
    powers = jnp.exp(scores - jnp.max(scores, axis=axis, keepdims=True))
    return powers * (1.0 / jnp.sum(powers, axis=axis, keepdims=True))


def teacher_kernel(pairing, placement, q_ref, k_ref, out_ref, packed, sems):
    me = lax.axis_index("section")
    home = jnp.int32(0)
    for layer in range(LAYERS):
        home = jnp.where(pairing[layer] == me, placement[layer], home)
    chip = home // 2
    row, col = masks()
    key = k_ref[0]

    def target(head, turned):
        total = jnp.zeros((TOKENS, TOKENS), jnp.float32)
        for twin in (2 * head, 2 * head + 1):
            query = q_ref[0, :, twin * HEAD_WIDTH : (twin + 1) * HEAD_WIDTH]
            if turned:
                total += softmax(dot(key, query, 1, 1) * INVERSE, row <= col, 0)
            else:
                total += softmax(dot(query, key, 1, 1) * INVERSE, col <= row, 1)
        return total * 0.5

    packed[PAIRS * TOKENS :, :] = jnp.zeros((PACKED - PAIRS * TOKENS, TOKENS), jnp.float32)
    started = []
    for pair in range(PAIRS):
        plain = target(2 * pair, False)
        turned = target(2 * pair + 1, True)
        packed[pair * TOKENS : (pair + 1) * TOKENS, :] = jnp.where(col <= row, plain, turned)
        at = PAIRS * TOKENS + pair
        packed[at : at + 1, :] = jnp.sum(
            jnp.where(row == col, turned, 0.0), axis=0, keepdims=True
        )
        end = (pair + 1) * TOKENS if pair < PAIRS - 1 else PACKED
        rows = slice(pair * TOKENS, end)
        copy = pltpu.make_async_copy(
            packed.at[rows, :], out_ref.at[chip, rows, :], sems.at[pair]
        )
        copy.start()
        started.append(copy)
    for copy in started:
        copy.wait()


def for_my_layers(pairing, placement, work):
    me = lax.axis_index("section")
    chip, core = me // 2, lax.rem(me, 2)

    def step(layer, carry):
        slots, rank = carry[:2], carry[2]
        home, source = placement[layer], pairing[layer]
        home_core = lax.rem(home, 2)
        here = home // 2 == chip
        mine = here & (lax.rem(source, 2) == core)
        slot = jnp.where(home_core == 0, slots[0], slots[1])

        @pl.when(mine)
        def _():
            work(layer, source // 2, home_core, slot, rank)

        return (
            slots[0] + (here & (home_core == 0)).astype(jnp.int32),
            slots[1] + (here & (home_core == 1)).astype(jnp.int32),
            rank + mine.astype(jnp.int32),
        )

    lax.fori_loop(0, LAYERS, step, (jnp.int32(0),) * 3)


def pack(ref, rank, pair, plain, turned):
    row, col = masks()
    ref[rank, pair * TOKENS : (pair + 1) * TOKENS, :] = jnp.where(col <= row, plain, turned)
    at = PAIRS * TOKENS + pair
    ref[rank, at : at + 1, :] = jnp.sum(
        jnp.where(row == col, turned, 0.0), axis=0, keepdims=True
    )


def scores_kernel(pairing, placement, scale_ref, qk_ref, raw_ref, logp_ref, table_ref):
    row, col = masks()
    at_row = lax.broadcasted_iota(jnp.int32, (2, LAYERS), 0)
    at_lane = lax.broadcasted_iota(jnp.int32, (2, LAYERS), 1)
    table = jnp.full((2, LAYERS), -1, jnp.int32)
    for layer in range(LAYERS):
        belongs = placement[layer] + LAYERS * pairing[layer]
        table = jnp.where((at_row == 1) & (at_lane == layer), belongs, table)
    table_ref[...] = table

    def work(layer, source_chip, home_core, slot, rank):
        code = layer + 8 * source_chip + 32 * home_core + 64 * slot
        table_ref[...] = jnp.where((at_row == 0) & (at_lane == rank), code, table_ref[...])
        key = qk_ref[home_core, slot, :, HEADS * HEAD_WIDTH :]

        def query(head):
            return qk_ref[home_core, slot, :, head * HEAD_WIDTH : (head + 1) * HEAD_WIDTH]

        tail_row = lax.broadcasted_iota(jnp.int32, (PACKED - PAIRS * TOKENS, TOKENS), 0)
        empty = jnp.zeros(tail_row.shape, jnp.float32)
        scales = empty
        for head in range(HEADS):
            scales = jnp.where(tail_row == HEADS + head, scale_ref[head, layer] * INVERSE, scales)
        raw_ref[rank, PAIRS * TOKENS :, :] = scales
        logp_ref[rank, PAIRS * TOKENS :, :] = empty
        for pair in range(PAIRS):
            plain = dot(query(2 * pair), key, 1, 1) * INVERSE
            turned = dot(key, query(2 * pair + 1), 1, 1) * INVERSE
            pack(raw_ref, rank, pair, plain, turned)
            plain = log_softmax(scale_ref[2 * pair, layer] * plain, col <= row, 1)
            turned = log_softmax(scale_ref[2 * pair + 1, layer] * turned, row <= col, 0)
            pack(logp_ref, rank, pair, plain, turned)

    for_my_layers(pairing, placement, work)


def student_kernel(table, arrived_ref, raw_ref, logp_ref, grad_ref, sent_ref, sums_ref):
    core = lax.rem(lax.axis_index("section"), 2)
    row, col = masks()
    lower = col <= row
    place = lax.broadcasted_iota(jnp.int32, (8, TOKENS), 0)
    lane = lax.broadcasted_iota(jnp.int32, (8, TOKENS), 1)
    tail_row = lax.broadcasted_iota(jnp.int32, (TAIL, TOKENS), 0)
    sums_ref[...] = jnp.zeros_like(sums_ref)

    held = jnp.int32(0)
    for rank in range(2 * SLOTS):
        held += (table[0, rank] >= 0).astype(jnp.int32)

    def work(rank, carry):
        code = table[0, rank]
        layer, source_chip = code & 7, (code >> 3) & 3
        home_core, slot = (code >> 5) & 1, code >> 6

        def terms(rows):
            target = arrived_ref[source_chip, rows, :]
            target_logp = jnp.log(jnp.maximum(target, SMALLEST))
            student_logp = logp_ref[rank, rows, :]
            difference = jnp.exp(student_logp) - target
            return (
                jnp.sum(target * (target_logp - student_logp), axis=0, keepdims=True),
                difference,
                difference * raw_ref[rank, rows, :],
            )

        def scale_of(head):
            at = PAIRS * TOKENS + HEADS + head
            return raw_ref[rank, at : at + 1, :]

        last, last_difference, last_moved = terms(slice(PAIRS * TOKENS, PACKED))
        found = jnp.zeros((8, TOKENS), jnp.float32)
        divergence = last
        tail = jnp.zeros((TAIL, TOKENS), jnp.float32)
        pieces = []
        for pair in range(PAIRS):
            one, difference, moved = terms(slice(pair * TOKENS, (pair + 1) * TOKENS))
            divergence += one
            first = scale_of(2 * pair)
            second = scale_of(2 * pair + 1)
            pieces.append(difference * jnp.where(lower, first, second))
            tail = jnp.where(tail_row == pair, last_difference[pair : pair + 1] * second, tail)
            of_first = jnp.sum(jnp.where(lower, moved, 0.0), axis=0, keepdims=True)
            of_second = jnp.sum(jnp.where(lower, 0.0, moved), axis=0, keepdims=True)
            of_second += last_moved[pair : pair + 1]
            found = jnp.where(place == 1 + 2 * pair, of_first, found)
            found = jnp.where(place == 2 + 2 * pair, of_second, found)
        found = jnp.where(place == 0, divergence, found)
        found = jnp.sum(found, axis=1, keepdims=True)
        goes_to = jnp.where(place == 0, layer, SCALE_LANE + LAYERS * (place - 1) + layer)
        found = jnp.where((lane == goes_to) & (place <= HEADS), found, 0.0)
        sums_ref[...] += jnp.sum(found, axis=0, keepdims=True)
        pieces.append(tail)

        def put(ref, at):
            for n, piece in enumerate(pieces):
                to = pl.multiple_of(at + n * TOKENS, TAIL)
                ref[pl.ds(to, piece.shape[0]), :] = piece.astype(jnp.bfloat16)

        @pl.when(home_core == core)
        def _():
            put(grad_ref, slot * SLOT_ROWS)

        @pl.when(home_core != core)
        def _():
            put(sent_ref, slot * SLOT_ROWS)

        return carry

    lax.fori_loop(0, held, work, 0)
    left, tile = sums_ref[...], jnp.zeros((TAIL, TOKENS), jnp.float32)
    for term in range(3):
        part = left.astype(jnp.bfloat16).astype(jnp.float32)
        tile = jnp.where(tail_row == term, part, tile)
        left -= part
    sent_ref[SENT:, :] = tile.astype(jnp.bfloat16)


def spread_kernel(pair_ref, out_ref):
    terms = pair_ref[:, SENT:, :].astype(jnp.float32)
    total = jnp.zeros((1, TOKENS), jnp.float32)
    for core in range(2):
        total += (terms[core, 0:1] + terms[core, 1:2]) + terms[core, 2:3]
    out_ref[...] = jnp.broadcast_to(total, out_ref.shape)


def gradient_kernel(table, grad_ref, sent_ref, qk_ref, q_out, k_out):
    me = lax.axis_index("section")
    core = lax.rem(me, 2)
    row, col = masks()
    held, layers = jnp.int32(0), [jnp.int32(0)] * SLOTS
    for layer in range(LAYERS):
        here = (table[1, layer] & (LAYERS - 1)) == me
        layers = [
            jnp.where(here & (held == slot), layer, had) for slot, had in enumerate(layers)
        ]
        held += here.astype(jnp.int32)
    for slot in range(SLOTS):

        @pl.when(slot < held)
        def _():
            direct = ((table[1, layers[slot]] >> 3) & 1) == core
            key = qk_ref[core, slot, :, HEADS * HEAD_WIDTH :]
            total = jnp.zeros((TOKENS, HEAD_WIDTH), jnp.float32)

            def rows(at, count):
                at = slot * SLOT_ROWS + at
                near = grad_ref[at : at + count, :].astype(jnp.float32)
                other = sent_ref[1 - core, at : at + count, :].astype(jnp.float32)
                return jnp.where(direct, near, other)

            tail = rows(PAIRS * TOKENS, TAIL)
            for head in range(HEADS):
                pair, over = head // 2, head % 2
                square = rows(pair * TOKENS, TOKENS)
                if over:
                    diagonal = jnp.where(row == col, tail[pair : pair + 1], 0.0)
                    grad = jnp.where(row < col, square, diagonal)
                else:
                    grad = jnp.where(col <= row, square, 0.0)
                grad = grad.astype(jnp.bfloat16)
                lanes = slice(head * HEAD_WIDTH, (head + 1) * HEAD_WIDTH)
                query = qk_ref[core, slot, :, lanes]
                q_out[0, slot, :, lanes] = dot(grad, key, 1 - over, 0).astype(jnp.bfloat16)
                total += dot(grad, query, over, 0)
            k_out[0, slot] = total.astype(jnp.bfloat16)

        @pl.when(slot >= held)
        def _():
            q_out[0, slot] = jnp.zeros(q_out.shape[2:], jnp.bfloat16)
            k_out[0, slot] = jnp.zeros(k_out.shape[2:], jnp.bfloat16)


def final_kernel(rows_ref, kl_ref, scale_ref):
    divergence = jnp.sum(rows_ref[0], axis=0, keepdims=True)
    kl_ref[...] = divergence[:, :LAYERS] / (STUDENT_HEADS * TOKENS)
    terms = jnp.sum(rows_ref[1], axis=0, keepdims=True)
    scale_ref[...] = jnp.concatenate(
        [terms[:, SCALE_LANE + LAYERS * h : SCALE_LANE + LAYERS * (h + 1)] for h in range(HEADS)], axis=0
    )


VMEM = pl.BlockSpec(memory_space=pltpu.VMEM)
ANY = pl.BlockSpec(memory_space=pl.ANY)
SMEM = pl.BlockSpec(memory_space=pltpu.SMEM)
SMALL = pltpu.CompilerParams(vmem_limit_bytes=16 * 2**20)


def kept(array):
    return pltpu.with_memory_space_constraint(array, pltpu.VMEM)


def cost(flops, moved):
    return pl.CostEstimate(flops=flops, bytes_accessed=moved, transcendentals=0)


def local(chips, groups, teacher_q, teacher_k, student_q, student_k, student_scale, pairing, placement):
    f32, bf16 = jnp.float32, jnp.bfloat16
    over_x = [[2 * x + core for x in range(chips)] for core in range(2)]
    of_chip = [[2 * x, 2 * x + 1] for x in range(chips)]
    members = len(groups[0])

    packed = pl.pallas_call(
        teacher_kernel,
        out_shape=jax.ShapeDtypeStruct((chips, PACKED, TOKENS), f32),
        in_specs=[SMEM, SMEM, VMEM, VMEM],
        out_specs=ANY,
        scratch_shapes=[
            pltpu.VMEM((PACKED, TOKENS), f32),
            pltpu.SemaphoreType.DMA((PAIRS,)),
        ],
        cost_estimate=cost(8 * 2 * TOKENS**3, 400_000),
        name="teacher",
    )(pairing, placement, teacher_q, teacher_k)
    arrived = lax.all_to_all(
        packed, "section", 0, 0, tiled=True, axis_index_groups=over_x
    )
    def of_both_cores(array):
        return lax.all_gather(array, "section", axis_index_groups=of_chip)

    chip_qk = kept(of_both_cores(jnp.concatenate((student_q[0], student_k[0]), axis=2)))
    at_once = 2 * SLOTS
    squares = pltpu.VMEM((at_once, PACKED, TOKENS), f32)
    raw, logp, table = pl.pallas_call(
        scores_kernel,
        out_shape=(squares, squares, pltpu.VMEM((2, LAYERS), jnp.int32)),
        in_specs=[SMEM, SMEM, SMEM, VMEM],
        out_specs=(VMEM, VMEM, VMEM),
        cost_estimate=cost(8 * 2 * TOKENS**3, 1_400_000),
        compiler_params=SMALL,
        name="scores",
    )(pairing, placement, student_scale.T, chip_qk)
    table = kept(table)

    grads, sent = pl.pallas_call(
        student_kernel,
        out_shape=(
            pltpu.VMEM((SENT, TOKENS), bf16),
            pltpu.VMEM((SENT + TAIL, TOKENS), bf16),
        ),
        in_specs=[SMEM, VMEM, VMEM, VMEM],
        out_specs=(VMEM, VMEM),
        scratch_shapes=[pltpu.VMEM((1, TOKENS), f32)],
        cost_estimate=cost(8 * 2 * TOKENS**3, 1_800_000),
        compiler_params=SMALL,
        name="student",
    )(table, *map(kept, (arrived, raw, logp)))

    chip_sent = kept(of_both_cores(sent))
    sums = pl.pallas_call(
        spread_kernel,
        out_shape=jax.ShapeDtypeStruct((members, TOKENS), f32),
        in_specs=[VMEM],
        out_specs=VMEM,
        compiler_params=SMALL,
        name="spread",
    )(chip_sent)
    rows = lax.all_to_all(
        sums.reshape(members, 1, TOKENS), AXES, 0, 0, tiled=True, axis_index_groups=groups
    )
    q_grad, k_grad = pl.pallas_call(
        gradient_kernel,
        out_shape=(
            jax.ShapeDtypeStruct(student_q.shape, bf16),
            jax.ShapeDtypeStruct(student_k.shape, bf16),
        ),
        in_specs=[SMEM, VMEM, VMEM, VMEM],
        out_specs=(VMEM, VMEM),
        cost_estimate=cost(16 * 2 * TOKENS**3, 900_000),
        compiler_params=SMALL,
        name="gradient",
    )(table, kept(grads), chip_sent, chip_qk)

    both = of_both_cores(rows.reshape(members, TOKENS))
    layer_kl, scale_grad = pl.pallas_call(
        final_kernel,
        out_shape=(
            jax.ShapeDtypeStruct((1, LAYERS), f32),
            jax.ShapeDtypeStruct((HEADS, LAYERS), f32),
        ),
        in_specs=[VMEM],
        out_specs=(VMEM, VMEM),
        compiler_params=SMALL,
        name="final",
    )(kept(both))
    return (q_grad, k_grad, layer_kl, scale_grad.T)


def reduction_groups(sections, heads, replicas):
    def flat(section, head, replica):
        return (section * heads + head) * replicas + replica

    chips = range(sections // 2)
    first = [
        [flat(2 * x, h, d) for x in chips for h in range(heads)] for d in range(replicas)
    ]
    second = [
        [flat(2 * x + 1, h, d) for x in chips for d in range(replicas)] for h in range(heads)
    ]
    return first + second


def solution(mesh):
    sections, heads, replicas = (mesh.shape[a] for a in AXES)
    return jax.shard_map(
        functools.partial(local, sections // 2, reduction_groups(sections, heads, replicas)),
        mesh=mesh,
        in_specs=(
            P("section", "dp", "head"),
            P("section", "dp", "head"),
            P("section", None, "dp", "head"),
            P("section", None, "dp", "head"),
            P(None, "head"),
            P(),
            P(),
        ),
        out_specs=(
            P("section", None, "dp", "head"),
            P("section", None, "dp", "head"),
            P("dp", None),
            P(None, "head"),
        ),
        check_vma=False,
    )
```

```python
import functools
import math

import jax
import jax.numpy as jnp
from jax import lax
from jax.experimental import pallas as pl
from jax.experimental.pallas import tpu as pltpu
from jax.sharding import PartitionSpec as P

STUDENT_HEADS = 32
HEAD_WIDTH = 128
TOKENS = 128
LAYERS = 8
SLOTS = 2
HEADS = 4
PACKED = HEADS // 2 * TOKENS + 8
SCALE_LANE = 32
PAIRS = HEADS // 2
TAIL = 16
SLOT_ROWS = PAIRS * TOKENS + TAIL
SENT = SLOTS * SLOT_ROWS
SUM_ROWS = 8
INVERSE = 1.0 / math.sqrt(HEAD_WIDTH)
HIDDEN = -1e30
SMALLEST = 1.2e-38
AXES = ("section", "head", "dp")


def dot(a, b, over_a, over_b):
    return lax.dot_general(
        a, b, (((over_a,), (over_b,)), ((), ())), preferred_element_type=jnp.float32
    )


def masks():
    row = lax.broadcasted_iota(jnp.int32, (TOKENS, TOKENS), 0)
    col = lax.broadcasted_iota(jnp.int32, (TOKENS, TOKENS), 1)
    return row, col


def log_softmax(scores, visible, axis):
    scores = jnp.where(visible, scores, HIDDEN)
    shifted = scores - jnp.max(scores, axis=axis, keepdims=True)
    return shifted - jnp.log(jnp.sum(jnp.exp(shifted), axis=axis, keepdims=True))


def softmax(scores, visible, axis):
    scores = jnp.where(visible, scores, HIDDEN)
    powers = jnp.exp(scores - jnp.max(scores, axis=axis, keepdims=True))
    return powers * (1.0 / jnp.sum(powers, axis=axis, keepdims=True))


def teacher_kernel(pairing, placement, q_ref, k_ref, out_ref, packed, sems):
    me = lax.axis_index("section")
    home = jnp.int32(0)
    for layer in range(LAYERS):
        home = jnp.where(pairing[layer] == me, placement[layer], home)
    chip = home // 2
    row, col = masks()
    key = k_ref[0]

    def target(head, turned):
        total = jnp.zeros((TOKENS, TOKENS), jnp.float32)
        for twin in (2 * head, 2 * head + 1):
            query = q_ref[0, :, twin * HEAD_WIDTH : (twin + 1) * HEAD_WIDTH]
            if turned:
                total += softmax(dot(key, query, 1, 1) * INVERSE, row <= col, 0)
            else:
                total += softmax(dot(query, key, 1, 1) * INVERSE, col <= row, 1)
        return total * 0.5

    packed[PAIRS * TOKENS :, :] = jnp.zeros((PACKED - PAIRS * TOKENS, TOKENS), jnp.float32)
    started = []
    for pair in range(PAIRS):
        plain = target(2 * pair, False)
        turned = target(2 * pair + 1, True)
        packed[pair * TOKENS : (pair + 1) * TOKENS, :] = jnp.where(col <= row, plain, turned)
        at = PAIRS * TOKENS + pair
        packed[at : at + 1, :] = jnp.sum(
            jnp.where(row == col, turned, 0.0), axis=0, keepdims=True
        )
        end = (pair + 1) * TOKENS if pair < PAIRS - 1 else PACKED
        rows = slice(pair * TOKENS, end)
        copy = pltpu.make_async_copy(
            packed.at[rows, :], out_ref.at[chip, rows, :], sems.at[pair]
        )
        copy.start()
        started.append(copy)
    for copy in started:
        copy.wait()


def for_my_layers(pairing, placement, work):
    me = lax.axis_index("section")
    chip, core = me // 2, lax.rem(me, 2)

    def step(layer, carry):
        slots, rank = carry[:2], carry[2]
        home, source = placement[layer], pairing[layer]
        home_core = lax.rem(home, 2)
        here = home // 2 == chip
        mine = here & (lax.rem(source, 2) == core)
        slot = jnp.where(home_core == 0, slots[0], slots[1])

        @pl.when(mine)
        def _():
            work(layer, source // 2, home_core, slot, rank)

        return (
            slots[0] + (here & (home_core == 0)).astype(jnp.int32),
            slots[1] + (here & (home_core == 1)).astype(jnp.int32),
            rank + mine.astype(jnp.int32),
        )

    lax.fori_loop(0, LAYERS, step, (jnp.int32(0),) * 3)


def pack(ref, rank, pair, plain, turned):
    row, col = masks()
    ref[rank, pair * TOKENS : (pair + 1) * TOKENS, :] = jnp.where(col <= row, plain, turned)
    at = PAIRS * TOKENS + pair
    ref[rank, at : at + 1, :] = jnp.sum(
        jnp.where(row == col, turned, 0.0), axis=0, keepdims=True
    )


def scores_kernel(pairing, placement, scale_ref, qk_ref, raw_ref, logp_ref, table_ref):
    row, col = masks()
    at_row = lax.broadcasted_iota(jnp.int32, (2, LAYERS), 0)
    at_lane = lax.broadcasted_iota(jnp.int32, (2, LAYERS), 1)
    table = jnp.full((2, LAYERS), -1, jnp.int32)
    for layer in range(LAYERS):
        belongs = placement[layer] + LAYERS * pairing[layer]
        table = jnp.where((at_row == 1) & (at_lane == layer), belongs, table)
    table_ref[...] = table

    def work(layer, source_chip, home_core, slot, rank):
        code = layer + 8 * source_chip + 32 * home_core + 64 * slot
        table_ref[...] = jnp.where((at_row == 0) & (at_lane == rank), code, table_ref[...])
        key = qk_ref[home_core, slot, :, HEADS * HEAD_WIDTH :]

        def query(head):
            return qk_ref[home_core, slot, :, head * HEAD_WIDTH : (head + 1) * HEAD_WIDTH]

        tail_row = lax.broadcasted_iota(jnp.int32, (PACKED - PAIRS * TOKENS, TOKENS), 0)
        empty = jnp.zeros(tail_row.shape, jnp.float32)
        scales = empty
        for head in range(HEADS):
            scales = jnp.where(tail_row == HEADS + head, scale_ref[head, layer] * INVERSE, scales)
        raw_ref[rank, PAIRS * TOKENS :, :] = scales
        logp_ref[rank, PAIRS * TOKENS :, :] = empty
        for pair in range(PAIRS):
            plain = dot(query(2 * pair), key, 1, 1) * INVERSE
            turned = dot(key, query(2 * pair + 1), 1, 1) * INVERSE
            pack(raw_ref, rank, pair, plain, turned)
            plain = log_softmax(scale_ref[2 * pair, layer] * plain, col <= row, 1)
            turned = log_softmax(scale_ref[2 * pair + 1, layer] * turned, row <= col, 0)
            pack(logp_ref, rank, pair, plain, turned)

    for_my_layers(pairing, placement, work)


def student_kernel(table, arrived_ref, raw_ref, logp_ref, out_ref, grad_ref, sent_ref, sums_ref):
    core = lax.rem(lax.axis_index("section"), 2)
    row, col = masks()
    lower = col <= row
    place = lax.broadcasted_iota(jnp.int32, (8, TOKENS), 0)
    lane = lax.broadcasted_iota(jnp.int32, (8, TOKENS), 1)
    tail_row = lax.broadcasted_iota(jnp.int32, (TAIL, TOKENS), 0)
    sums_ref[...] = jnp.zeros_like(sums_ref)

    held = jnp.int32(0)
    for rank in range(2 * SLOTS):
        held += (table[0, rank] >= 0).astype(jnp.int32)

    def work(rank, carry):
        code = table[0, rank]
        layer, source_chip = code & 7, (code >> 3) & 3
        home_core, slot = (code >> 5) & 1, code >> 6

        def terms(rows):
            target = arrived_ref[source_chip, rows, :]
            target_logp = jnp.log(jnp.maximum(target, SMALLEST))
            student_logp = logp_ref[rank, rows, :]
            difference = jnp.exp(student_logp) - target
            return (
                jnp.sum(target * (target_logp - student_logp), axis=0, keepdims=True),
                difference,
                difference * raw_ref[rank, rows, :],
            )

        def scale_of(head):
            at = PAIRS * TOKENS + HEADS + head
            return raw_ref[rank, at : at + 1, :]

        last, last_difference, last_moved = terms(slice(PAIRS * TOKENS, PACKED))
        found = jnp.zeros((8, TOKENS), jnp.float32)
        divergence = last
        tail = jnp.zeros((TAIL, TOKENS), jnp.float32)
        pieces = []
        for pair in range(PAIRS):
            one, difference, moved = terms(slice(pair * TOKENS, (pair + 1) * TOKENS))
            divergence += one
            first = scale_of(2 * pair)
            second = scale_of(2 * pair + 1)
            pieces.append(difference * jnp.where(lower, first, second))
            tail = jnp.where(tail_row == pair, last_difference[pair : pair + 1] * second, tail)
            of_first = jnp.sum(jnp.where(lower, moved, 0.0), axis=0, keepdims=True)
            of_second = jnp.sum(jnp.where(lower, 0.0, moved), axis=0, keepdims=True)
            of_second += last_moved[pair : pair + 1]
            found = jnp.where(place == 1 + 2 * pair, of_first, found)
            found = jnp.where(place == 2 + 2 * pair, of_second, found)
        found = jnp.where(place == 0, divergence, found)
        found = jnp.sum(found, axis=1, keepdims=True)
        goes_to = jnp.where(place == 0, layer, SCALE_LANE + LAYERS * (place - 1) + layer)
        found = jnp.where((lane == goes_to) & (place <= HEADS), found, 0.0)
        sums_ref[...] += jnp.sum(found, axis=0, keepdims=True)
        pieces.append(tail)

        def put(ref, at):
            for n, piece in enumerate(pieces):
                to = pl.multiple_of(at + n * TOKENS, TAIL)
                ref[pl.ds(to, piece.shape[0]), :] = piece.astype(jnp.bfloat16)

        @pl.when(home_core == core)
        def _():
            put(grad_ref, slot * SLOT_ROWS)

        @pl.when(home_core != core)
        def _():
            put(sent_ref, slot * SLOT_ROWS)

        return carry

    lax.fori_loop(0, held, work, 0)
    out_ref[...] = jnp.broadcast_to(sums_ref[...][None], out_ref.shape)


def gradient_kernel(table, grad_ref, sent_ref, qk_ref, q_out, k_out):
    me = lax.axis_index("section")
    core = lax.rem(me, 2)
    row, col = masks()
    held, layers = jnp.int32(0), [jnp.int32(0)] * SLOTS
    for layer in range(LAYERS):
        here = (table[1, layer] & (LAYERS - 1)) == me
        layers = [
            jnp.where(here & (held == slot), layer, had) for slot, had in enumerate(layers)
        ]
        held += here.astype(jnp.int32)
    for slot in range(SLOTS):

        @pl.when(slot < held)
        def _():
            direct = ((table[1, layers[slot]] >> 3) & 1) == core
            key = qk_ref[core, slot, :, HEADS * HEAD_WIDTH :]
            total = jnp.zeros((TOKENS, HEAD_WIDTH), jnp.float32)

            def rows(at, count):
                at = slot * SLOT_ROWS + at
                near = grad_ref[at : at + count, :].astype(jnp.float32)
                other = sent_ref[1 - core, at : at + count, :].astype(jnp.float32)
                return jnp.where(direct, near, other)

            tail = rows(PAIRS * TOKENS, TAIL)
            for head in range(HEADS):
                pair, over = head // 2, head % 2
                square = rows(pair * TOKENS, TOKENS)
                if over:
                    diagonal = jnp.where(row == col, tail[pair : pair + 1], 0.0)
                    grad = jnp.where(row < col, square, diagonal)
                else:
                    grad = jnp.where(col <= row, square, 0.0)
                grad = grad.astype(jnp.bfloat16)
                lanes = slice(head * HEAD_WIDTH, (head + 1) * HEAD_WIDTH)
                query = qk_ref[core, slot, :, lanes]
                q_out[0, slot, :, lanes] = dot(grad, key, 1 - over, 0).astype(jnp.bfloat16)
                total += dot(grad, query, over, 0)
            k_out[0, slot] = total.astype(jnp.bfloat16)

        @pl.when(slot >= held)
        def _():
            q_out[0, slot] = jnp.zeros(q_out.shape[2:], jnp.bfloat16)
            k_out[0, slot] = jnp.zeros(k_out.shape[2:], jnp.bfloat16)


def final_kernel(rows_ref, kl_ref, scale_ref):
    def total(core):
        each = jnp.sum(rows_ref[core], axis=0)
        return each[0:1] + each[SUM_ROWS : SUM_ROWS + 1]

    divergence = total(0)
    kl_ref[...] = divergence[:, :LAYERS] / (STUDENT_HEADS * TOKENS)
    terms = total(1)
    scale_ref[...] = jnp.concatenate(
        [terms[:, SCALE_LANE + LAYERS * h : SCALE_LANE + LAYERS * (h + 1)] for h in range(HEADS)], axis=0
    )


VMEM = pl.BlockSpec(memory_space=pltpu.VMEM)
ANY = pl.BlockSpec(memory_space=pl.ANY)
SMEM = pl.BlockSpec(memory_space=pltpu.SMEM)
SMALL = pltpu.CompilerParams(vmem_limit_bytes=16 * 2**20)


def kept(array):
    return pltpu.with_memory_space_constraint(array, pltpu.VMEM)


def cost(flops, moved):
    return pl.CostEstimate(flops=flops, bytes_accessed=moved, transcendentals=0)


def local(chips, groups, teacher_q, teacher_k, student_q, student_k, student_scale, pairing, placement):
    f32, bf16 = jnp.float32, jnp.bfloat16
    over_x = [[2 * x + core for x in range(chips)] for core in range(2)]
    of_chip = [[2 * x, 2 * x + 1] for x in range(chips)]
    members = len(groups[0])

    packed = pl.pallas_call(
        teacher_kernel,
        out_shape=jax.ShapeDtypeStruct((chips, PACKED, TOKENS), f32),
        in_specs=[SMEM, SMEM, VMEM, VMEM],
        out_specs=ANY,
        scratch_shapes=[
            pltpu.VMEM((PACKED, TOKENS), f32),
            pltpu.SemaphoreType.DMA((PAIRS,)),
        ],
        cost_estimate=cost(8 * 2 * TOKENS**3, 400_000),
        name="teacher",
    )(pairing, placement, teacher_q, teacher_k)
    arrived = lax.all_to_all(
        packed, "section", 0, 0, tiled=True, axis_index_groups=over_x
    )
    def of_both_cores(array):
        return lax.all_gather(array, "section", axis_index_groups=of_chip)

    chip_qk = kept(of_both_cores(jnp.concatenate((student_q[0], student_k[0]), axis=2)))
    at_once = 2 * SLOTS
    squares = pltpu.VMEM((at_once, PACKED, TOKENS), f32)
    raw, logp, table = pl.pallas_call(
        scores_kernel,
        out_shape=(squares, squares, pltpu.VMEM((2, LAYERS), jnp.int32)),
        in_specs=[SMEM, SMEM, SMEM, VMEM],
        out_specs=(VMEM, VMEM, VMEM),
        cost_estimate=cost(8 * 2 * TOKENS**3, 1_400_000),
        compiler_params=SMALL,
        name="scores",
    )(pairing, placement, student_scale.T, chip_qk)
    table = kept(table)

    sums, grads, sent = pl.pallas_call(
        student_kernel,
        out_shape=(
            pltpu.VMEM((members, SUM_ROWS, TOKENS), f32),
            pltpu.VMEM((SENT, TOKENS), bf16),
            pltpu.VMEM((SENT, TOKENS), bf16),
        ),
        in_specs=[SMEM, VMEM, VMEM, VMEM],
        out_specs=(VMEM, VMEM, VMEM),
        scratch_shapes=[pltpu.VMEM((1, TOKENS), f32)],
        cost_estimate=cost(8 * 2 * TOKENS**3, 1_800_000),
        compiler_params=SMALL,
        name="student",
    )(table, *map(kept, (arrived, raw, logp)))

    sums = lax.all_gather(sums, "section", axis=1, tiled=True, axis_index_groups=of_chip)
    rows = lax.all_to_all(sums, AXES, 0, 0, tiled=True, axis_index_groups=groups)
    chip_sent = kept(of_both_cores(sent))
    q_grad, k_grad = pl.pallas_call(
        gradient_kernel,
        out_shape=(
            jax.ShapeDtypeStruct(student_q.shape, bf16),
            jax.ShapeDtypeStruct(student_k.shape, bf16),
        ),
        in_specs=[SMEM, VMEM, VMEM, VMEM],
        out_specs=(VMEM, VMEM),
        cost_estimate=cost(16 * 2 * TOKENS**3, 900_000),
        compiler_params=SMALL,
        name="gradient",
    )(table, kept(grads), chip_sent, chip_qk)

    both = of_both_cores(rows)
    layer_kl, scale_grad = pl.pallas_call(
        final_kernel,
        out_shape=(
            jax.ShapeDtypeStruct((1, LAYERS), f32),
            jax.ShapeDtypeStruct((HEADS, LAYERS), f32),
        ),
        in_specs=[VMEM],
        out_specs=(VMEM, VMEM),
        compiler_params=SMALL,
        name="final",
    )(kept(both))
    return (q_grad, k_grad, layer_kl, scale_grad.T)


def reduction_groups(sections, heads, replicas):
    def flat(section, head, replica):
        return (section * heads + head) * replicas + replica

    chips = range(sections // 2)
    first = [
        [flat(2 * x, h, d) for x in chips for h in range(heads)] for d in range(replicas)
    ]
    second = [
        [flat(2 * x + 1, h, d) for x in chips for d in range(replicas)] for h in range(heads)
    ]
    return first + second


def solution(mesh):
    sections, heads, replicas = (mesh.shape[a] for a in AXES)
    return jax.shard_map(
        functools.partial(local, sections // 2, reduction_groups(sections, heads, replicas)),
        mesh=mesh,
        in_specs=(
            P("section", "dp", "head"),
            P("section", "dp", "head"),
            P("section", None, "dp", "head"),
            P("section", None, "dp", "head"),
            P(None, "head"),
            P(),
            P(),
        ),
        out_specs=(
            P("section", None, "dp", "head"),
            P("section", None, "dp", "head"),
            P("dp", None),
            P(None, "head"),
        ),
        check_vma=False,
    )
```

```python
import functools
import math

import jax
import jax.numpy as jnp
from jax import lax
from jax.experimental import pallas as pl
from jax.experimental.pallas import tpu as pltpu
from jax.sharding import PartitionSpec as P

STUDENT_HEADS = 32
HEAD_WIDTH = 128
TOKENS = 128
LAYERS = 8
SLOTS = 2
HEADS = 4
PACKED = HEADS // 2 * TOKENS + 8
SCALE_LANE = 32
PAIRS = HEADS // 2
TAIL = 16
SLOT_ROWS = PAIRS * TOKENS + TAIL
SENT = SLOTS * SLOT_ROWS
INVERSE = 1.0 / math.sqrt(HEAD_WIDTH)
HIDDEN = -1e30
SMALLEST = 1.2e-38
AXES = ("section", "head", "dp")


def dot(a, b, over_a, over_b):
    return lax.dot_general(
        a, b, (((over_a,), (over_b,)), ((), ())), preferred_element_type=jnp.float32
    )


def masks():
    row = lax.broadcasted_iota(jnp.int32, (TOKENS, TOKENS), 0)
    col = lax.broadcasted_iota(jnp.int32, (TOKENS, TOKENS), 1)
    return row, col


def log_softmax(scores, visible, axis):
    scores = jnp.where(visible, scores, HIDDEN)
    shifted = scores - jnp.max(scores, axis=axis, keepdims=True)
    return shifted - jnp.log(jnp.sum(jnp.exp(shifted), axis=axis, keepdims=True))


def softmax(scores, visible, axis):
    scores = jnp.where(visible, scores, HIDDEN)
    powers = jnp.exp(scores - jnp.max(scores, axis=axis, keepdims=True))
    return powers * (1.0 / jnp.sum(powers, axis=axis, keepdims=True))


def teacher_kernel(pairing, placement, q_ref, k_ref, out_ref, packed, sems):
    me = lax.axis_index("section")
    home = jnp.int32(0)
    for layer in range(LAYERS):
        home = jnp.where(pairing[layer] == me, placement[layer], home)
    chip = home // 2
    row, col = masks()
    key = k_ref[0]

    def target(head, turned):
        total = jnp.zeros((TOKENS, TOKENS), jnp.float32)
        for twin in (2 * head, 2 * head + 1):
            query = q_ref[0, :, twin * HEAD_WIDTH : (twin + 1) * HEAD_WIDTH]
            if turned:
                total += softmax(dot(key, query, 1, 1) * INVERSE, row <= col, 0)
            else:
                total += softmax(dot(query, key, 1, 1) * INVERSE, col <= row, 1)
        return total * 0.5

    packed[PAIRS * TOKENS :, :] = jnp.zeros((PACKED - PAIRS * TOKENS, TOKENS), jnp.float32)
    started = []
    for pair in range(PAIRS):
        plain = target(2 * pair, False)
        turned = target(2 * pair + 1, True)
        packed[pair * TOKENS : (pair + 1) * TOKENS, :] = jnp.where(col <= row, plain, turned)
        at = PAIRS * TOKENS + pair
        packed[at : at + 1, :] = jnp.sum(
            jnp.where(row == col, turned, 0.0), axis=0, keepdims=True
        )
        end = (pair + 1) * TOKENS if pair < PAIRS - 1 else PACKED
        rows = slice(pair * TOKENS, end)
        copy = pltpu.make_async_copy(
            packed.at[rows, :], out_ref.at[chip, rows, :], sems.at[pair]
        )
        copy.start()
        started.append(copy)
    for copy in started:
        copy.wait()


def for_my_layers(pairing, placement, work):
    me = lax.axis_index("section")
    chip, core = me // 2, lax.rem(me, 2)

    def step(layer, carry):
        slots, rank = carry[:2], carry[2]
        home, source = placement[layer], pairing[layer]
        home_core = lax.rem(home, 2)
        here = home // 2 == chip
        mine = here & (lax.rem(source, 2) == core)
        slot = jnp.where(home_core == 0, slots[0], slots[1])

        @pl.when(mine)
        def _():
            work(layer, source // 2, home_core, slot, rank)

        return (
            slots[0] + (here & (home_core == 0)).astype(jnp.int32),
            slots[1] + (here & (home_core == 1)).astype(jnp.int32),
            rank + mine.astype(jnp.int32),
        )

    lax.fori_loop(0, LAYERS, step, (jnp.int32(0),) * 3)


def pack(ref, rank, pair, plain, turned):
    row, col = masks()
    ref[rank, pair * TOKENS : (pair + 1) * TOKENS, :] = jnp.where(col <= row, plain, turned)
    at = PAIRS * TOKENS + pair
    ref[rank, at : at + 1, :] = jnp.sum(
        jnp.where(row == col, turned, 0.0), axis=0, keepdims=True
    )


def scores_kernel(pairing, placement, scale_ref, qk_ref, raw_ref, logp_ref, table_ref):
    row, col = masks()
    at_row = lax.broadcasted_iota(jnp.int32, (2, LAYERS), 0)
    at_lane = lax.broadcasted_iota(jnp.int32, (2, LAYERS), 1)
    table = jnp.full((2, LAYERS), -1, jnp.int32)
    for layer in range(LAYERS):
        belongs = placement[layer] + LAYERS * pairing[layer]
        table = jnp.where((at_row == 1) & (at_lane == layer), belongs, table)
    table_ref[...] = table

    def work(layer, source_chip, home_core, slot, rank):
        code = layer + 8 * source_chip + 32 * home_core + 64 * slot
        table_ref[...] = jnp.where((at_row == 0) & (at_lane == rank), code, table_ref[...])
        key = qk_ref[home_core, slot, :, HEADS * HEAD_WIDTH :]

        def query(head):
            return qk_ref[home_core, slot, :, head * HEAD_WIDTH : (head + 1) * HEAD_WIDTH]

        tail_row = lax.broadcasted_iota(jnp.int32, (PACKED - PAIRS * TOKENS, TOKENS), 0)
        empty = jnp.zeros(tail_row.shape, jnp.float32)
        scales = empty
        for head in range(HEADS):
            scales = jnp.where(tail_row == HEADS + head, scale_ref[head, layer] * INVERSE, scales)
        raw_ref[rank, PAIRS * TOKENS :, :] = scales
        logp_ref[rank, PAIRS * TOKENS :, :] = empty
        for pair in range(PAIRS):
            plain = dot(query(2 * pair), key, 1, 1) * INVERSE
            turned = dot(key, query(2 * pair + 1), 1, 1) * INVERSE
            pack(raw_ref, rank, pair, plain, turned)
            plain = log_softmax(scale_ref[2 * pair, layer] * plain, col <= row, 1)
            turned = log_softmax(scale_ref[2 * pair + 1, layer] * turned, row <= col, 0)
            pack(logp_ref, rank, pair, plain, turned)

    for_my_layers(pairing, placement, work)


def student_kernel(table, arrived_ref, raw_ref, logp_ref, sums_ref, grad_ref, sent_ref):
    core = lax.rem(lax.axis_index("section"), 2)
    row, col = masks()
    lower = col <= row
    place = lax.broadcasted_iota(jnp.int32, (8, TOKENS), 0)
    lane = lax.broadcasted_iota(jnp.int32, (8, TOKENS), 1)
    tail_row = lax.broadcasted_iota(jnp.int32, (TAIL, TOKENS), 0)
    sums_ref[...] = jnp.zeros_like(sums_ref)

    held = jnp.int32(0)
    for rank in range(2 * SLOTS):
        held += (table[0, rank] >= 0).astype(jnp.int32)

    def work(rank, carry):
        code = table[0, rank]
        layer, source_chip = code & 7, (code >> 3) & 3
        home_core, slot = (code >> 5) & 1, code >> 6

        def terms(rows):
            target = arrived_ref[source_chip, rows, :]
            target_logp = jnp.log(jnp.maximum(target, SMALLEST))
            student_logp = logp_ref[rank, rows, :]
            difference = jnp.exp(student_logp) - target
            return (
                jnp.sum(target * (target_logp - student_logp), axis=0, keepdims=True),
                difference,
                difference * raw_ref[rank, rows, :],
            )

        def scale_of(head):
            at = PAIRS * TOKENS + HEADS + head
            return raw_ref[rank, at : at + 1, :]

        last, last_difference, last_moved = terms(slice(PAIRS * TOKENS, PACKED))
        found = jnp.zeros((8, TOKENS), jnp.float32)
        divergence = last
        tail = jnp.zeros((TAIL, TOKENS), jnp.float32)
        pieces = []
        for pair in range(PAIRS):
            one, difference, moved = terms(slice(pair * TOKENS, (pair + 1) * TOKENS))
            divergence += one
            first = scale_of(2 * pair)
            second = scale_of(2 * pair + 1)
            pieces.append(difference * jnp.where(lower, first, second))
            tail = jnp.where(tail_row == pair, last_difference[pair : pair + 1] * second, tail)
            of_first = jnp.sum(jnp.where(lower, moved, 0.0), axis=0, keepdims=True)
            of_second = jnp.sum(jnp.where(lower, 0.0, moved), axis=0, keepdims=True)
            of_second += last_moved[pair : pair + 1]
            found = jnp.where(place == 1 + 2 * pair, of_first, found)
            found = jnp.where(place == 2 + 2 * pair, of_second, found)
        found = jnp.where(place == 0, divergence, found)
        found = jnp.sum(found, axis=1, keepdims=True)
        goes_to = jnp.where(place == 0, layer, SCALE_LANE + LAYERS * (place - 1) + layer)
        found = jnp.where((lane == goes_to) & (place <= HEADS), found, 0.0)
        sums_ref[...] += jnp.sum(found, axis=0, keepdims=True)
        pieces.append(tail)

        def put(ref, at):
            for n, piece in enumerate(pieces):
                to = pl.multiple_of(at + n * TOKENS, TAIL)
                ref[pl.ds(to, piece.shape[0]), :] = piece.astype(jnp.bfloat16)

        @pl.when(home_core == core)
        def _():
            put(grad_ref, slot * SLOT_ROWS)

        @pl.when(home_core != core)
        def _():
            put(sent_ref, slot * SLOT_ROWS)

        return carry

    lax.fori_loop(0, held, work, 0)


def spread_kernel(pair_ref, out_ref):
    out_ref[...] = jnp.broadcast_to(pair_ref[0] + pair_ref[1], out_ref.shape)


def gradient_kernel(table, grad_ref, sent_ref, qk_ref, q_out, k_out):
    me = lax.axis_index("section")
    core = lax.rem(me, 2)
    row, col = masks()
    held, layers = jnp.int32(0), [jnp.int32(0)] * SLOTS
    for layer in range(LAYERS):
        here = (table[1, layer] & (LAYERS - 1)) == me
        layers = [
            jnp.where(here & (held == slot), layer, had) for slot, had in enumerate(layers)
        ]
        held += here.astype(jnp.int32)
    for slot in range(SLOTS):

        @pl.when(slot < held)
        def _():
            direct = ((table[1, layers[slot]] >> 3) & 1) == core
            key = qk_ref[core, slot, :, HEADS * HEAD_WIDTH :]
            total = jnp.zeros((TOKENS, HEAD_WIDTH), jnp.float32)

            def rows(at, count):
                at = slot * SLOT_ROWS + at
                near = grad_ref[at : at + count, :].astype(jnp.float32)
                other = sent_ref[1 - core, at : at + count, :].astype(jnp.float32)
                return jnp.where(direct, near, other)

            tail = rows(PAIRS * TOKENS, TAIL)
            for head in range(HEADS):
                pair, over = head // 2, head % 2
                square = rows(pair * TOKENS, TOKENS)
                if over:
                    diagonal = jnp.where(row == col, tail[pair : pair + 1], 0.0)
                    grad = jnp.where(row < col, square, diagonal)
                else:
                    grad = jnp.where(col <= row, square, 0.0)
                grad = grad.astype(jnp.bfloat16)
                lanes = slice(head * HEAD_WIDTH, (head + 1) * HEAD_WIDTH)
                query = qk_ref[core, slot, :, lanes]
                q_out[0, slot, :, lanes] = dot(grad, key, 1 - over, 0).astype(jnp.bfloat16)
                total += dot(grad, query, over, 0)
            k_out[0, slot] = total.astype(jnp.bfloat16)

        @pl.when(slot >= held)
        def _():
            q_out[0, slot] = jnp.zeros(q_out.shape[2:], jnp.bfloat16)
            k_out[0, slot] = jnp.zeros(k_out.shape[2:], jnp.bfloat16)


def final_kernel(rows_ref, kl_ref, scale_ref):
    divergence = jnp.sum(rows_ref[0], axis=0, keepdims=True)
    kl_ref[...] = divergence[:, :LAYERS] / (STUDENT_HEADS * TOKENS)
    terms = jnp.sum(rows_ref[1], axis=0, keepdims=True)
    scale_ref[...] = jnp.concatenate(
        [terms[:, SCALE_LANE + LAYERS * h : SCALE_LANE + LAYERS * (h + 1)] for h in range(HEADS)], axis=0
    )


VMEM = pl.BlockSpec(memory_space=pltpu.VMEM)
ANY = pl.BlockSpec(memory_space=pl.ANY)
SMEM = pl.BlockSpec(memory_space=pltpu.SMEM)
SMALL = pltpu.CompilerParams(vmem_limit_bytes=16 * 2**20)


def kept(array):
    return pltpu.with_memory_space_constraint(array, pltpu.VMEM)


def cost(flops, moved):
    return pl.CostEstimate(flops=flops, bytes_accessed=moved, transcendentals=0)


def local(chips, groups, teacher_q, teacher_k, student_q, student_k, student_scale, pairing, placement):
    f32, bf16 = jnp.float32, jnp.bfloat16
    over_x = [[2 * x + core for x in range(chips)] for core in range(2)]
    of_chip = [[2 * x, 2 * x + 1] for x in range(chips)]
    members = len(groups[0])

    packed = pl.pallas_call(
        teacher_kernel,
        out_shape=jax.ShapeDtypeStruct((chips, PACKED, TOKENS), f32),
        in_specs=[SMEM, SMEM, VMEM, VMEM],
        out_specs=ANY,
        scratch_shapes=[
            pltpu.VMEM((PACKED, TOKENS), f32),
            pltpu.SemaphoreType.DMA((PAIRS,)),
        ],
        cost_estimate=cost(8 * 2 * TOKENS**3, 400_000),
        name="teacher",
    )(pairing, placement, teacher_q, teacher_k)
    arrived = lax.all_to_all(
        packed, "section", 0, 0, tiled=True, axis_index_groups=over_x
    )
    def of_both_cores(array):
        return lax.all_gather(array, "section", axis_index_groups=of_chip)

    chip_qk = kept(of_both_cores(jnp.concatenate((student_q[0], student_k[0]), axis=2)))
    at_once = 2 * SLOTS
    squares = pltpu.VMEM((at_once, PACKED, TOKENS), f32)
    raw, logp, table = pl.pallas_call(
        scores_kernel,
        out_shape=(squares, squares, pltpu.VMEM((2, LAYERS), jnp.int32)),
        in_specs=[SMEM, SMEM, SMEM, VMEM],
        out_specs=(VMEM, VMEM, VMEM),
        cost_estimate=cost(8 * 2 * TOKENS**3, 1_400_000),
        compiler_params=SMALL,
        name="scores",
    )(pairing, placement, student_scale.T, chip_qk)
    table = kept(table)

    sums, grads, sent = pl.pallas_call(
        student_kernel,
        out_shape=(
            pltpu.VMEM((1, TOKENS), f32),
            pltpu.VMEM((SENT, TOKENS), bf16),
            pltpu.VMEM((SENT, TOKENS), bf16),
        ),
        in_specs=[SMEM, VMEM, VMEM, VMEM],
        out_specs=(VMEM, VMEM, VMEM),
        cost_estimate=cost(8 * 2 * TOKENS**3, 1_800_000),
        compiler_params=SMALL,
        name="student",
    )(table, *map(kept, (arrived, raw, logp)))

    sums = pl.pallas_call(
        spread_kernel,
        out_shape=jax.ShapeDtypeStruct((members, TOKENS), f32),
        in_specs=[VMEM],
        out_specs=VMEM,
        compiler_params=SMALL,
        name="spread",
    )(kept(of_both_cores(sums)))
    chip_sent = kept(of_both_cores(sent))
    rows = lax.all_to_all(
        sums.reshape(members, 1, TOKENS), AXES, 0, 0, tiled=True, axis_index_groups=groups
    )
    q_grad, k_grad = pl.pallas_call(
        gradient_kernel,
        out_shape=(
            jax.ShapeDtypeStruct(student_q.shape, bf16),
            jax.ShapeDtypeStruct(student_k.shape, bf16),
        ),
        in_specs=[SMEM, VMEM, VMEM, VMEM],
        out_specs=(VMEM, VMEM),
        cost_estimate=cost(16 * 2 * TOKENS**3, 900_000),
        compiler_params=SMALL,
        name="gradient",
    )(table, kept(grads), chip_sent, chip_qk)

    both = of_both_cores(rows.reshape(members, TOKENS))
    layer_kl, scale_grad = pl.pallas_call(
        final_kernel,
        out_shape=(
            jax.ShapeDtypeStruct((1, LAYERS), f32),
            jax.ShapeDtypeStruct((HEADS, LAYERS), f32),
        ),
        in_specs=[VMEM],
        out_specs=(VMEM, VMEM),
        compiler_params=SMALL,
        name="final",
    )(kept(both))
    return (q_grad, k_grad, layer_kl, scale_grad.T)


def reduction_groups(sections, heads, replicas):
    def flat(section, head, replica):
        return (section * heads + head) * replicas + replica

    chips = range(sections // 2)
    first = [
        [flat(2 * x, h, d) for x in chips for h in range(heads)] for d in range(replicas)
    ]
    second = [
        [flat(2 * x + 1, h, d) for x in chips for d in range(replicas)] for h in range(heads)
    ]
    return first + second


def solution(mesh):
    sections, heads, replicas = (mesh.shape[a] for a in AXES)
    return jax.shard_map(
        functools.partial(local, sections // 2, reduction_groups(sections, heads, replicas)),
        mesh=mesh,
        in_specs=(
            P("section", "dp", "head"),
            P("section", "dp", "head"),
            P("section", None, "dp", "head"),
            P("section", None, "dp", "head"),
            P(None, "head"),
            P(),
            P(),
        ),
        out_specs=(
            P("section", None, "dp", "head"),
            P("section", None, "dp", "head"),
            P("dp", None),
            P(None, "head"),
        ),
        check_vma=False,
    )
```

```python
import functools
import math

import jax
import jax.numpy as jnp
from jax import lax
from jax.experimental import pallas as pl
from jax.experimental.pallas import tpu as pltpu
from jax.sharding import PartitionSpec as P

STUDENT_HEADS = 32
HEAD_WIDTH = 128
TOKENS = 128
LAYERS = 8
SLOTS = 2
HEADS = 4
PACKED = HEADS // 2 * TOKENS + 8
SCALE_LANE = 32
PAIRS = HEADS // 2
TAIL = 16
SLOT_ROWS = PAIRS * TOKENS + TAIL
SENT = SLOTS * SLOT_ROWS
INVERSE = 1.0 / math.sqrt(HEAD_WIDTH)
HIDDEN = -1e30
SMALLEST = 1.2e-38
AXES = ("section", "head", "dp")


def dot(a, b, over_a, over_b):
    return lax.dot_general(
        a, b, (((over_a,), (over_b,)), ((), ())), preferred_element_type=jnp.float32
    )


def masks():
    row = lax.broadcasted_iota(jnp.int32, (TOKENS, TOKENS), 0)
    col = lax.broadcasted_iota(jnp.int32, (TOKENS, TOKENS), 1)
    return row, col


def log_softmax(scores, visible, axis):
    scores = jnp.where(visible, scores, HIDDEN)
    shifted = scores - jnp.max(scores, axis=axis, keepdims=True)
    return shifted - jnp.log(jnp.sum(jnp.exp(shifted), axis=axis, keepdims=True))


def softmax(scores, visible, axis):
    scores = jnp.where(visible, scores, HIDDEN)
    powers = jnp.exp(scores - jnp.max(scores, axis=axis, keepdims=True))
    return powers * (1.0 / jnp.sum(powers, axis=axis, keepdims=True))


def teacher_kernel(pairing, placement, q_ref, k_ref, out_ref, packed, sems):
    me = lax.axis_index("section")
    home = jnp.int32(0)
    for layer in range(LAYERS):
        home = jnp.where(pairing[layer] == me, placement[layer], home)
    chip = home // 2
    row, col = masks()
    key = k_ref[0]

    def target(head, turned):
        total = jnp.zeros((TOKENS, TOKENS), jnp.float32)
        for twin in (2 * head, 2 * head + 1):
            query = q_ref[0, :, twin * HEAD_WIDTH : (twin + 1) * HEAD_WIDTH]
            if turned:
                total += softmax(dot(key, query, 1, 1) * INVERSE, row <= col, 0)
            else:
                total += softmax(dot(query, key, 1, 1) * INVERSE, col <= row, 1)
        return total * 0.5

    packed[PAIRS * TOKENS :, :] = jnp.zeros((PACKED - PAIRS * TOKENS, TOKENS), jnp.float32)
    started = []
    for pair in range(PAIRS):
        plain = target(2 * pair, False)
        turned = target(2 * pair + 1, True)
        packed[pair * TOKENS : (pair + 1) * TOKENS, :] = jnp.where(col <= row, plain, turned)
        at = PAIRS * TOKENS + pair
        packed[at : at + 1, :] = jnp.sum(
            jnp.where(row == col, turned, 0.0), axis=0, keepdims=True
        )
        end = (pair + 1) * TOKENS if pair < PAIRS - 1 else PACKED
        rows = slice(pair * TOKENS, end)
        copy = pltpu.make_async_copy(
            packed.at[rows, :], out_ref.at[chip, rows, :], sems.at[pair]
        )
        copy.start()
        started.append(copy)
    for copy in started:
        copy.wait()


def for_my_layers(pairing, placement, work):
    me = lax.axis_index("section")
    chip, core = me // 2, lax.rem(me, 2)

    def step(layer, carry):
        slots, rank = carry[:2], carry[2]
        home, source = placement[layer], pairing[layer]
        home_core = lax.rem(home, 2)
        here = home // 2 == chip
        mine = here & (lax.rem(source, 2) == core)
        slot = jnp.where(home_core == 0, slots[0], slots[1])

        @pl.when(mine)
        def _():
            work(layer, source // 2, home_core, slot, rank)

        return (
            slots[0] + (here & (home_core == 0)).astype(jnp.int32),
            slots[1] + (here & (home_core == 1)).astype(jnp.int32),
            rank + mine.astype(jnp.int32),
        )

    lax.fori_loop(0, LAYERS, step, (jnp.int32(0),) * 3)


def pack(ref, rank, pair, plain, turned):
    row, col = masks()
    ref[rank, pair * TOKENS : (pair + 1) * TOKENS, :] = jnp.where(col <= row, plain, turned)
    at = PAIRS * TOKENS + pair
    ref[rank, at : at + 1, :] = jnp.sum(
        jnp.where(row == col, turned, 0.0), axis=0, keepdims=True
    )


def scores_kernel(pairing, placement, scale_ref, qk_ref, raw_ref, logp_ref, table_ref):
    row, col = masks()
    at_row = lax.broadcasted_iota(jnp.int32, (2, LAYERS), 0)
    at_lane = lax.broadcasted_iota(jnp.int32, (2, LAYERS), 1)
    table = jnp.full((2, LAYERS), -1, jnp.int32)
    for layer in range(LAYERS):
        belongs = placement[layer] + LAYERS * pairing[layer]
        table = jnp.where((at_row == 1) & (at_lane == layer), belongs, table)
    table_ref[...] = table

    def work(layer, source_chip, home_core, slot, rank):
        code = layer + 8 * source_chip + 32 * home_core + 64 * slot
        table_ref[...] = jnp.where((at_row == 0) & (at_lane == rank), code, table_ref[...])
        key = qk_ref[home_core, slot, :, HEADS * HEAD_WIDTH :]

        def query(head):
            return qk_ref[home_core, slot, :, head * HEAD_WIDTH : (head + 1) * HEAD_WIDTH]

        tail_row = lax.broadcasted_iota(jnp.int32, (PACKED - PAIRS * TOKENS, TOKENS), 0)
        empty = jnp.zeros(tail_row.shape, jnp.float32)
        scales = empty
        for head in range(HEADS):
            scales = jnp.where(tail_row == HEADS + head, scale_ref[head, layer] * INVERSE, scales)
        raw_ref[rank, PAIRS * TOKENS :, :] = scales
        logp_ref[rank, PAIRS * TOKENS :, :] = empty
        for pair in range(PAIRS):
            plain = dot(query(2 * pair), key, 1, 1) * INVERSE
            turned = dot(key, query(2 * pair + 1), 1, 1) * INVERSE
            pack(raw_ref, rank, pair, plain, turned)
            plain = log_softmax(scale_ref[2 * pair, layer] * plain, col <= row, 1)
            turned = log_softmax(scale_ref[2 * pair + 1, layer] * turned, row <= col, 0)
            pack(logp_ref, rank, pair, plain, turned)

    for_my_layers(pairing, placement, work)


def student_kernel(table, arrived_ref, raw_ref, logp_ref, sums_ref):
    row, col = masks()
    lower = col <= row
    place = lax.broadcasted_iota(jnp.int32, (8, TOKENS), 0)
    lane = lax.broadcasted_iota(jnp.int32, (8, TOKENS), 1)
    sums_ref[...] = jnp.zeros_like(sums_ref)

    held = jnp.int32(0)
    for rank in range(2 * SLOTS):
        held += (table[0, rank] >= 0).astype(jnp.int32)

    def work(rank, carry):
        code = table[0, rank]
        layer, source_chip = code & 7, (code >> 3) & 3

        def terms(rows):
            target = arrived_ref[source_chip, rows, :]
            target_logp = jnp.log(jnp.maximum(target, SMALLEST))
            student_logp = logp_ref[rank, rows, :]
            difference = jnp.exp(student_logp) - target
            return (
                jnp.sum(target * (target_logp - student_logp), axis=0, keepdims=True),
                difference * raw_ref[rank, rows, :],
            )

        last, last_moved = terms(slice(PAIRS * TOKENS, PACKED))
        found = jnp.zeros((8, TOKENS), jnp.float32)
        divergence = last
        for pair in range(PAIRS):
            one, moved = terms(slice(pair * TOKENS, (pair + 1) * TOKENS))
            divergence += one
            of_first = jnp.sum(jnp.where(lower, moved, 0.0), axis=0, keepdims=True)
            of_second = jnp.sum(jnp.where(lower, 0.0, moved), axis=0, keepdims=True)
            of_second += last_moved[pair : pair + 1]
            found = jnp.where(place == 1 + 2 * pair, of_first, found)
            found = jnp.where(place == 2 + 2 * pair, of_second, found)
        found = jnp.where(place == 0, divergence, found)
        found = jnp.sum(found, axis=1, keepdims=True)
        goes_to = jnp.where(place == 0, layer, SCALE_LANE + LAYERS * (place - 1) + layer)
        found = jnp.where((lane == goes_to) & (place <= HEADS), found, 0.0)
        sums_ref[...] += jnp.sum(found, axis=0, keepdims=True)
        return carry

    lax.fori_loop(0, held, work, 0)


def slope_kernel(table, arrived_ref, raw_ref, logp_ref, grad_ref, sent_ref):
    core = lax.rem(lax.axis_index("section"), 2)
    row, col = masks()
    lower = col <= row
    tail_row = lax.broadcasted_iota(jnp.int32, (TAIL, TOKENS), 0)
    held = jnp.int32(0)
    for rank in range(2 * SLOTS):
        held += (table[0, rank] >= 0).astype(jnp.int32)

    def work(rank, carry):
        code = table[0, rank]
        source_chip, home_core, slot = (code >> 3) & 3, (code >> 5) & 1, code >> 6

        def difference(rows):
            return jnp.exp(logp_ref[rank, rows, :]) - arrived_ref[source_chip, rows, :]

        def scale_of(head):
            at = PAIRS * TOKENS + HEADS + head
            return raw_ref[rank, at : at + 1, :]

        last = difference(slice(PAIRS * TOKENS, PACKED))
        tail = jnp.zeros((TAIL, TOKENS), jnp.float32)
        pieces = []
        for pair in range(PAIRS):
            first, second = scale_of(2 * pair), scale_of(2 * pair + 1)
            square = difference(slice(pair * TOKENS, (pair + 1) * TOKENS))
            pieces.append(square * jnp.where(lower, first, second))
            tail = jnp.where(tail_row == pair, last[pair : pair + 1] * second, tail)
        pieces.append(tail)

        def put(ref, at):
            for n, piece in enumerate(pieces):
                to = pl.multiple_of(at + n * TOKENS, TAIL)
                ref[pl.ds(to, piece.shape[0]), :] = piece.astype(jnp.bfloat16)

        @pl.when(home_core == core)
        def _():
            put(grad_ref, slot * SLOT_ROWS)

        @pl.when(home_core != core)
        def _():
            put(sent_ref, slot * SLOT_ROWS)

        return carry

    lax.fori_loop(0, held, work, 0)


def spread_kernel(pair_ref, out_ref):
    out_ref[...] = jnp.broadcast_to(pair_ref[0] + pair_ref[1], out_ref.shape)


def gradient_kernel(table, grad_ref, sent_ref, qk_ref, q_out, k_out):
    me = lax.axis_index("section")
    core = lax.rem(me, 2)
    row, col = masks()
    held, layers = jnp.int32(0), [jnp.int32(0)] * SLOTS
    for layer in range(LAYERS):
        here = (table[1, layer] & (LAYERS - 1)) == me
        layers = [
            jnp.where(here & (held == slot), layer, had) for slot, had in enumerate(layers)
        ]
        held += here.astype(jnp.int32)
    for slot in range(SLOTS):

        @pl.when(slot < held)
        def _():
            direct = ((table[1, layers[slot]] >> 3) & 1) == core
            key = qk_ref[core, slot, :, HEADS * HEAD_WIDTH :]
            total = jnp.zeros((TOKENS, HEAD_WIDTH), jnp.float32)

            def rows(at, count):
                at = slot * SLOT_ROWS + at
                near = grad_ref[at : at + count, :].astype(jnp.float32)
                other = sent_ref[1 - core, at : at + count, :].astype(jnp.float32)
                return jnp.where(direct, near, other)

            tail = rows(PAIRS * TOKENS, TAIL)
            for head in range(HEADS):
                pair, over = head // 2, head % 2
                square = rows(pair * TOKENS, TOKENS)
                if over:
                    diagonal = jnp.where(row == col, tail[pair : pair + 1], 0.0)
                    grad = jnp.where(row < col, square, diagonal)
                else:
                    grad = jnp.where(col <= row, square, 0.0)
                grad = grad.astype(jnp.bfloat16)
                lanes = slice(head * HEAD_WIDTH, (head + 1) * HEAD_WIDTH)
                query = qk_ref[core, slot, :, lanes]
                q_out[0, slot, :, lanes] = dot(grad, key, 1 - over, 0).astype(jnp.bfloat16)
                total += dot(grad, query, over, 0)
            k_out[0, slot] = total.astype(jnp.bfloat16)

        @pl.when(slot >= held)
        def _():
            q_out[0, slot] = jnp.zeros(q_out.shape[2:], jnp.bfloat16)
            k_out[0, slot] = jnp.zeros(k_out.shape[2:], jnp.bfloat16)


def final_kernel(rows_ref, kl_ref, scale_ref):
    divergence = jnp.sum(rows_ref[0], axis=0, keepdims=True)
    kl_ref[...] = divergence[:, :LAYERS] / (STUDENT_HEADS * TOKENS)
    terms = jnp.sum(rows_ref[1], axis=0, keepdims=True)
    scale_ref[...] = jnp.concatenate(
        [terms[:, SCALE_LANE + LAYERS * h : SCALE_LANE + LAYERS * (h + 1)] for h in range(HEADS)], axis=0
    )


VMEM = pl.BlockSpec(memory_space=pltpu.VMEM)
ANY = pl.BlockSpec(memory_space=pl.ANY)
SMEM = pl.BlockSpec(memory_space=pltpu.SMEM)
SMALL = pltpu.CompilerParams(vmem_limit_bytes=16 * 2**20)


def kept(array):
    return pltpu.with_memory_space_constraint(array, pltpu.VMEM)


def cost(flops, moved):
    return pl.CostEstimate(flops=flops, bytes_accessed=moved, transcendentals=0)


def local(chips, groups, teacher_q, teacher_k, student_q, student_k, student_scale, pairing, placement):
    f32, bf16 = jnp.float32, jnp.bfloat16
    over_x = [[2 * x + core for x in range(chips)] for core in range(2)]
    of_chip = [[2 * x, 2 * x + 1] for x in range(chips)]
    members = len(groups[0])

    packed = pl.pallas_call(
        teacher_kernel,
        out_shape=jax.ShapeDtypeStruct((chips, PACKED, TOKENS), f32),
        in_specs=[SMEM, SMEM, VMEM, VMEM],
        out_specs=ANY,
        scratch_shapes=[
            pltpu.VMEM((PACKED, TOKENS), f32),
            pltpu.SemaphoreType.DMA((PAIRS,)),
        ],
        cost_estimate=cost(8 * 2 * TOKENS**3, 400_000),
        name="teacher",
    )(pairing, placement, teacher_q, teacher_k)
    arrived = lax.all_to_all(
        packed, "section", 0, 0, tiled=True, axis_index_groups=over_x
    )
    def of_both_cores(array):
        return lax.all_gather(array, "section", axis_index_groups=of_chip)

    chip_qk = kept(of_both_cores(jnp.concatenate((student_q[0], student_k[0]), axis=2)))
    at_once = 2 * SLOTS
    squares = pltpu.VMEM((at_once, PACKED, TOKENS), f32)
    raw, logp, table = pl.pallas_call(
        scores_kernel,
        out_shape=(squares, squares, pltpu.VMEM((2, LAYERS), jnp.int32)),
        in_specs=[SMEM, SMEM, SMEM, VMEM],
        out_specs=(VMEM, VMEM, VMEM),
        cost_estimate=cost(8 * 2 * TOKENS**3, 1_400_000),
        compiler_params=SMALL,
        name="scores",
    )(pairing, placement, student_scale.T, chip_qk)
    table = kept(table)

    work_on = (table, *map(kept, (arrived, raw, logp)))
    sums = pl.pallas_call(
        student_kernel,
        out_shape=pltpu.VMEM((1, TOKENS), f32),
        in_specs=[SMEM, VMEM, VMEM, VMEM],
        out_specs=VMEM,
        cost_estimate=cost(8 * 2 * TOKENS**3, 1_800_000),
        compiler_params=SMALL,
        name="student",
    )(*work_on)
    packed_grads = pltpu.VMEM((SENT, TOKENS), bf16)
    grads, sent = pl.pallas_call(
        slope_kernel,
        out_shape=(packed_grads, packed_grads),
        in_specs=[SMEM, VMEM, VMEM, VMEM],
        out_specs=(VMEM, VMEM),
        cost_estimate=cost(8 * 2 * TOKENS**3, 1_800_000),
        compiler_params=SMALL,
        name="slope",
    )(*work_on)

    sums = pl.pallas_call(
        spread_kernel,
        out_shape=jax.ShapeDtypeStruct((members, TOKENS), f32),
        in_specs=[VMEM],
        out_specs=VMEM,
        compiler_params=SMALL,
        name="spread",
    )(kept(of_both_cores(sums)))
    chip_sent = kept(of_both_cores(sent))
    rows = lax.all_to_all(
        sums.reshape(members, 1, TOKENS), AXES, 0, 0, tiled=True, axis_index_groups=groups
    )
    q_grad, k_grad = pl.pallas_call(
        gradient_kernel,
        out_shape=(
            jax.ShapeDtypeStruct(student_q.shape, bf16),
            jax.ShapeDtypeStruct(student_k.shape, bf16),
        ),
        in_specs=[SMEM, VMEM, VMEM, VMEM],
        out_specs=(VMEM, VMEM),
        cost_estimate=cost(16 * 2 * TOKENS**3, 900_000),
        compiler_params=SMALL,
        name="gradient",
    )(table, kept(grads), chip_sent, chip_qk)

    both = of_both_cores(rows.reshape(members, TOKENS))
    layer_kl, scale_grad = pl.pallas_call(
        final_kernel,
        out_shape=(
            jax.ShapeDtypeStruct((1, LAYERS), f32),
            jax.ShapeDtypeStruct((HEADS, LAYERS), f32),
        ),
        in_specs=[VMEM],
        out_specs=(VMEM, VMEM),
        compiler_params=SMALL,
        name="final",
    )(kept(both))
    return (q_grad, k_grad, layer_kl, scale_grad.T)


def reduction_groups(sections, heads, replicas):
    def flat(section, head, replica):
        return (section * heads + head) * replicas + replica

    chips = range(sections // 2)
    first = [
        [flat(2 * x, h, d) for x in chips for h in range(heads)] for d in range(replicas)
    ]
    second = [
        [flat(2 * x + 1, h, d) for x in chips for d in range(replicas)] for h in range(heads)
    ]
    return first + second


def solution(mesh):
    sections, heads, replicas = (mesh.shape[a] for a in AXES)
    return jax.shard_map(
        functools.partial(local, sections // 2, reduction_groups(sections, heads, replicas)),
        mesh=mesh,
        in_specs=(
            P("section", "dp", "head"),
            P("section", "dp", "head"),
            P("section", None, "dp", "head"),
            P("section", None, "dp", "head"),
            P(None, "head"),
            P(),
            P(),
        ),
        out_specs=(
            P("section", None, "dp", "head"),
            P("section", None, "dp", "head"),
            P("dp", None),
            P(None, "head"),
        ),
        check_vma=False,
    )
```

```python
import functools
import math

import jax
import jax.numpy as jnp
from jax import lax
from jax.experimental import pallas as pl
from jax.experimental.pallas import tpu as pltpu
from jax.sharding import PartitionSpec as P

STUDENT_HEADS = 32
HEAD_WIDTH = 128
TOKENS = 128
LAYERS = 8
SLOTS = 2
HEADS = 4
PACKED = HEADS // 2 * TOKENS + 8
SCALE_LANE = 32
PAIRS = HEADS // 2
TAIL = 16
SLOT_ROWS = PAIRS * TOKENS + TAIL
SENT = SLOTS * SLOT_ROWS
INVERSE = 1.0 / math.sqrt(HEAD_WIDTH)
HIDDEN = -1e30
SMALLEST = 1.2e-38
AXES = ("section", "head", "dp")


def dot(a, b, over_a, over_b):
    return lax.dot_general(
        a, b, (((over_a,), (over_b,)), ((), ())), preferred_element_type=jnp.float32
    )


def masks():
    row = lax.broadcasted_iota(jnp.int32, (TOKENS, TOKENS), 0)
    col = lax.broadcasted_iota(jnp.int32, (TOKENS, TOKENS), 1)
    return row, col


def log_softmax(scores, visible, axis):
    scores = jnp.where(visible, scores, HIDDEN)
    shifted = scores - jnp.max(scores, axis=axis, keepdims=True)
    return shifted - jnp.log(jnp.sum(jnp.exp(shifted), axis=axis, keepdims=True))


def softmax(scores, visible, axis):
    scores = jnp.where(visible, scores, HIDDEN)
    powers = jnp.exp(scores - jnp.max(scores, axis=axis, keepdims=True))
    return powers * (1.0 / jnp.sum(powers, axis=axis, keepdims=True))


def teacher_kernel(pairing, placement, q_ref, k_ref, out_ref, packed, sems):
    me = lax.axis_index("section")
    home = jnp.int32(0)
    for layer in range(LAYERS):
        home = jnp.where(pairing[layer] == me, placement[layer], home)
    chip = home // 2
    row, col = masks()
    key = k_ref[0]

    def target(head, turned):
        total = jnp.zeros((TOKENS, TOKENS), jnp.float32)
        for twin in (2 * head, 2 * head + 1):
            query = q_ref[0, :, twin * HEAD_WIDTH : (twin + 1) * HEAD_WIDTH]
            if turned:
                total += softmax(dot(key, query, 1, 1) * INVERSE, row <= col, 0)
            else:
                total += softmax(dot(query, key, 1, 1) * INVERSE, col <= row, 1)
        return total * 0.5

    packed[PAIRS * TOKENS :, :] = jnp.zeros((PACKED - PAIRS * TOKENS, TOKENS), jnp.float32)
    started = []
    for pair in range(PAIRS):
        plain = target(2 * pair, False)
        turned = target(2 * pair + 1, True)
        packed[pair * TOKENS : (pair + 1) * TOKENS, :] = jnp.where(col <= row, plain, turned)
        at = PAIRS * TOKENS + pair
        packed[at : at + 1, :] = jnp.sum(
            jnp.where(row == col, turned, 0.0), axis=0, keepdims=True
        )
        end = (pair + 1) * TOKENS if pair < PAIRS - 1 else PACKED
        rows = slice(pair * TOKENS, end)
        copy = pltpu.make_async_copy(
            packed.at[rows, :], out_ref.at[chip, rows, :], sems.at[pair]
        )
        copy.start()
        started.append(copy)
    for copy in started:
        copy.wait()


def arrival_core(source, chip):
    return (source ^ (source >> 2) ^ (chip >> 1)) & 1


def for_my_layers(pairing, placement, work):
    me = lax.axis_index("section")
    chip, core = me // 2, lax.rem(me, 2)

    def step(layer, carry):
        slots, rank = carry[:2], carry[2]
        home, source = placement[layer], pairing[layer]
        home_core = lax.rem(home, 2)
        here = home // 2 == chip
        mine = here & (arrival_core(source, chip) == core)
        slot = jnp.where(home_core == 0, slots[0], slots[1])

        @pl.when(mine)
        def _():
            work(layer, source // 2, home_core, slot, rank)

        return (
            slots[0] + (here & (home_core == 0)).astype(jnp.int32),
            slots[1] + (here & (home_core == 1)).astype(jnp.int32),
            rank + mine.astype(jnp.int32),
        )

    lax.fori_loop(0, LAYERS, step, (jnp.int32(0),) * 3)


def pack(ref, rank, pair, plain, turned):
    row, col = masks()
    ref[rank, pair * TOKENS : (pair + 1) * TOKENS, :] = jnp.where(col <= row, plain, turned)
    at = PAIRS * TOKENS + pair
    ref[rank, at : at + 1, :] = jnp.sum(
        jnp.where(row == col, turned, 0.0), axis=0, keepdims=True
    )


def scores_kernel(pairing, placement, scale_ref, qk_ref, raw_ref, logp_ref, table_ref):
    row, col = masks()
    at_row = lax.broadcasted_iota(jnp.int32, (2, LAYERS), 0)
    at_lane = lax.broadcasted_iota(jnp.int32, (2, LAYERS), 1)
    table = jnp.full((2, LAYERS), -1, jnp.int32)
    for layer in range(LAYERS):
        belongs = placement[layer] + LAYERS * pairing[layer]
        table = jnp.where((at_row == 1) & (at_lane == layer), belongs, table)
    table_ref[...] = table

    def work(layer, source_chip, home_core, slot, rank):
        code = layer + 8 * source_chip + 32 * home_core + 64 * slot
        table_ref[...] = jnp.where((at_row == 0) & (at_lane == rank), code, table_ref[...])
        key = qk_ref[home_core, slot, :, HEADS * HEAD_WIDTH :]

        def query(head):
            return qk_ref[home_core, slot, :, head * HEAD_WIDTH : (head + 1) * HEAD_WIDTH]

        tail_row = lax.broadcasted_iota(jnp.int32, (PACKED - PAIRS * TOKENS, TOKENS), 0)
        empty = jnp.zeros(tail_row.shape, jnp.float32)
        scales = empty
        for head in range(HEADS):
            scales = jnp.where(tail_row == HEADS + head, scale_ref[head, layer] * INVERSE, scales)
        raw_ref[rank, PAIRS * TOKENS :, :] = scales
        logp_ref[rank, PAIRS * TOKENS :, :] = empty
        for pair in range(PAIRS):
            plain = dot(query(2 * pair), key, 1, 1) * INVERSE
            turned = dot(key, query(2 * pair + 1), 1, 1) * INVERSE
            pack(raw_ref, rank, pair, plain, turned)
            plain = log_softmax(scale_ref[2 * pair, layer] * plain, col <= row, 1)
            turned = log_softmax(scale_ref[2 * pair + 1, layer] * turned, row <= col, 0)
            pack(logp_ref, rank, pair, plain, turned)

    for_my_layers(pairing, placement, work)


def student_kernel(table, arrived_ref, raw_ref, logp_ref, sums_ref, grad_ref, sent_ref):
    core = lax.rem(lax.axis_index("section"), 2)
    row, col = masks()
    lower = col <= row
    place = lax.broadcasted_iota(jnp.int32, (8, TOKENS), 0)
    lane = lax.broadcasted_iota(jnp.int32, (8, TOKENS), 1)
    tail_row = lax.broadcasted_iota(jnp.int32, (TAIL, TOKENS), 0)
    sums_ref[...] = jnp.zeros_like(sums_ref)

    held = jnp.int32(0)
    for rank in range(2 * SLOTS):
        held += (table[0, rank] >= 0).astype(jnp.int32)

    def work(rank, carry):
        code = table[0, rank]
        layer, source_chip = code & 7, (code >> 3) & 3
        home_core, slot = (code >> 5) & 1, code >> 6

        def terms(rows):
            target = arrived_ref[source_chip, rows, :]
            target_logp = jnp.log(jnp.maximum(target, SMALLEST))
            student_logp = logp_ref[rank, rows, :]
            difference = jnp.exp(student_logp) - target
            return (
                jnp.sum(target * (target_logp - student_logp), axis=0, keepdims=True),
                difference,
                difference * raw_ref[rank, rows, :],
            )

        def scale_of(head):
            at = PAIRS * TOKENS + HEADS + head
            return raw_ref[rank, at : at + 1, :]

        last, last_difference, last_moved = terms(slice(PAIRS * TOKENS, PACKED))
        found = jnp.zeros((8, TOKENS), jnp.float32)
        divergence = last
        tail = jnp.zeros((TAIL, TOKENS), jnp.float32)
        pieces = []
        for pair in range(PAIRS):
            one, difference, moved = terms(slice(pair * TOKENS, (pair + 1) * TOKENS))
            divergence += one
            first = scale_of(2 * pair)
            second = scale_of(2 * pair + 1)
            pieces.append(difference * jnp.where(lower, first, second))
            tail = jnp.where(tail_row == pair, last_difference[pair : pair + 1] * second, tail)
            of_first = jnp.sum(jnp.where(lower, moved, 0.0), axis=0, keepdims=True)
            of_second = jnp.sum(jnp.where(lower, 0.0, moved), axis=0, keepdims=True)
            of_second += last_moved[pair : pair + 1]
            found = jnp.where(place == 1 + 2 * pair, of_first, found)
            found = jnp.where(place == 2 + 2 * pair, of_second, found)
        found = jnp.where(place == 0, divergence, found)
        found = jnp.sum(found, axis=1, keepdims=True)
        goes_to = jnp.where(place == 0, layer, SCALE_LANE + LAYERS * (place - 1) + layer)
        found = jnp.where((lane == goes_to) & (place <= HEADS), found, 0.0)
        sums_ref[...] += jnp.sum(found, axis=0, keepdims=True)
        pieces.append(tail)

        def put(ref, at):
            for n, piece in enumerate(pieces):
                to = pl.multiple_of(at + n * TOKENS, TAIL)
                ref[pl.ds(to, piece.shape[0]), :] = piece.astype(jnp.bfloat16)

        @pl.when(home_core == core)
        def _():
            put(grad_ref, slot * SLOT_ROWS)

        @pl.when(home_core != core)
        def _():
            put(sent_ref, slot * SLOT_ROWS)

        return carry

    lax.fori_loop(0, held, work, 0)


def spread_kernel(pair_ref, out_ref):
    out_ref[...] = jnp.broadcast_to(pair_ref[0] + pair_ref[1], out_ref.shape)


def gradient_kernel(table, grad_ref, sent_ref, qk_ref, q_out, k_out):
    me = lax.axis_index("section")
    core = lax.rem(me, 2)
    row, col = masks()
    held, layers = jnp.int32(0), [jnp.int32(0)] * SLOTS
    for layer in range(LAYERS):
        here = (table[1, layer] & (LAYERS - 1)) == me
        layers = [
            jnp.where(here & (held == slot), layer, had) for slot, had in enumerate(layers)
        ]
        held += here.astype(jnp.int32)
    for slot in range(SLOTS):

        @pl.when(slot < held)
        def _():
            direct = arrival_core(table[1, layers[slot]] >> 3, me // 2) == core
            key = qk_ref[core, slot, :, HEADS * HEAD_WIDTH :]
            total = jnp.zeros((TOKENS, HEAD_WIDTH), jnp.float32)

            def rows(at, count):
                at = slot * SLOT_ROWS + at
                near = grad_ref[at : at + count, :].astype(jnp.float32)
                other = sent_ref[1 - core, at : at + count, :].astype(jnp.float32)
                return jnp.where(direct, near, other)

            tail = rows(PAIRS * TOKENS, TAIL)
            for head in range(HEADS):
                pair, over = head // 2, head % 2
                square = rows(pair * TOKENS, TOKENS)
                if over:
                    diagonal = jnp.where(row == col, tail[pair : pair + 1], 0.0)
                    grad = jnp.where(row < col, square, diagonal)
                else:
                    grad = jnp.where(col <= row, square, 0.0)
                grad = grad.astype(jnp.bfloat16)
                lanes = slice(head * HEAD_WIDTH, (head + 1) * HEAD_WIDTH)
                query = qk_ref[core, slot, :, lanes]
                q_out[0, slot, :, lanes] = dot(grad, key, 1 - over, 0).astype(jnp.bfloat16)
                total += dot(grad, query, over, 0)
            k_out[0, slot] = total.astype(jnp.bfloat16)

        @pl.when(slot >= held)
        def _():
            q_out[0, slot] = jnp.zeros(q_out.shape[2:], jnp.bfloat16)
            k_out[0, slot] = jnp.zeros(k_out.shape[2:], jnp.bfloat16)


def final_kernel(rows_ref, kl_ref, scale_ref):
    divergence = jnp.sum(rows_ref[0], axis=0, keepdims=True)
    kl_ref[...] = divergence[:, :LAYERS] / (STUDENT_HEADS * TOKENS)
    terms = jnp.sum(rows_ref[1], axis=0, keepdims=True)
    scale_ref[...] = jnp.concatenate(
        [terms[:, SCALE_LANE + LAYERS * h : SCALE_LANE + LAYERS * (h + 1)] for h in range(HEADS)], axis=0
    )


VMEM = pl.BlockSpec(memory_space=pltpu.VMEM)
ANY = pl.BlockSpec(memory_space=pl.ANY)
SMEM = pl.BlockSpec(memory_space=pltpu.SMEM)
SMALL = pltpu.CompilerParams(vmem_limit_bytes=16 * 2**20)


def kept(array):
    return pltpu.with_memory_space_constraint(array, pltpu.VMEM)


def cost(flops, moved):
    return pl.CostEstimate(flops=flops, bytes_accessed=moved, transcendentals=0)


def local(chips, groups, teacher_q, teacher_k, student_q, student_k, student_scale, pairing, placement):
    f32, bf16 = jnp.float32, jnp.bfloat16
    over_x = [[2 * x + (core ^ (x // 2 & 1)) for x in range(chips)] for core in range(2)]
    of_chip = [[2 * x, 2 * x + 1] for x in range(chips)]
    members = len(groups[0])

    packed = pl.pallas_call(
        teacher_kernel,
        out_shape=jax.ShapeDtypeStruct((chips, PACKED, TOKENS), f32),
        in_specs=[SMEM, SMEM, VMEM, VMEM],
        out_specs=ANY,
        scratch_shapes=[
            pltpu.VMEM((PACKED, TOKENS), f32),
            pltpu.SemaphoreType.DMA((PAIRS,)),
        ],
        cost_estimate=cost(8 * 2 * TOKENS**3, 400_000),
        name="teacher",
    )(pairing, placement, teacher_q, teacher_k)
    arrived = lax.all_to_all(
        packed, "section", 0, 0, tiled=True, axis_index_groups=over_x
    )
    def of_both_cores(array):
        return lax.all_gather(array, "section", axis_index_groups=of_chip)

    chip_qk = kept(of_both_cores(jnp.concatenate((student_q[0], student_k[0]), axis=2)))
    at_once = 2 * SLOTS
    squares = pltpu.VMEM((at_once, PACKED, TOKENS), f32)
    raw, logp, table = pl.pallas_call(
        scores_kernel,
        out_shape=(squares, squares, pltpu.VMEM((2, LAYERS), jnp.int32)),
        in_specs=[SMEM, SMEM, SMEM, VMEM],
        out_specs=(VMEM, VMEM, VMEM),
        cost_estimate=cost(8 * 2 * TOKENS**3, 1_400_000),
        compiler_params=SMALL,
        name="scores",
    )(pairing, placement, student_scale.T, chip_qk)
    table = kept(table)

    sums, grads, sent = pl.pallas_call(
        student_kernel,
        out_shape=(
            pltpu.VMEM((1, TOKENS), f32),
            pltpu.VMEM((SENT, TOKENS), bf16),
            pltpu.VMEM((SENT, TOKENS), bf16),
        ),
        in_specs=[SMEM, VMEM, VMEM, VMEM],
        out_specs=(VMEM, VMEM, VMEM),
        cost_estimate=cost(8 * 2 * TOKENS**3, 1_800_000),
        compiler_params=SMALL,
        name="student",
    )(table, *map(kept, (arrived, raw, logp)))

    sums = pl.pallas_call(
        spread_kernel,
        out_shape=jax.ShapeDtypeStruct((members, TOKENS), f32),
        in_specs=[VMEM],
        out_specs=VMEM,
        compiler_params=SMALL,
        name="spread",
    )(kept(of_both_cores(sums)))
    chip_sent = kept(of_both_cores(sent))
    rows = lax.all_to_all(
        sums.reshape(members, 1, TOKENS), AXES, 0, 0, tiled=True, axis_index_groups=groups
    )
    q_grad, k_grad = pl.pallas_call(
        gradient_kernel,
        out_shape=(
            jax.ShapeDtypeStruct(student_q.shape, bf16),
            jax.ShapeDtypeStruct(student_k.shape, bf16),
        ),
        in_specs=[SMEM, VMEM, VMEM, VMEM],
        out_specs=(VMEM, VMEM),
        cost_estimate=cost(16 * 2 * TOKENS**3, 900_000),
        compiler_params=SMALL,
        name="gradient",
    )(table, kept(grads), chip_sent, chip_qk)

    both = of_both_cores(rows.reshape(members, TOKENS))
    layer_kl, scale_grad = pl.pallas_call(
        final_kernel,
        out_shape=(
            jax.ShapeDtypeStruct((1, LAYERS), f32),
            jax.ShapeDtypeStruct((HEADS, LAYERS), f32),
        ),
        in_specs=[VMEM],
        out_specs=(VMEM, VMEM),
        compiler_params=SMALL,
        name="final",
    )(kept(both))
    return (q_grad, k_grad, layer_kl, scale_grad.T)


def reduction_groups(sections, heads, replicas):
    def flat(section, head, replica):
        return (section * heads + head) * replicas + replica

    chips = range(sections // 2)
    first = [
        [flat(2 * x, h, d) for x in chips for h in range(heads)] for d in range(replicas)
    ]
    second = [
        [flat(2 * x + 1, h, d) for x in chips for d in range(replicas)] for h in range(heads)
    ]
    return first + second


def solution(mesh):
    sections, heads, replicas = (mesh.shape[a] for a in AXES)
    return jax.shard_map(
        functools.partial(local, sections // 2, reduction_groups(sections, heads, replicas)),
        mesh=mesh,
        in_specs=(
            P("section", "dp", "head"),
            P("section", "dp", "head"),
            P("section", None, "dp", "head"),
            P("section", None, "dp", "head"),
            P(None, "head"),
            P(),
            P(),
        ),
        out_specs=(
            P("section", None, "dp", "head"),
            P("section", None, "dp", "head"),
            P("dp", None),
            P(None, "head"),
        ),
        check_vma=False,
    )
```

```python
import functools
import math

import jax
import jax.numpy as jnp
from jax import lax
from jax.experimental import pallas as pl
from jax.experimental.pallas import tpu as pltpu
from jax.sharding import PartitionSpec as P

STUDENT_HEADS = 32
HEAD_WIDTH = 128
TOKENS = 128
LAYERS = 8
SLOTS = 2
HEADS = 4
PACKED = HEADS // 2 * TOKENS + 8
SCALE_LANE = 32
PAIRS = HEADS // 2
TAIL = 16
SLOT_ROWS = PAIRS * TOKENS + TAIL
SENT = SLOTS * SLOT_ROWS
INVERSE = 1.0 / math.sqrt(HEAD_WIDTH)
HIDDEN = -1e30
SMALLEST = 1.2e-38
AXES = ("section", "head", "dp")


def dot(a, b, over_a, over_b):
    return lax.dot_general(
        a, b, (((over_a,), (over_b,)), ((), ())), preferred_element_type=jnp.float32
    )


def masks():
    row = lax.broadcasted_iota(jnp.int32, (TOKENS, TOKENS), 0)
    col = lax.broadcasted_iota(jnp.int32, (TOKENS, TOKENS), 1)
    return row, col


def log_softmax(scores, visible, axis):
    scores = jnp.where(visible, scores, HIDDEN)
    shifted = scores - jnp.max(scores, axis=axis, keepdims=True)
    return shifted - jnp.log(jnp.sum(jnp.exp(shifted), axis=axis, keepdims=True))


def softmax(scores, visible, axis):
    scores = jnp.where(visible, scores, HIDDEN)
    powers = jnp.exp(scores - jnp.max(scores, axis=axis, keepdims=True))
    return powers * (1.0 / jnp.sum(powers, axis=axis, keepdims=True))


def teacher_kernel(pairing, placement, q_ref, k_ref, out_ref, packed, sems):
    me = lax.axis_index("section")
    home = jnp.int32(0)
    for layer in range(LAYERS):
        home = jnp.where(pairing[layer] == me, placement[layer], home)
    chip = home // 2
    row, col = masks()
    key = k_ref[0]

    def target(head, turned):
        total = jnp.zeros((TOKENS, TOKENS), jnp.float32)
        for twin in (2 * head, 2 * head + 1):
            query = q_ref[0, :, twin * HEAD_WIDTH : (twin + 1) * HEAD_WIDTH]
            if turned:
                total += softmax(dot(key, query, 1, 1) * INVERSE, row <= col, 0)
            else:
                total += softmax(dot(query, key, 1, 1) * INVERSE, col <= row, 1)
        return total * 0.5

    packed[PAIRS * TOKENS :, :] = jnp.zeros((PACKED - PAIRS * TOKENS, TOKENS), jnp.float32)
    started = []
    for pair in range(PAIRS):
        plain = target(2 * pair, False)
        turned = target(2 * pair + 1, True)
        packed[pair * TOKENS : (pair + 1) * TOKENS, :] = jnp.where(col <= row, plain, turned)
        at = PAIRS * TOKENS + pair
        packed[at : at + 1, :] = jnp.sum(
            jnp.where(row == col, turned, 0.0), axis=0, keepdims=True
        )
        end = (pair + 1) * TOKENS if pair < PAIRS - 1 else PACKED
        rows = slice(pair * TOKENS, end)
        copy = pltpu.make_async_copy(
            packed.at[rows, :], out_ref.at[chip, rows, :], sems.at[pair]
        )
        copy.start()
        started.append(copy)
    for copy in started:
        copy.wait()


def for_my_layers(pairing, placement, work):
    me = lax.axis_index("section")
    chip, core = me // 2, lax.rem(me, 2)

    def step(layer, carry):
        slots, rank = carry[:2], carry[2]
        home, source = placement[layer], pairing[layer]
        home_core = lax.rem(home, 2)
        here = home // 2 == chip
        mine = here & (lax.rem(source, 2) == core)
        slot = jnp.where(home_core == 0, slots[0], slots[1])

        @pl.when(mine)
        def _():
            work(layer, source // 2, home_core, slot, rank)

        return (
            slots[0] + (here & (home_core == 0)).astype(jnp.int32),
            slots[1] + (here & (home_core == 1)).astype(jnp.int32),
            rank + mine.astype(jnp.int32),
        )

    lax.fori_loop(0, LAYERS, step, (jnp.int32(0),) * 3)


def pack(ref, rank, pair, plain, turned):
    row, col = masks()
    ref[rank, pair * TOKENS : (pair + 1) * TOKENS, :] = jnp.where(col <= row, plain, turned)
    at = PAIRS * TOKENS + pair
    ref[rank, at : at + 1, :] = jnp.sum(
        jnp.where(row == col, turned, 0.0), axis=0, keepdims=True
    )


def scores_kernel(pairing, placement, scale_ref, qk_ref, raw_ref, logp_ref, table_ref):
    row, col = masks()
    at_row = lax.broadcasted_iota(jnp.int32, (2, LAYERS), 0)
    at_lane = lax.broadcasted_iota(jnp.int32, (2, LAYERS), 1)
    table = jnp.full((2, LAYERS), -1, jnp.int32)
    for layer in range(LAYERS):
        belongs = placement[layer] + LAYERS * pairing[layer]
        table = jnp.where((at_row == 1) & (at_lane == layer), belongs, table)
    table_ref[...] = table

    def work(layer, source_chip, home_core, slot, rank):
        code = layer + 8 * source_chip + 32 * home_core + 64 * slot
        table_ref[...] = jnp.where((at_row == 0) & (at_lane == rank), code, table_ref[...])
        key = qk_ref[home_core, slot, :, HEADS * HEAD_WIDTH :]

        def query(head):
            return qk_ref[home_core, slot, :, head * HEAD_WIDTH : (head + 1) * HEAD_WIDTH]

        tail_row = lax.broadcasted_iota(jnp.int32, (PACKED - PAIRS * TOKENS, TOKENS), 0)
        empty = jnp.zeros(tail_row.shape, jnp.float32)
        scales = empty
        for head in range(HEADS):
            scales = jnp.where(tail_row == HEADS + head, scale_ref[head, layer] * INVERSE, scales)
        raw_ref[rank, PAIRS * TOKENS :, :] = scales
        logp_ref[rank, PAIRS * TOKENS :, :] = empty
        for pair in range(PAIRS):
            plain = dot(query(2 * pair), key, 1, 1) * INVERSE
            turned = dot(key, query(2 * pair + 1), 1, 1) * INVERSE
            pack(raw_ref, rank, pair, plain, turned)
            plain = log_softmax(scale_ref[2 * pair, layer] * plain, col <= row, 1)
            turned = log_softmax(scale_ref[2 * pair + 1, layer] * turned, row <= col, 0)
            pack(logp_ref, rank, pair, plain, turned)

    for_my_layers(pairing, placement, work)


def student_kernel(table, arrived_ref, raw_ref, logp_ref, sums_ref, grad_ref, sent_ref):
    core = lax.rem(lax.axis_index("section"), 2)
    row, col = masks()
    lower = col <= row
    place = lax.broadcasted_iota(jnp.int32, (8, TOKENS), 0)
    lane = lax.broadcasted_iota(jnp.int32, (8, TOKENS), 1)
    tail_row = lax.broadcasted_iota(jnp.int32, (TAIL, TOKENS), 0)
    sums_ref[...] = jnp.zeros_like(sums_ref)

    held = jnp.int32(0)
    for rank in range(2 * SLOTS):
        held += (table[0, rank] >= 0).astype(jnp.int32)

    def work(rank, carry):
        code = table[0, rank]
        layer, source_chip = code & 7, (code >> 3) & 3
        home_core, slot = (code >> 5) & 1, code >> 6

        def terms(rows):
            target = arrived_ref[source_chip, rows, :]
            target_logp = jnp.log(jnp.maximum(target, SMALLEST))
            student_logp = logp_ref[rank, rows, :]
            difference = jnp.exp(student_logp) - target
            return (
                jnp.sum(target * (target_logp - student_logp), axis=0, keepdims=True),
                difference,
                difference * raw_ref[rank, rows, :],
            )

        def scale_of(head):
            at = PAIRS * TOKENS + HEADS + head
            return raw_ref[rank, at : at + 1, :]

        last, last_difference, last_moved = terms(slice(PAIRS * TOKENS, PACKED))
        found = jnp.zeros((8, TOKENS), jnp.float32)
        divergence = last
        tail = jnp.zeros((TAIL, TOKENS), jnp.float32)
        pieces = []
        for pair in range(PAIRS):
            one, difference, moved = terms(slice(pair * TOKENS, (pair + 1) * TOKENS))
            divergence += one
            first = scale_of(2 * pair)
            second = scale_of(2 * pair + 1)
            pieces.append(difference * jnp.where(lower, first, second))
            tail = jnp.where(tail_row == pair, last_difference[pair : pair + 1] * second, tail)
            of_first = jnp.sum(jnp.where(lower, moved, 0.0), axis=0, keepdims=True)
            of_second = jnp.sum(jnp.where(lower, 0.0, moved), axis=0, keepdims=True)
            of_second += last_moved[pair : pair + 1]
            found = jnp.where(place == 1 + 2 * pair, of_first, found)
            found = jnp.where(place == 2 + 2 * pair, of_second, found)
        found = jnp.where(place == 0, divergence, found)
        found = jnp.sum(found, axis=1, keepdims=True)
        goes_to = jnp.where(place == 0, layer, SCALE_LANE + LAYERS * (place - 1) + layer)
        found = jnp.where((lane == goes_to) & (place <= HEADS), found, 0.0)
        sums_ref[...] += jnp.sum(found, axis=0, keepdims=True)
        pieces.append(tail)

        def put(ref, at):
            for n, piece in enumerate(pieces):
                to = pl.multiple_of(at + n * TOKENS, TAIL)
                ref[pl.ds(to, piece.shape[0]), :] = piece.astype(jnp.bfloat16)

        @pl.when(home_core == core)
        def _():
            put(grad_ref, slot * SLOT_ROWS)

        @pl.when(home_core != core)
        def _():
            put(sent_ref, slot * SLOT_ROWS)

        return carry

    lax.fori_loop(0, held, work, 0)


def spread_kernel(pair_ref, out_ref):
    out_ref[...] = jnp.broadcast_to(pair_ref[0] + pair_ref[1], out_ref.shape)


def gradient_kernel(table, grad_ref, sent_ref, qk_ref, q_out, k_out):
    me = lax.axis_index("section")
    core = lax.rem(me, 2)
    row, col = masks()
    held, layers = jnp.int32(0), [jnp.int32(0)] * SLOTS
    for layer in range(LAYERS):
        here = (table[1, layer] & (LAYERS - 1)) == me
        layers = [
            jnp.where(here & (held == slot), layer, had) for slot, had in enumerate(layers)
        ]
        held += here.astype(jnp.int32)
    for slot in range(SLOTS):

        @pl.when(slot < held)
        def _():
            direct = ((table[1, layers[slot]] >> 3) & 1) == core
            key = qk_ref[core, slot, :, HEADS * HEAD_WIDTH :]
            total = jnp.zeros((TOKENS, HEAD_WIDTH), jnp.float32)

            def rows(at, count):
                at = slot * SLOT_ROWS + at
                near = grad_ref[at : at + count, :].astype(jnp.float32)
                other = sent_ref[1 - core, at : at + count, :].astype(jnp.float32)
                return jnp.where(direct, near, other)

            tail = rows(PAIRS * TOKENS, TAIL)
            for head in range(HEADS):
                pair, over = head // 2, head % 2
                square = rows(pair * TOKENS, TOKENS)
                if over:
                    diagonal = jnp.where(row == col, tail[pair : pair + 1], 0.0)
                    grad = jnp.where(row < col, square, diagonal)
                else:
                    grad = jnp.where(col <= row, square, 0.0)
                grad = grad.astype(jnp.bfloat16)
                lanes = slice(head * HEAD_WIDTH, (head + 1) * HEAD_WIDTH)
                query = qk_ref[core, slot, :, lanes]
                q_out[0, slot, :, lanes] = dot(grad, key, 1 - over, 0).astype(jnp.bfloat16)
                total += dot(grad, query, over, 0)
            k_out[0, slot] = total.astype(jnp.bfloat16)

        @pl.when(slot >= held)
        def _():
            q_out[0, slot] = jnp.zeros(q_out.shape[2:], jnp.bfloat16)
            k_out[0, slot] = jnp.zeros(k_out.shape[2:], jnp.bfloat16)


def final_kernel(rows_ref, kl_ref, scale_ref):
    divergence = jnp.sum(rows_ref[1], axis=0, keepdims=True)
    kl_ref[...] = divergence[:, :LAYERS] / (STUDENT_HEADS * TOKENS)
    terms = jnp.sum(rows_ref[0], axis=0, keepdims=True)
    scale_ref[...] = jnp.concatenate(
        [terms[:, SCALE_LANE + LAYERS * h : SCALE_LANE + LAYERS * (h + 1)] for h in range(HEADS)], axis=0
    )


VMEM = pl.BlockSpec(memory_space=pltpu.VMEM)
ANY = pl.BlockSpec(memory_space=pl.ANY)
SMEM = pl.BlockSpec(memory_space=pltpu.SMEM)
SMALL = pltpu.CompilerParams(vmem_limit_bytes=16 * 2**20)


def kept(array):
    return pltpu.with_memory_space_constraint(array, pltpu.VMEM)


def cost(flops, moved):
    return pl.CostEstimate(flops=flops, bytes_accessed=moved, transcendentals=0)


def local(chips, groups, teacher_q, teacher_k, student_q, student_k, student_scale, pairing, placement):
    f32, bf16 = jnp.float32, jnp.bfloat16
    over_x = [[2 * x + core for x in range(chips)] for core in range(2)]
    of_chip = [[2 * x, 2 * x + 1] for x in range(chips)]
    members = len(groups[0])

    packed = pl.pallas_call(
        teacher_kernel,
        out_shape=jax.ShapeDtypeStruct((chips, PACKED, TOKENS), f32),
        in_specs=[SMEM, SMEM, VMEM, VMEM],
        out_specs=ANY,
        scratch_shapes=[
            pltpu.VMEM((PACKED, TOKENS), f32),
            pltpu.SemaphoreType.DMA((PAIRS,)),
        ],
        cost_estimate=cost(8 * 2 * TOKENS**3, 400_000),
        name="teacher",
    )(pairing, placement, teacher_q, teacher_k)
    arrived = lax.all_to_all(
        packed, "section", 0, 0, tiled=True, axis_index_groups=over_x
    )
    def of_both_cores(array):
        return lax.all_gather(array, "section", axis_index_groups=of_chip)

    chip_qk = kept(of_both_cores(jnp.concatenate((student_q[0], student_k[0]), axis=2)))
    at_once = 2 * SLOTS
    squares = pltpu.VMEM((at_once, PACKED, TOKENS), f32)
    raw, logp, table = pl.pallas_call(
        scores_kernel,
        out_shape=(squares, squares, pltpu.VMEM((2, LAYERS), jnp.int32)),
        in_specs=[SMEM, SMEM, SMEM, VMEM],
        out_specs=(VMEM, VMEM, VMEM),
        cost_estimate=cost(8 * 2 * TOKENS**3, 1_400_000),
        compiler_params=SMALL,
        name="scores",
    )(pairing, placement, student_scale.T, chip_qk)
    table = kept(table)

    sums, grads, sent = pl.pallas_call(
        student_kernel,
        out_shape=(
            pltpu.VMEM((1, TOKENS), f32),
            pltpu.VMEM((SENT, TOKENS), bf16),
            pltpu.VMEM((SENT, TOKENS), bf16),
        ),
        in_specs=[SMEM, VMEM, VMEM, VMEM],
        out_specs=(VMEM, VMEM, VMEM),
        cost_estimate=cost(8 * 2 * TOKENS**3, 1_800_000),
        compiler_params=SMALL,
        name="student",
    )(table, *map(kept, (arrived, raw, logp)))

    sums = pl.pallas_call(
        spread_kernel,
        out_shape=jax.ShapeDtypeStruct((members, TOKENS), f32),
        in_specs=[VMEM],
        out_specs=VMEM,
        compiler_params=SMALL,
        name="spread",
    )(kept(of_both_cores(sums)))
    chip_sent = kept(of_both_cores(sent))
    rows = lax.all_to_all(
        sums.reshape(members, 1, TOKENS), AXES, 0, 0, tiled=True, axis_index_groups=groups
    )
    q_grad, k_grad = pl.pallas_call(
        gradient_kernel,
        out_shape=(
            jax.ShapeDtypeStruct(student_q.shape, bf16),
            jax.ShapeDtypeStruct(student_k.shape, bf16),
        ),
        in_specs=[SMEM, VMEM, VMEM, VMEM],
        out_specs=(VMEM, VMEM),
        cost_estimate=cost(16 * 2 * TOKENS**3, 900_000),
        compiler_params=SMALL,
        name="gradient",
    )(table, kept(grads), chip_sent, chip_qk)

    both = of_both_cores(rows.reshape(members, TOKENS))
    layer_kl, scale_grad = pl.pallas_call(
        final_kernel,
        out_shape=(
            jax.ShapeDtypeStruct((1, LAYERS), f32),
            jax.ShapeDtypeStruct((HEADS, LAYERS), f32),
        ),
        in_specs=[VMEM],
        out_specs=(VMEM, VMEM),
        compiler_params=SMALL,
        name="final",
    )(kept(both))
    return (q_grad, k_grad, layer_kl, scale_grad.T)


def reduction_groups(sections, heads, replicas):
    def flat(section, head, replica):
        return (section * heads + head) * replicas + replica

    chips = range(sections // 2)
    first = [
        [flat(2 * x + 1, h, d) for x in chips for h in range(heads)] for d in range(replicas)
    ]
    second = [
        [flat(2 * x, h, d) for x in chips for d in range(replicas)] for h in range(heads)
    ]
    return first + second


def solution(mesh):
    sections, heads, replicas = (mesh.shape[a] for a in AXES)
    return jax.shard_map(
        functools.partial(local, sections // 2, reduction_groups(sections, heads, replicas)),
        mesh=mesh,
        in_specs=(
            P("section", "dp", "head"),
            P("section", "dp", "head"),
            P("section", None, "dp", "head"),
            P("section", None, "dp", "head"),
            P(None, "head"),
            P(),
            P(),
        ),
        out_specs=(
            P("section", None, "dp", "head"),
            P("section", None, "dp", "head"),
            P("dp", None),
            P(None, "head"),
        ),
        check_vma=False,
    )
```

```python
import functools
import math

import jax
import jax.numpy as jnp
from jax import lax
from jax.experimental import pallas as pl
from jax.experimental.pallas import tpu as pltpu
from jax.sharding import PartitionSpec as P

STUDENT_HEADS = 32
HEAD_WIDTH = 128
TOKENS = 128
LAYERS = 8
SLOTS = 2
HEADS = 4
PACKED = HEADS // 2 * TOKENS + 8
SCALE_LANE = 32
PAIRS = HEADS // 2
TAIL = 16
SLOT_ROWS = PAIRS * TOKENS + TAIL
SENT = SLOTS * SLOT_ROWS
INVERSE = 1.0 / math.sqrt(HEAD_WIDTH)
HIDDEN = -1e30
SMALLEST = 1.2e-38
AXES = ("section", "head", "dp")


def dot(a, b, over_a, over_b):
    return lax.dot_general(
        a, b, (((over_a,), (over_b,)), ((), ())), preferred_element_type=jnp.float32
    )


def masks():
    row = lax.broadcasted_iota(jnp.int32, (TOKENS, TOKENS), 0)
    col = lax.broadcasted_iota(jnp.int32, (TOKENS, TOKENS), 1)
    return row, col


def log_softmax(scores, visible, axis):
    scores = jnp.where(visible, scores, HIDDEN)
    shifted = scores - jnp.max(scores, axis=axis, keepdims=True)
    return shifted - jnp.log(jnp.sum(jnp.exp(shifted), axis=axis, keepdims=True))


def softmax(scores, visible, axis):
    scores = jnp.where(visible, scores, HIDDEN)
    powers = jnp.exp(scores - jnp.max(scores, axis=axis, keepdims=True))
    return powers * (1.0 / jnp.sum(powers, axis=axis, keepdims=True))


def teacher_kernel(pairing, placement, q_ref, k_ref, out_ref, packed, sems):
    me = lax.axis_index("section")
    home = jnp.int32(0)
    for layer in range(LAYERS):
        home = jnp.where(pairing[layer] == me, placement[layer], home)
    chip = home // 2
    row, col = masks()
    key = k_ref[0]

    def target(head, turned):
        total = jnp.zeros((TOKENS, TOKENS), jnp.float32)
        for twin in (2 * head, 2 * head + 1):
            query = q_ref[0, :, twin * HEAD_WIDTH : (twin + 1) * HEAD_WIDTH]
            if turned:
                total += softmax(dot(key, query, 1, 1) * INVERSE, row <= col, 0)
            else:
                total += softmax(dot(query, key, 1, 1) * INVERSE, col <= row, 1)
        return total * 0.5

    packed[PAIRS * TOKENS :, :] = jnp.zeros((PACKED - PAIRS * TOKENS, TOKENS), jnp.float32)
    started = []
    for pair in range(PAIRS):
        plain = target(2 * pair, False)
        turned = target(2 * pair + 1, True)
        packed[pair * TOKENS : (pair + 1) * TOKENS, :] = jnp.where(col <= row, plain, turned)
        at = PAIRS * TOKENS + pair
        packed[at : at + 1, :] = jnp.sum(
            jnp.where(row == col, turned, 0.0), axis=0, keepdims=True
        )
        end = (pair + 1) * TOKENS if pair < PAIRS - 1 else PACKED
        rows = slice(pair * TOKENS, end)
        copy = pltpu.make_async_copy(
            packed.at[rows, :], out_ref.at[chip, rows, :], sems.at[pair]
        )
        copy.start()
        started.append(copy)
    for copy in started:
        copy.wait()


def for_my_layers(pairing, placement, work):
    me = lax.axis_index("section")
    chip, core = me // 2, lax.rem(me, 2)

    def step(layer, carry):
        slots, rank = carry[:2], carry[2]
        home, source = placement[layer], pairing[layer]
        home_core = lax.rem(home, 2)
        here = home // 2 == chip
        mine = here & (lax.rem(source, 2) == core)
        slot = jnp.where(home_core == 0, slots[0], slots[1])

        @pl.when(mine)
        def _():
            work(layer, source // 2, home_core, slot, rank)

        return (
            slots[0] + (here & (home_core == 0)).astype(jnp.int32),
            slots[1] + (here & (home_core == 1)).astype(jnp.int32),
            rank + mine.astype(jnp.int32),
        )

    lax.fori_loop(0, LAYERS, step, (jnp.int32(0),) * 3)


def pack(ref, rank, pair, plain, turned):
    row, col = masks()
    ref[rank, pair * TOKENS : (pair + 1) * TOKENS, :] = jnp.where(col <= row, plain, turned)
    at = PAIRS * TOKENS + pair
    ref[rank, at : at + 1, :] = jnp.sum(
        jnp.where(row == col, turned, 0.0), axis=0, keepdims=True
    )


def scores_kernel(pairing, placement, scale_ref, qk_ref, raw_ref, logp_ref, table_ref):
    row, col = masks()
    at_row = lax.broadcasted_iota(jnp.int32, (2, LAYERS), 0)
    at_lane = lax.broadcasted_iota(jnp.int32, (2, LAYERS), 1)
    table = jnp.full((2, LAYERS), -1, jnp.int32)
    for layer in range(LAYERS):
        belongs = placement[layer] + LAYERS * pairing[layer]
        table = jnp.where((at_row == 1) & (at_lane == layer), belongs, table)
    table_ref[...] = table

    def work(layer, source_chip, home_core, slot, rank):
        code = layer + 8 * source_chip + 32 * home_core + 64 * slot
        table_ref[...] = jnp.where((at_row == 0) & (at_lane == rank), code, table_ref[...])
        key = qk_ref[home_core, slot, :, HEADS * HEAD_WIDTH :]

        def query(head):
            return qk_ref[home_core, slot, :, head * HEAD_WIDTH : (head + 1) * HEAD_WIDTH]

        tail_row = lax.broadcasted_iota(jnp.int32, (PACKED - PAIRS * TOKENS, TOKENS), 0)
        empty = jnp.zeros(tail_row.shape, jnp.float32)
        scales = empty
        for head in range(HEADS):
            scales = jnp.where(tail_row == HEADS + head, scale_ref[head, layer] * INVERSE, scales)
        raw_ref[rank, PAIRS * TOKENS :, :] = scales
        logp_ref[rank, PAIRS * TOKENS :, :] = empty
        for pair in range(PAIRS):
            plain = dot(query(2 * pair), key, 1, 1) * INVERSE
            turned = dot(key, query(2 * pair + 1), 1, 1) * INVERSE
            pack(raw_ref, rank, pair, plain, turned)
            plain = log_softmax(scale_ref[2 * pair, layer] * plain, col <= row, 1)
            turned = log_softmax(scale_ref[2 * pair + 1, layer] * turned, row <= col, 0)
            pack(logp_ref, rank, pair, plain, turned)

    for_my_layers(pairing, placement, work)


def student_kernel(table, arrived_ref, raw_ref, logp_ref, sums_ref):
    row, col = masks()
    lower = col <= row
    place = lax.broadcasted_iota(jnp.int32, (8, TOKENS), 0)
    lane = lax.broadcasted_iota(jnp.int32, (8, TOKENS), 1)
    sums_ref[...] = jnp.zeros_like(sums_ref)

    held = jnp.int32(0)
    for rank in range(2 * SLOTS):
        held += (table[0, rank] >= 0).astype(jnp.int32)

    def work(rank, carry):
        code = table[0, rank]
        layer, source_chip = code & 7, (code >> 3) & 3

        def terms(rows):
            target = arrived_ref[source_chip, rows, :]
            target_logp = jnp.log(jnp.maximum(target, SMALLEST))
            student_logp = logp_ref[rank, rows, :]
            difference = jnp.exp(student_logp) - target
            return (
                jnp.sum(target * (target_logp - student_logp), axis=0, keepdims=True),
                difference * raw_ref[rank, rows, :],
            )

        last, last_moved = terms(slice(PAIRS * TOKENS, PACKED))
        found = jnp.zeros((8, TOKENS), jnp.float32)
        divergence = last
        for pair in range(PAIRS):
            one, moved = terms(slice(pair * TOKENS, (pair + 1) * TOKENS))
            divergence += one
            of_first = jnp.sum(jnp.where(lower, moved, 0.0), axis=0, keepdims=True)
            of_second = jnp.sum(jnp.where(lower, 0.0, moved), axis=0, keepdims=True)
            of_second += last_moved[pair : pair + 1]
            found = jnp.where(place == 1 + 2 * pair, of_first, found)
            found = jnp.where(place == 2 + 2 * pair, of_second, found)
        found = jnp.where(place == 0, divergence, found)
        found = jnp.sum(found, axis=1, keepdims=True)
        goes_to = jnp.where(place == 0, layer, SCALE_LANE + LAYERS * (place - 1) + layer)
        found = jnp.where((lane == goes_to) & (place <= HEADS), found, 0.0)
        sums_ref[...] += jnp.sum(found, axis=0, keepdims=True)
        return carry

    lax.fori_loop(0, held, work, 0)


def slope_kernel(table, arrived_ref, raw_ref, logp_ref, grad_ref, sent_ref):
    core = lax.rem(lax.axis_index("section"), 2)
    row, col = masks()
    lower = col <= row
    tail_row = lax.broadcasted_iota(jnp.int32, (TAIL, TOKENS), 0)
    held = jnp.int32(0)
    for rank in range(2 * SLOTS):
        held += (table[0, rank] >= 0).astype(jnp.int32)

    def work(rank, carry):
        code = table[0, rank]
        source_chip, home_core, slot = (code >> 3) & 3, (code >> 5) & 1, code >> 6

        def difference(rows):
            return jnp.exp(logp_ref[rank, rows, :]) - arrived_ref[source_chip, rows, :]

        def scale_of(head):
            at = PAIRS * TOKENS + HEADS + head
            return raw_ref[rank, at : at + 1, :]

        last = difference(slice(PAIRS * TOKENS, PACKED))
        tail = jnp.zeros((TAIL, TOKENS), jnp.float32)
        pieces = []
        for pair in range(PAIRS):
            first, second = scale_of(2 * pair), scale_of(2 * pair + 1)
            square = difference(slice(pair * TOKENS, (pair + 1) * TOKENS))
            pieces.append(square * jnp.where(lower, first, second))
            tail = jnp.where(tail_row == pair, last[pair : pair + 1] * second, tail)
        pieces.append(tail)

        def put(ref, at):
            for n, piece in enumerate(pieces):
                to = pl.multiple_of(at + n * TOKENS, TAIL)
                ref[pl.ds(to, piece.shape[0]), :] = piece.astype(jnp.bfloat16)

        @pl.when(home_core == core)
        def _():
            put(grad_ref, slot * SLOT_ROWS)

        @pl.when(home_core != core)
        def _():
            put(sent_ref, slot * SLOT_ROWS)

        return carry

    lax.fori_loop(0, held, work, 0)


def spread_kernel(pair_ref, out_ref):
    out_ref[...] = jnp.broadcast_to(pair_ref[0] + pair_ref[1], out_ref.shape)


def gradient_kernel(table, grad_ref, sent_ref, qk_ref, q_out, k_out):
    me = lax.axis_index("section")
    core = lax.rem(me, 2)
    row, col = masks()
    held, layers = jnp.int32(0), [jnp.int32(0)] * SLOTS
    for layer in range(LAYERS):
        here = (table[1, layer] & (LAYERS - 1)) == me
        layers = [
            jnp.where(here & (held == slot), layer, had) for slot, had in enumerate(layers)
        ]
        held += here.astype(jnp.int32)
    for slot in range(SLOTS):

        @pl.when(slot < held)
        def _():
            direct = ((table[1, layers[slot]] >> 3) & 1) == core
            key = qk_ref[core, slot, :, HEADS * HEAD_WIDTH :]
            total = jnp.zeros((TOKENS, HEAD_WIDTH), jnp.float32)

            def rows(at, count):
                at = slot * SLOT_ROWS + at
                near = grad_ref[at : at + count, :].astype(jnp.float32)
                other = sent_ref[1 - core, at : at + count, :].astype(jnp.float32)
                return jnp.where(direct, near, other)

            tail = rows(PAIRS * TOKENS, TAIL)
            for head in range(HEADS):
                pair, over = head // 2, head % 2
                square = rows(pair * TOKENS, TOKENS)
                if over:
                    diagonal = jnp.where(row == col, tail[pair : pair + 1], 0.0)
                    grad = jnp.where(row < col, square, diagonal)
                else:
                    grad = jnp.where(col <= row, square, 0.0)
                grad = grad.astype(jnp.bfloat16)
                lanes = slice(head * HEAD_WIDTH, (head + 1) * HEAD_WIDTH)
                query = qk_ref[core, slot, :, lanes]
                q_out[0, slot, :, lanes] = dot(grad, key, 1 - over, 0).astype(jnp.bfloat16)
                total += dot(grad, query, over, 0)
            k_out[0, slot] = total.astype(jnp.bfloat16)

        @pl.when(slot >= held)
        def _():
            q_out[0, slot] = jnp.zeros(q_out.shape[2:], jnp.bfloat16)
            k_out[0, slot] = jnp.zeros(k_out.shape[2:], jnp.bfloat16)


def final_kernel(rows_ref, kl_ref, scale_ref):
    divergence = jnp.sum(rows_ref[1], axis=0, keepdims=True)
    kl_ref[...] = divergence[:, :LAYERS] / (STUDENT_HEADS * TOKENS)
    terms = jnp.sum(rows_ref[0], axis=0, keepdims=True)
    scale_ref[...] = jnp.concatenate(
        [terms[:, SCALE_LANE + LAYERS * h : SCALE_LANE + LAYERS * (h + 1)] for h in range(HEADS)], axis=0
    )


VMEM = pl.BlockSpec(memory_space=pltpu.VMEM)
ANY = pl.BlockSpec(memory_space=pl.ANY)
SMEM = pl.BlockSpec(memory_space=pltpu.SMEM)
SMALL = pltpu.CompilerParams(vmem_limit_bytes=16 * 2**20)


def kept(array):
    return pltpu.with_memory_space_constraint(array, pltpu.VMEM)


def cost(flops, moved):
    return pl.CostEstimate(flops=flops, bytes_accessed=moved, transcendentals=0)


def local(chips, groups, teacher_q, teacher_k, student_q, student_k, student_scale, pairing, placement):
    f32, bf16 = jnp.float32, jnp.bfloat16
    over_x = [[2 * x + core for x in range(chips)] for core in range(2)]
    of_chip = [[2 * x, 2 * x + 1] for x in range(chips)]
    members = len(groups[0])

    packed = pl.pallas_call(
        teacher_kernel,
        out_shape=jax.ShapeDtypeStruct((chips, PACKED, TOKENS), f32),
        in_specs=[SMEM, SMEM, VMEM, VMEM],
        out_specs=ANY,
        scratch_shapes=[
            pltpu.VMEM((PACKED, TOKENS), f32),
            pltpu.SemaphoreType.DMA((PAIRS,)),
        ],
        cost_estimate=cost(8 * 2 * TOKENS**3, 400_000),
        name="teacher",
    )(pairing, placement, teacher_q, teacher_k)
    arrived = lax.all_to_all(
        packed, "section", 0, 0, tiled=True, axis_index_groups=over_x
    )
    def of_both_cores(array):
        return lax.all_gather(array, "section", axis_index_groups=of_chip)

    chip_qk = kept(of_both_cores(jnp.concatenate((student_q[0], student_k[0]), axis=2)))
    at_once = 2 * SLOTS
    squares = pltpu.VMEM((at_once, PACKED, TOKENS), f32)
    raw, logp, table = pl.pallas_call(
        scores_kernel,
        out_shape=(squares, squares, pltpu.VMEM((2, LAYERS), jnp.int32)),
        in_specs=[SMEM, SMEM, SMEM, VMEM],
        out_specs=(VMEM, VMEM, VMEM),
        cost_estimate=cost(8 * 2 * TOKENS**3, 1_400_000),
        compiler_params=SMALL,
        name="scores",
    )(pairing, placement, student_scale.T, chip_qk)
    table = kept(table)

    work_on = (table, *map(kept, (arrived, raw, logp)))
    sums = pl.pallas_call(
        student_kernel,
        out_shape=pltpu.VMEM((1, TOKENS), f32),
        in_specs=[SMEM, VMEM, VMEM, VMEM],
        out_specs=VMEM,
        cost_estimate=cost(8 * 2 * TOKENS**3, 1_800_000),
        compiler_params=SMALL,
        name="student",
    )(*work_on)
    packed_grads = pltpu.VMEM((SENT, TOKENS), bf16)
    grads, sent = pl.pallas_call(
        slope_kernel,
        out_shape=(packed_grads, packed_grads),
        in_specs=[SMEM, VMEM, VMEM, VMEM],
        out_specs=(VMEM, VMEM),
        cost_estimate=cost(8 * 2 * TOKENS**3, 1_800_000),
        compiler_params=SMALL,
        name="slope",
    )(*work_on)

    sums = pl.pallas_call(
        spread_kernel,
        out_shape=jax.ShapeDtypeStruct((members, TOKENS), f32),
        in_specs=[VMEM],
        out_specs=VMEM,
        compiler_params=SMALL,
        name="spread",
    )(kept(of_both_cores(sums)))
    chip_sent = kept(of_both_cores(sent))
    rows = lax.all_to_all(
        sums.reshape(members, 1, TOKENS), AXES, 0, 0, tiled=True, axis_index_groups=groups
    )
    q_grad, k_grad = pl.pallas_call(
        gradient_kernel,
        out_shape=(
            jax.ShapeDtypeStruct(student_q.shape, bf16),
            jax.ShapeDtypeStruct(student_k.shape, bf16),
        ),
        in_specs=[SMEM, VMEM, VMEM, VMEM],
        out_specs=(VMEM, VMEM),
        cost_estimate=cost(16 * 2 * TOKENS**3, 900_000),
        compiler_params=SMALL,
        name="gradient",
    )(table, kept(grads), chip_sent, chip_qk)

    both = of_both_cores(rows.reshape(members, TOKENS))
    layer_kl, scale_grad = pl.pallas_call(
        final_kernel,
        out_shape=(
            jax.ShapeDtypeStruct((1, LAYERS), f32),
            jax.ShapeDtypeStruct((HEADS, LAYERS), f32),
        ),
        in_specs=[VMEM],
        out_specs=(VMEM, VMEM),
        compiler_params=SMALL,
        name="final",
    )(kept(both))
    return (q_grad, k_grad, layer_kl, scale_grad.T)


def reduction_groups(sections, heads, replicas):
    def flat(section, head, replica):
        return (section * heads + head) * replicas + replica

    chips = range(sections // 2)
    first = [
        [flat(2 * x + 1, h, d) for x in chips for h in range(heads)] for d in range(replicas)
    ]
    second = [
        [flat(2 * x, h, d) for x in chips for d in range(replicas)] for h in range(heads)
    ]
    return first + second


def solution(mesh):
    sections, heads, replicas = (mesh.shape[a] for a in AXES)
    return jax.shard_map(
        functools.partial(local, sections // 2, reduction_groups(sections, heads, replicas)),
        mesh=mesh,
        in_specs=(
            P("section", "dp", "head"),
            P("section", "dp", "head"),
            P("section", None, "dp", "head"),
            P("section", None, "dp", "head"),
            P(None, "head"),
            P(),
            P(),
        ),
        out_specs=(
            P("section", None, "dp", "head"),
            P("section", None, "dp", "head"),
            P("dp", None),
            P(None, "head"),
        ),
        check_vma=False,
    )
```
